32 devices in a mesh: dp: 8 (over y, x, core), shard: 4 (over z).
Axes of the slice: x: 2, y: 2, z: 4, core: 2. Of those that a mesh axis runs over, the one named last changes fastest.
Arguments:
- tokens: bfloat16 [32, 128, 2048], P(('dp', 'shard')), may hold values from -6 to 6
- segments: int32 [32, 128], P(('dp', 'shard')), may hold values from 0 to 5, never falling along the last dimension, each value on 1 to 64 neighbouring positions
- ln_gain: bfloat16 [2048], P('shard'), may hold values from 0.099609375 to 1.8984375
- ln_bias: bfloat16 [2048], P('shard'), may hold values from -1.75 to 1.75
- w_qkv: bfloat16 [2048, 6144], P('shard'), may hold values from -0.1875 to 0.1875
- b_qkv: bfloat16 [6144], P('shard'), may hold values from -1.75 to 1.75
- w_out: bfloat16 [2048, 2048], P('shard'), may hold values from -0.375 to 0.375
- b_out: bfloat16 [2048], P('shard'), may hold values from -1.75 to 1.75
- w_fc1: bfloat16 [2048, 8192], P('shard'), may hold values from -0.125 to 0.125
- b_fc1: bfloat16 [8192], P('shard'), may hold values from -1.75 to 1.75
- w_fc2: bfloat16 [8192, 2048], P('shard'), may hold values from -0.09375 to 0.09375
- b_fc2: bfloat16 [2048], P('shard'), may hold values from -1.75 to 1.75
- cotangent: bfloat16 [32, 128, 2048], P(('dp', 'shard')), may hold values from -6 to 6
Outputs:
- block_output: bfloat16 [32, 128, 2048], P(('dp', 'shard'))
- input_grad: float32 [32, 128, 2048], P(('dp', 'shard'))
- gain_grad: float32 [2048], P('shard')
- shift_grad: float32 [2048], P('shard')
- qkv_grad: float32 [2048, 6144], P('shard')
- qkv_bias_grad: float32 [6144], P('shard')
- out_grad: float32 [2048, 2048], P('shard')
- out_bias_grad: float32 [2048], P('shard')
- fc1_grad: float32 [2048, 8192], P('shard')
- fc1_bias_grad: float32 [8192], P('shard')
- fc2_grad: float32 [8192, 2048], P('shard')
- fc2_bias_grad: float32 [2048], P('shard')
The draws below stay inside these ranges and needn't reach their ends.
Inputs may be any that keep to these rules, and one draw needn't show every extreme that they name: `segments`: within a sequence segment numbers never fall; each of the 6 documents has 1 to 64 tokens and one has exactly 64.
All inputs are finite; a program needn't handle non-finite values.
Results may differ from the reference program's by a relative error of at most 0.012.
The reference program's roundings to bfloat16 on the way count: a program that leaves them out, or rounds other values in their place, can miss the bound.
Values may be sent and summed in bfloat16 or wider, within the bound.
No kernel may reach another device: no remote copies, remote signals or barrier semaphores. Data moves between devices by JAX's collectives and lax.ppermute only.
A program may use at most 576 MiB of HBM per device.

```python
import math
import jax
import jax.numpy as jnp
import numpy as np
from jax import lax

D = 2048
HEADS = 32
HEAD_DIM = 64
ROT = 32
FF = 8192
LEN = 128
DOCS = 6
SEQS = 32


def strengthened(values, own_key, source, target, parts, factor):
    owner, partner = [(jnp.arange(values.shape[dim]) // (values.shape[dim] // parts)).reshape([-1 if axis == dim else 1 for axis in range(values.ndim)]) for dim in (source, target)]
    chosen = jax.random.permutation(own_key, parts)[partner]
    strong = (owner == chosen) | (owner == (partner + parts // 2) % parts)
    return jnp.where(strong, factor * values, values)


def shard_levels(own_key, dims, pieces, smallest, high):
    factor_of = 1.0
    for position, shards_of in pieces:
        draws = jax.random.uniform(jax.random.fold_in(jax.random.fold_in(own_key, 6), position), (shards_of,), jnp.float32, smallest / len(pieces), high / len(pieces))
        factor_of = factor_of * jnp.repeat(jnp.exp(draws), dims[position] // shards_of).reshape((-1,) + (1,) * (len(dims) - 1 - position))
    return factor_of


def length_profile(amount, total, reach, slope):
    weights = [(1 << 20) // math.isqrt(standing ** slope) + 1 for standing in range(2, amount + 1)]
    rest, holding = total - reach - (amount - 1), [1] * (amount - 1)
    while rest > 0:
        candidates = [i for i in range(amount - 1) if holding[i] < reach]
        pool, budget = sum([weights[i] for i in candidates]), rest
        for i in candidates:
            more = min(reach - holding[i], max(1, budget * weights[i] // pool), rest)
            holding[i] = holding[i] + more
            rest = rest - more
    return np.array([reach] + holding)


def ragged_sizes(own_key, amount, total, bound, lean):
    if amount == 2:
        one = jax.random.randint(own_key, (), max(1, total - bound), min(bound, total - 1) + 1)
        return jnp.stack([one, total - one])
    lengths = jnp.asarray(length_profile(amount, total, bound, lean), jnp.int32)
    twos = (amount - 1) // 2
    donor, taker = lengths[1:1 + 2 * twos:2], lengths[2:2 + 2 * twos:2]
    slack = jnp.minimum(donor - 1, bound - taker)
    passed = jax.random.randint(jax.random.fold_in(own_key, 1), (twos,), 0, 1 << 20) % (slack + 1)
    lengths = lengths.at[1:1 + 2 * twos:2].set(donor - passed).at[2:2 + 2 * twos:2].set(taker + passed)
    return lengths[jax.random.permutation(jax.random.fold_in(own_key, 2), amount)]


def gaussian(stream_key, dims, scale, limit, shards=(), held_as=jnp.bfloat16):
    drawn = jax.random.normal(stream_key, dims, jnp.float32) * scale
    if len(shards) > 0:
        drawn = shard_levels(stream_key, dims, shards, -0.22, 0.18) * drawn
    return jnp.clip(drawn, min=-limit, max=limit).astype(held_as)


def bell_draw_with(rng, dims, width, bound, shards, heavy, held_as=jnp.bfloat16):
    values = width * jax.random.normal(rng, dims, jnp.float32)
    if shards:
        values = values * shard_levels(rng, dims, shards, -0.22, 0.18)
    return jnp.clip(strengthened(values, jax.random.fold_in(rng, 3), *heavy), -bound, bound).astype(held_as)


def setup_inputs(seed: int = 0) -> dict:
    keys = jax.random.split(jax.random.key(seed), 14)
    return {
        "tokens": gaussian(keys[0], (SEQS, LEN, D), 1.0, 6.0, ((0, 32),)),
        "segments": jax.vmap(lambda own: jnp.searchsorted(jnp.cumsum(ragged_sizes(own, DOCS, LEN, LEN // 2, 0)), jnp.arange(LEN), side="right"))(jax.random.split(keys[1], SEQS)).reshape((SEQS, LEN)).astype(jnp.int32),
        "ln_gain": jnp.clip(1.0 + 0.18 * jax.random.normal(keys[2], (D,), jnp.float32), 0.099609375, 1.8984375).astype(jnp.bfloat16),
        "ln_bias": gaussian(keys[3], (D,), 0.3, 1.75, ((0, 4),)),
        "w_qkv": gaussian(keys[4], (D, 3 * D), (D // 2) ** -0.5, 0.1875, ((0, 4),)),
        "b_qkv": gaussian(keys[5], (3 * D,), 0.3, 1.75, ((0, 4),)),
        "w_out": gaussian(keys[6], (D, D), (D // 8) ** -0.5, 0.375, ((0, 4),)),
        "b_out": gaussian(keys[7], (D,), 0.3, 1.75, ((0, 4),)),
        "w_fc1": gaussian(keys[8], (D, FF), D ** -0.5, 0.125, ((0, 4),)),
        "b_fc1": gaussian(keys[9], (FF,), 0.3, 1.75, ((0, 4),)),
        "w_fc2": gaussian(keys[10], (FF, D), (FF // 2) ** -0.5, 0.09375, ((0, 4),)),
        "b_fc2": gaussian(keys[11], (D,), 0.3, 1.75, ((0, 4),)),
        "cotangent": bell_draw_with(keys[12], (SEQS, LEN, D), 1.0, 6.0, ((0, 32),), (0, 2, 32, 2.75)),
    }


epsilon = 1e-05
masked_value = -1e+30
exactness = lax.Precision.HIGHEST

@jax.custom_vjp
def low(v):
    return lax.optimization_barrier(v.astype(jnp.bfloat16)).astype(jnp.float32)

@jax.custom_vjp
def low_back(v):
    return v

def low_keep(v):
    return (low(v), None)

def low_pass(kept, grad):
    return (grad,)

def back_keep(v):
    return (v, None)

def back_low(kept, grad):
    return (low(grad),)
low.defvjp(low_keep, low_pass)
low_back.defvjp(back_keep, back_low)

def layer_norm(seq_rows, gain_full, shift_full):
    average = lax.optimization_barrier(jnp.mean(seq_rows, axis=-1, keepdims=True))
    centred = seq_rows - average
    variance = lax.optimization_barrier(jnp.mean(centred * centred, axis=-1, keepdims=True))
    return centred * lax.rsqrt(variance + epsilon) * gain_full + shift_full

def rotary_tables(segment):
    positions = jnp.arange(segment.shape[0], dtype=jnp.int32)
    change = jnp.concatenate([jnp.ones((1,), dtype=bool), segment[1:] != segment[:-1]])
    run_start = lax.cummax(jnp.where(change, positions, 0), axis=0)
    distance = (positions - run_start).astype(jnp.float32)
    frequency = jnp.exp(jnp.arange(ROT // 2, dtype=jnp.float32) * (-2.0 * math.log(10000.0) / ROT))
    angles = distance[:, None] * frequency[None, :]
    return (jnp.cos(angles), jnp.sin(angles))

def rotate(values, cos_table, sin_table):
    half_rot = ROT // 2
    first_half = values[..., :half_rot]
    second = values[..., half_rot:ROT]
    remainder = values[..., ROT:]
    cos_wide = cos_table[..., None, :]
    sin_wide = sin_table[..., None, :]
    return jnp.concatenate([first_half * cos_wide - second * sin_wide, second * cos_wide + first_half * sin_wide, remainder], axis=-1)

def attention(queries, key_rows, values, segment):
    length = queries.shape[0]
    block_rows = min(512, length)
    positions = jnp.arange(length, dtype=jnp.int32)
    score_scale = HEAD_DIM ** (-0.5)

    def one_block(offset):
        query_block = lax.dynamic_slice_in_dim(queries, offset, block_rows, 0)
        seg_block = lax.dynamic_slice_in_dim(segment, offset, block_rows, 0)
        places = offset + jnp.arange(block_rows, dtype=jnp.int32)
        scores = low_back(jnp.einsum('qhd,khd->hqk', query_block, key_rows, precision=exactness) * score_scale)
        allowed = (seg_block[:, None] == segment[None, :]) & (places[:, None] >= positions[None, :])
        scores = jnp.where(allowed[None], scores, masked_value)
        prob_rows = low(jax.nn.softmax(scores, axis=-1))
        return jnp.einsum('hqk,khd->qhd', prob_rows, values, precision=exactness)
    offsets = jnp.arange(length // block_rows, dtype=jnp.int32) * block_rows
    blocks = lax.map(jax.checkpoint(one_block), offsets)
    return blocks.reshape(length, HEADS, HEAD_DIM)

def one_sequence(seq_rows, segment, parameters):
    gain_full, shift_full, qkv_full, qkv_bias, out_full, out_bias, fc1_full, fc1_bias, fc2_full, fc2_bias = parameters
    length = seq_rows.shape[0]
    normed = low(layer_norm(seq_rows, gain_full, shift_full))
    mixed_rows = low_back(jnp.dot(normed, qkv_full, precision=exactness) + qkv_bias)
    cos_table, sin_table = rotary_tables(segment)
    queries = mixed_rows[:, :D].reshape(length, HEADS, HEAD_DIM)
    key_rows = mixed_rows[:, D:2 * D].reshape(length, HEADS, HEAD_DIM)
    values = low(mixed_rows[:, 2 * D:].reshape(length, HEADS, HEAD_DIM))
    queries = low(rotate(queries, cos_table, sin_table))
    key_rows = low(rotate(key_rows, cos_table, sin_table))
    context = low_back(low(attention(queries, key_rows, values, segment).reshape(length, D)))
    attended = jnp.dot(context, out_full, precision=exactness) + out_bias
    hidden = low_back(jnp.dot(normed, fc1_full, precision=exactness) + fc1_bias)
    active = low(jax.nn.gelu(hidden, approximate=True))
    return seq_rows + attended + jnp.dot(active, fc2_full, precision=exactness) + fc2_bias

def reference(tokens, segments, ln_gain, ln_bias, w_qkv, b_qkv, w_out, b_out, w_fc1, b_fc1, w_fc2, b_fc2, cotangent):
    group_size = 1
    for candidate in range(1, SEQS + 1):
        if SEQS % candidate == 0 and candidate * LEN <= 4096:
            group_size = candidate
    parameters = (ln_gain.astype(jnp.float32), ln_bias.astype(jnp.float32), w_qkv.astype(jnp.float32), b_qkv.astype(jnp.float32), w_out.astype(jnp.float32), b_out.astype(jnp.float32), w_fc1.astype(jnp.float32), b_fc1.astype(jnp.float32), w_fc2.astype(jnp.float32), b_fc2.astype(jnp.float32))

    def per_group(group_rows, group_marks, group_weights):
        return jax.vmap(one_sequence, in_axes=(0, 0, None))(group_rows, group_marks, group_weights)
    checked = jax.checkpoint(per_group)

    def forward(all_rows, weights):
        grouped = all_rows.reshape(SEQS // group_size, group_size, LEN, D)
        marks = segments.reshape(SEQS // group_size, group_size, LEN)

        def scan_step(carried, scan_item):
            return (carried, checked(scan_item[0], scan_item[1], weights))
        unused, outputs = lax.scan(scan_step, jnp.zeros((), jnp.float32), (grouped, marks))
        return outputs.reshape(SEQS, LEN, D)
    result, pullback = jax.vjp(forward, tokens.astype(jnp.float32), parameters)
    input_grad, weight_grads = pullback(cotangent.astype(jnp.float32))
    factor = 1.0 / math.sqrt(SEQS * LEN)
    gain_grad, shift_grad, qkv_grad, qkv_bias_grad, out_grad, out_bias_grad, fc1_grad, fc1_bias_grad, fc2_grad, fc2_bias_grad = weight_grads
    return (result.astype(jnp.bfloat16), input_grad, gain_grad * factor, shift_grad * factor, qkv_grad * factor, qkv_bias_grad * factor, out_grad * factor, out_bias_grad * factor, fc1_grad * factor, fc1_bias_grad * factor, fc2_grad * factor, fc2_bias_grad * factor)
```

```python
import math

import jax
import jax.numpy as jnp
from jax import lax
from jax.sharding import PartitionSpec as P

HEADS = 32
HEAD_DIM = 64
ROT = 32
CORES = 2

epsilon = 1e-05
masked_value = -1e30
AXES = ("dp", "shard")
f32 = jnp.float32
bf16 = jnp.bfloat16


def rotary_tables(segment):
    positions = jnp.arange(segment.shape[0], dtype=jnp.int32)
    change = jnp.concatenate([jnp.ones((1,), dtype=bool), segment[1:] != segment[:-1]])
    run_start = lax.cummax(jnp.where(change, positions, 0), axis=0)
    distance = (positions - run_start).astype(f32)
    frequency = jnp.exp(jnp.arange(ROT // 2, dtype=f32) * (-2.0 * math.log(10000.0) / ROT))
    angles = distance[:, None] * frequency[None, :]
    return (jnp.cos(angles), jnp.sin(angles))


def rotate(values, cos_table, sin_table, sign):
    half_rot = ROT // 2
    first_half = values[..., :half_rot]
    second = values[..., half_rot:ROT]
    remainder = values[..., ROT:]
    cos_wide = cos_table[..., None, :]
    sin_wide = sign * sin_table[..., None, :]
    return jnp.concatenate(
        [
            first_half * cos_wide - second * sin_wide,
            second * cos_wide + first_half * sin_wide,
            remainder,
        ],
        axis=-1,
    )


def attention(queries, key_rows, values, segments, context_grad):
    length = queries.shape[1]
    scale = HEAD_DIM ** (-0.5)
    positions = jnp.arange(length, dtype=jnp.int32)
    allowed = (segments[:, :, None] == segments[:, None, :]) & (
        positions[:, None] >= positions[None, :]
    )
    scores = jnp.einsum("bqhd,bkhd->bhqk", queries, key_rows, preferred_element_type=f32) * scale
    scores = jnp.where(allowed[:, None], scores, masked_value)
    weights = jnp.exp(scores - jnp.max(scores, axis=-1, keepdims=True))
    probs = weights / jnp.sum(weights, axis=-1, keepdims=True)
    low = probs.astype(bf16)
    context = jnp.einsum("bhqk,bkhd->bqhd", low, values, preferred_element_type=f32).astype(bf16)
    prob_grad = jnp.einsum("bqhd,bkhd->bhqk", context_grad, values, preferred_element_type=f32)
    inner = jnp.sum(prob_grad * probs, axis=-1, keepdims=True)
    score_grad = (probs * (prob_grad - inner)).astype(bf16)
    query_grad = (
        jnp.einsum("bhqk,bkhd->bqhd", score_grad, key_rows, preferred_element_type=f32) * scale
    )
    key_grad = (
        jnp.einsum("bhqk,bqhd->bkhd", score_grad, queries, preferred_element_type=f32) * scale
    )
    value_grad = jnp.einsum("bhqk,bqhd->bkhd", low, context_grad, preferred_element_type=f32)
    return context, query_grad, key_grad, value_grad


class Links:
    def __init__(self, planes, replicas):
        self.S = planes
        self.J = replicas // CORES
        self.B = 2 if self.J % 2 == 0 else 1
        self.A = self.J // self.B
        dp = lax.axis_index("dp")
        self.s = lax.axis_index("shard")
        self.c = dp % CORES
        self.j = dp // CORES
        self.b = self.j % self.B
        self.a = self.j // self.B

    def move(self, x, da=0, db=0, dc=0, ds=0):
        pairs = []
        for a in range(self.A):
            for b in range(self.B):
                for c in range(CORES):
                    for s in range(self.S):
                        to = ((a + da) % self.A, (b + db) % self.B, (c + dc) % CORES, (s + ds) % self.S)
                        pairs.append((self.flat(a, b, c, s), self.flat(*to)))
        return lax.ppermute(x, AXES, pairs)

    def flat(self, a, b, c, s):
        return ((a * self.B + b) * CORES + c) * self.S + s

    def line(self, x, axis):
        size = {"a": self.A, "b": self.B, "c": CORES, "s": self.S}[axis]
        here = {"a": self.a, "b": self.b, "c": self.c, "s": self.s}[axis]
        held = [x] + [self.move(x, **{"d" + axis: k}) for k in range(1, size)]
        return in_order(held, here)

    def spread(self, x, axis):
        size = {"a": self.A, "b": self.B, "c": CORES, "s": self.S}[axis]
        here = {"a": self.a, "b": self.b, "c": self.c, "s": self.s}[axis]
        total = pick(x, here, 0).astype(f32)
        for k in range(1, size):
            sent = pick(x, (here + k) % size, 0).astype(bf16)
            total = total + self.move(sent, **{"d" + axis: k}).astype(f32)
        return total

    def plane_gather(self, x):
        half = x.shape[1] // 2
        first = self.line(self.line(x[:, :half], "b"), "a")
        second = jnp.swapaxes(self.line(self.line(x[:, half:], "a"), "b"), 0, 1)
        both = jnp.concatenate([first, second], axis=-1)
        return both.reshape((self.J,) + x.shape)

    def plane_spread(self, x):
        rows, columns = x.shape[1:]
        x = x.reshape(self.A, self.B, rows, columns)
        half = columns // 2
        first = self.spread(self.spread(x[..., :half], "a").astype(bf16), "b")
        second = self.spread(
            self.spread(jnp.swapaxes(x[..., half:], 0, 1), "b").astype(bf16), "a"
        )
        return jnp.concatenate([first, second], axis=-1).astype(bf16)


def pick(x, index, axis):
    return lax.dynamic_index_in_dim(x, index, axis, keepdims=False)


def in_order(held, here):
    size = len(held)
    if size == 1:
        return held[0][None]
    if size == 2:
        return jnp.where(here == 0, jnp.stack(held), jnp.stack(held[::-1]))
    backwards = jnp.stack(held[::-1])
    return lax.dynamic_slice_in_dim(
        jnp.concatenate([backwards, backwards]), size - 1 - here, size, 0
    )


def local(
    tokens,
    segments,
    ln_gain,
    ln_bias,
    w_qkv,
    b_qkv,
    w_out,
    b_out,
    w_fc1,
    b_fc1,
    w_fc2,
    b_fc2,
    cotangent,
):
    planes = lax.axis_size("shard")
    replicas = lax.axis_size("dp")
    net = Links(planes, replicas)
    S, J, c, j, s = net.S, net.J, net.c, net.j, net.s
    seqs, length, width = tokens.shape
    rows = seqs * length
    ff = w_fc1.shape[1]
    ff_own = ff // (S * CORES)
    heads_own = HEADS // (S * CORES)
    mix_own = heads_own * HEAD_DIM
    part = width // (S * J)
    members = S * CORES

    vectors = [ln_gain, ln_bias, b_qkv, b_out, b_fc1, b_fc2]
    small = net.line(jnp.concatenate(vectors), "s")
    whole = []
    start = 0
    for vector in vectors:
        whole.append(small[:, start : start + vector.shape[0]].reshape(-1).astype(f32))
        start += vector.shape[0]
    gain_full, shift_full, qkv_bias, out_bias, fc1_bias, fc2_bias = whole
    cut = lambda v: lax.dynamic_slice_in_dim(v, (s * CORES + c) * ff_own, ff_own, 0)
    fc1_bias = cut(fc1_bias)
    qkv_bias = lax.dynamic_slice_in_dim(
        qkv_bias.reshape(3, width), (s * CORES + c) * mix_own, mix_own, 1
    ).reshape(-1)

    def group(x):
        held = [x]
        for k in range(1, S):
            held.append(net.move(held[-1], ds=1))
        other = [net.move(x, dc=1) for x in held]
        return jnp.stack([v for pair in zip(held, other) for v in pair])

    def deal(x):
        x = x.reshape(S, CORES, rows, width)
        mine = x[:, 0].astype(f32) + net.move(x[:, 1].astype(bf16), dc=1).astype(f32)
        total = mine[0]
        for k in range(1, S):
            total = total + net.move(mine[k].astype(bf16), ds=-k).astype(f32)
        return total

    def columns_of(weight, offset_of, size):
        height = weight.shape[0]
        got = [
            net.move(
                lax.dynamic_slice(weight, (j * part, offset_of((s + k) % S)), (part, size)), ds=k
            )
            for k in range(1, S)
        ]
        full = net.plane_gather(jnp.concatenate(got, axis=0))
        full = full.reshape(J, S - 1, part, size)
        held = [lax.dynamic_slice(weight, (0, offset_of(s)), (height, size))]
        held += [full[:, k].reshape(height, size) for k in range(S - 1)]
        return in_order(held, s).reshape(height * S, size)

    fc1_cols = columns_of(w_fc1, lambda plane: (plane * CORES + c) * ff_own, ff_own)
    token_rows = group(tokens.reshape(rows, width))
    out_rows = group(cotangent.reshape(rows, width))
    qkv_cols = jnp.concatenate(
        [
            columns_of(
                w_qkv[:, i * width : (i + 1) * width],
                lambda plane: (plane * CORES + c) * mix_own,
                mix_own,
            )
            for i in range(3)
        ],
        axis=1,
    )
    fc2_rows = lax.dynamic_slice_in_dim(w_fc2, c * ff_own, ff_own, 0)
    out_rows_w = lax.dynamic_slice_in_dim(w_out, c * mix_own, mix_own, 0)
    group_segments = group(segments.reshape(seqs, length)).reshape(members * seqs, length)

    total = members * rows
    inputs = token_rows.reshape(total, width).astype(f32)
    out_rows = out_rows.reshape(total, width)

    def normalise(x):
        average = jnp.mean(x, axis=1, keepdims=True)
        centred = x - average
        inverse = lax.rsqrt(jnp.mean(centred * centred, axis=1, keepdims=True) + epsilon)
        return centred * inverse, inverse

    hidden_in = (normalise(inputs)[0] * gain_full + shift_full).astype(bf16)

    hidden = jnp.dot(hidden_in, fc1_cols, preferred_element_type=f32) + fc1_bias
    active, gelu_back = jax.vjp(lambda v: jax.nn.gelu(v, approximate=True), hidden)
    active = active.astype(bf16)
    active_grad = jnp.einsum("td,fd->tf", out_rows, fc2_rows, preferred_element_type=f32)
    hidden_grad = gelu_back(active_grad)[0].astype(bf16)
    fc2_term = jnp.einsum("tf,td->fd", active, out_rows, preferred_element_type=f32).astype(bf16)
    fc1_term = jnp.einsum("td,tf->df", hidden_in, hidden_grad, preferred_element_type=f32).astype(
        bf16
    )
    fc2_part = net.plane_spread(fc2_term.reshape(J, ff_own // J, width))

    def to_plane(term):
        columns = term.shape[1]
        term = jnp.swapaxes(term.reshape(S, J, part, columns), 0, 1).reshape(
            J, S * part, columns
        )
        term = net.plane_spread(term).reshape(S, part, columns)
        held = [pick(term, s, 0)]
        held += [net.move(pick(term, (s + k) % S, 0), ds=k) for k in range(1, S)]
        return jnp.concatenate(list(in_order(held, s)), axis=1)

    fc1_part = to_plane(fc1_term)

    mixed = jnp.dot(hidden_in, qkv_cols, preferred_element_type=f32) + qkv_bias
    cos_table, sin_table = jax.vmap(rotary_tables)(group_segments)
    head_shape = (members * seqs, length, heads_own, HEAD_DIM)
    queries = rotate(mixed[:, :mix_own].reshape(head_shape), cos_table, sin_table, 1.0).astype(bf16)
    key_rows = rotate(
        mixed[:, mix_own : 2 * mix_own].reshape(head_shape), cos_table, sin_table, 1.0
    ).astype(bf16)
    values = mixed[:, 2 * mix_own :].reshape(head_shape).astype(bf16)
    context_grad = jnp.einsum("te,de->td", out_rows, out_rows_w, preferred_element_type=f32).astype(
        bf16
    )
    context, query_grad, key_grad, value_grad = attention(
        queries, key_rows, values, group_segments, context_grad.reshape(head_shape)
    )
    context = context.reshape(total, mix_own)
    mixed_grad = jnp.concatenate(
        [
            rotate(query_grad, cos_table, sin_table, -1.0).reshape(total, mix_own),
            rotate(key_grad, cos_table, sin_table, -1.0).reshape(total, mix_own),
            value_grad.reshape(total, mix_own),
        ],
        axis=1,
    ).astype(bf16)
    out_term = jnp.einsum("td,te->de", context, out_rows, preferred_element_type=f32).astype(bf16)
    out_part = net.plane_spread(out_term.reshape(J, mix_own // J, width))
    qkv_term = jnp.einsum("td,te->de", hidden_in, mixed_grad, preferred_element_type=f32).astype(
        bf16
    )
    qkv_part = to_plane(qkv_term)

    branch = jnp.dot(context, out_rows_w, preferred_element_type=f32) + jnp.dot(
        active, fc2_rows, preferred_element_type=f32
    )
    own_inputs = tokens.reshape(rows, width).astype(f32)
    output = (own_inputs + deal(branch) + (out_bias + fc2_bias)).astype(bf16).reshape(tokens.shape)
    normed_grad = deal(
        jnp.einsum("te,de->td", mixed_grad, qkv_cols, preferred_element_type=f32)
        + jnp.einsum("tf,df->td", hidden_grad, fc1_cols, preferred_element_type=f32)
    )
    normed, inverse = normalise(own_inputs)
    scaled = normed_grad * gain_full
    input_grad = cotangent.reshape(rows, width).astype(f32) + inverse * (
        scaled
        - jnp.mean(scaled, axis=1, keepdims=True)
        - normed * jnp.mean(scaled * normed, axis=1, keepdims=True)
    )

    factor = 1.0 / math.sqrt(rows * planes * replicas)

    def plane_sum(x):
        for axis in ("a", "b"):
            x = jnp.sum(net.line(x, axis), axis=0)
        return x

    def own(x):
        size = x.shape[-1] // S
        return lax.dynamic_slice_in_dim(x, s * size, size, x.ndim - 1) * factor

    sums = plane_sum(
        jnp.concatenate(
            [
                jnp.sum(out_rows, axis=0, dtype=f32),
                jnp.sum(hidden_grad, axis=0, dtype=f32),
                jnp.sum(mixed_grad, axis=0, dtype=f32),
            ]
        )
    )
    bias_own = own(sums[:width])
    fc1_bias_own = net.line(sums[width : width + ff_own], "c").reshape(-1) * factor
    mixed_sums = net.line(net.line(sums[width + ff_own :], "c"), "s")
    qkv_bias_own = own(
        jnp.transpose(mixed_sums.reshape(S, CORES, 3, mix_own), (2, 0, 1, 3)).reshape(-1)
    )
    norm_sums = jnp.stack([jnp.sum(normed_grad * normed, axis=0), jnp.sum(normed_grad, axis=0)])
    norm_sums = jnp.sum(net.line(plane_sum(norm_sums), "c"), axis=0)
    norm_sums = jnp.sum(net.line(norm_sums, "s"), axis=0)
    gain_own, shift_own = own(norm_sums)

    def both(x):
        other = net.move(x, dc=1)
        return jnp.where(c == 0, x, other), jnp.where(c == 0, other, x)

    fc2_own = net.plane_gather(fc2_part).reshape(ff_own, width)
    fc2_own = jnp.concatenate(both(fc2_own), axis=0).astype(f32) * factor
    fc1_both = both(net.plane_gather(fc1_part).reshape(width // S, S * ff_own))
    fc1_own = (
        jnp.concatenate(
            [x[:, p * ff_own : (p + 1) * ff_own] for p in range(S) for x in fc1_both], axis=1
        ).astype(f32)
        * factor
    )
    out_own = net.plane_gather(out_part).reshape(mix_own, width)
    out_own = jnp.concatenate(both(out_own), axis=0).astype(f32) * factor
    qkv_both = both(net.plane_gather(qkv_part).reshape(width // S, S * 3 * mix_own))
    qkv_own = (
        jnp.concatenate(
            [
                x[:, (p * 3 + i) * mix_own : (p * 3 + i + 1) * mix_own]
                for i in range(3)
                for p in range(S)
                for x in qkv_both
            ],
            axis=1,
        ).astype(f32)
        * factor
    )
    return (
        output,
        input_grad.reshape(tokens.shape),
        gain_own,
        shift_own,
        qkv_own,
        qkv_bias_own,
        out_own,
        bias_own,
        fc1_own,
        fc1_bias_own,
        fc2_own,
        bias_own,
    )


def solution(mesh):
    return jax.shard_map(
        local,
        mesh=mesh,
        in_specs=(
            P(("dp", "shard"), None, None),
            P(("dp", "shard"), None),
            P("shard"),
            P("shard"),
            P("shard", None),
            P("shard"),
            P("shard", None),
            P("shard"),
            P("shard", None),
            P("shard"),
            P("shard", None),
            P("shard"),
            P(("dp", "shard"), None, None),
        ),
        out_specs=(
            P(("dp", "shard"), None, None),
            P(("dp", "shard"), None, None),
            P("shard"),
            P("shard"),
            P("shard", None),
            P("shard"),
            P("shard", None),
            P("shard"),
            P("shard", None),
            P("shard"),
            P("shard", None),
            P("shard"),
        ),
        check_vma=False,
    )
```

```python
import math

import jax
import jax.numpy as jnp
from jax import lax
from jax.experimental import pallas as pl
from jax.experimental.pallas import tpu as pltpu
from jax.sharding import PartitionSpec as P

HEADS = 32
HEAD_DIM = 64
ROT = 32
CORES = 2
LANES = 128

epsilon = 1e-05
masked_value = -1e30
AXES = ("dp", "shard")
f32 = jnp.float32
bf16 = jnp.bfloat16
VMEM = 48 * 1024 * 1024


def rotary_tables(segments):
    seqs, length = segments.shape
    positions = jnp.broadcast_to(jnp.arange(length, dtype=jnp.int32), segments.shape)
    change = jnp.concatenate(
        [jnp.ones((seqs, 1), dtype=bool), segments[:, 1:] != segments[:, :-1]], axis=1
    )
    run_start = lax.cummax(jnp.where(change, positions, 0), axis=1)
    distance = (positions - run_start).astype(f32).reshape(-1, 1)
    lane = jnp.arange(LANES, dtype=jnp.int32) % HEAD_DIM
    half = ROT // 2
    frequency = jnp.exp((lane % half).astype(f32) * (-2.0 * math.log(10000.0) / ROT))
    angles = distance * frequency[None, :]
    sines = jnp.sin(angles)
    cos_table = jnp.where(lane < ROT, jnp.cos(angles), 1.0)
    low_table = jnp.where(lane < half, -sines, 0.0)
    high_table = jnp.where((lane >= half) & (lane < ROT), sines, 0.0)
    starts = jnp.broadcast_to(run_start.reshape(-1, 1), (seqs * length, LANES))
    return starts, cos_table, low_table, high_table


def attention_kernel(
    starts_ref, cos_ref, low_ref, high_ref, mixed_ref, outer_ref, context_ref, grad_ref
):
    length, width = outer_ref.shape
    half = ROT // 2
    scale = HEAD_DIM ** (-0.5)

    def wide(table):
        return jnp.concatenate([table[...]] * (width // LANES), axis=1)

    cos_table, low_table, high_table = wide(cos_ref), wide(low_ref), wide(high_ref)

    def rotate(v, sign):
        turned = pltpu.roll(v, width - half, 1) * low_table + pltpu.roll(v, half, 1) * high_table
        return v * cos_table + sign * turned

    def dot(a, b, dims):
        return lax.dot_general(a, b, (dims, ((), ())), preferred_element_type=f32)

    queries = rotate(mixed_ref[:, :width], 1.0).astype(bf16)
    key_rows = rotate(mixed_ref[:, width : 2 * width], 1.0).astype(bf16)
    values = mixed_ref[:, 2 * width :].astype(bf16)
    outer = outer_ref[...]
    row = lax.broadcasted_iota(jnp.int32, (length, length), 0)
    column = lax.broadcasted_iota(jnp.int32, (length, length), 1)
    allowed = (column <= row) & (column >= starts_ref[...])
    context, query_grad, key_grad, value_grad = [], [], [], []
    for head in range(width // HEAD_DIM):
        span = slice(head * HEAD_DIM, (head + 1) * HEAD_DIM)
        q, k, v, g = queries[:, span], key_rows[:, span], values[:, span], outer[:, span]
        scores = jnp.where(allowed, dot(q, k, ((1,), (1,))) * scale, masked_value)
        weights = jnp.exp(scores - jnp.max(scores, axis=1, keepdims=True))
        probs = weights / jnp.sum(weights, axis=1, keepdims=True)
        low = probs.astype(bf16)
        context.append(dot(low, v, ((1,), (0,))))
        prob_grad = dot(g, v, ((1,), (1,)))
        inner = jnp.sum(prob_grad * probs, axis=1, keepdims=True)
        score_grad = (probs * (prob_grad - inner)).astype(bf16)
        query_grad.append(dot(score_grad, k, ((1,), (0,))) * scale)
        key_grad.append(dot(score_grad, q, ((0,), (0,))) * scale)
        value_grad.append(dot(low, g, ((0,), (0,))))
    context_ref[...] = jnp.concatenate(context, axis=1).astype(bf16)
    grad_ref[:, :width] = rotate(jnp.concatenate(query_grad, axis=1), -1.0).astype(bf16)
    grad_ref[:, width : 2 * width] = rotate(jnp.concatenate(key_grad, axis=1), -1.0).astype(bf16)
    grad_ref[:, 2 * width :] = jnp.concatenate(value_grad, axis=1).astype(bf16)


def attention(tables, mixed, outer, length):
    rows, width = outer.shape
    wide = lambda columns: pl.BlockSpec((length, columns), lambda i: (i, 0))
    return pl.pallas_call(
        attention_kernel,
        grid=(rows // length,),
        in_specs=[wide(LANES)] * 4 + [wide(3 * width), wide(width)],
        out_specs=[wide(width), wide(3 * width)],
        out_shape=[
            jax.ShapeDtypeStruct((rows, width), bf16),
            jax.ShapeDtypeStruct((rows, 3 * width), bf16),
        ],
        cost_estimate=pl.CostEstimate(
            flops=14 * rows * length * width * 4,
            bytes_accessed=rows * width * 24,
            transcendentals=rows * length * width // HEAD_DIM,
        ),
        compiler_params=pltpu.CompilerParams(vmem_limit_bytes=VMEM),
    )(*tables, mixed, outer)


def pack_kernel(spots_ref, fc1_ref, q_ref, k_ref, v_ref, small_ref, out_ref):
    part, own = fc1_ref.shape
    piece = q_ref.shape[1]
    out_ref[:part, :own] = fc1_ref[...]
    for i, ref in enumerate((q_ref, k_ref, v_ref)):
        out_ref[:part, own + i * piece : own + (i + 1) * piece] = ref[...]
    out_ref[part:, :] = small_ref[...]


def pack(w_fc1, w_qkv, small, row, place, part, own, piece):
    width = w_fc1.shape[0]
    third = w_qkv.shape[1] // 3 // piece
    cols = own + 3 * piece
    spots = jnp.stack([row, place]).astype(jnp.int32)
    cut = lambda i: pl.BlockSpec((part, piece), lambda _, spots: (spots[0], i * third + spots[1]))
    return pl.pallas_call(
        pack_kernel,
        grid_spec=pltpu.PrefetchScalarGridSpec(
            num_scalar_prefetch=1,
            grid=(1,),
            in_specs=[
                pl.BlockSpec((part, own), lambda _, spots: (spots[0], spots[1])),
                cut(0),
                cut(1),
                cut(2),
                pl.BlockSpec(small.shape, lambda _, spots: (0, 0)),
            ],
            out_specs=pl.BlockSpec((part + small.shape[0], cols), lambda _, spots: (0, 0)),
        ),
        out_shape=jax.ShapeDtypeStruct((part + small.shape[0], cols), bf16),
        cost_estimate=pl.CostEstimate(flops=0, bytes_accessed=part * cols * 4, transcendentals=0),
        compiler_params=pltpu.CompilerParams(vmem_limit_bytes=VMEM),
    )(spots, w_fc1, w_qkv, w_qkv, w_qkv, small)


def assemble_kernel(order_ref, spots_ref, fc1_ref, q_ref, k_ref, v_ref, got_ref, fc1_out, qkv_out):
    planes, own, piece = fc1_out.shape[0], fc1_ref.shape[1], q_ref.shape[1]
    here = spots_ref[0]
    fc1_out[here] = fc1_ref[...]
    for i, ref in enumerate((q_ref, k_ref, v_ref)):
        qkv_out[here, :, i * piece : (i + 1) * piece] = ref[...]
    for k in range(1, planes):
        there = spots_ref[k]
        fc1_out[there] = got_ref[k - 1, :, :own]
        qkv_out[there] = got_ref[k - 1, :, own:]


def assemble(w_fc1, w_qkv, got, order, spots, own, piece):
    blocks, others, rows, cols = got.shape
    planes = others + 1
    height = w_fc1.shape[0]
    third = w_qkv.shape[1] // 3 // piece
    cut = lambda i: pl.BlockSpec(
        (None, rows, piece), lambda n, order, spots: (order[n], 0, i * third + spots[planes])
    )
    result = lambda size: pl.BlockSpec(
        (planes, None, rows, size), lambda n, order, spots: (0, order[n], 0, 0)
    )
    fc1, qkv = pl.pallas_call(
        assemble_kernel,
        grid_spec=pltpu.PrefetchScalarGridSpec(
            num_scalar_prefetch=2,
            grid=(blocks,),
            in_specs=[
                pl.BlockSpec(
                    (None, rows, own), lambda n, order, spots: (order[n], 0, spots[planes])
                ),
                cut(0),
                cut(1),
                cut(2),
                pl.BlockSpec((None, others, rows, cols), lambda n, order, spots: (n, 0, 0, 0)),
            ],
            out_specs=[result(own), result(3 * piece)],
        ),
        out_shape=[
            jax.ShapeDtypeStruct((planes, blocks, rows, own), bf16),
            jax.ShapeDtypeStruct((planes, blocks, rows, 3 * piece), bf16),
        ],
        cost_estimate=pl.CostEstimate(
            flops=0, bytes_accessed=planes * height * cols * 4, transcendentals=0
        ),
        compiler_params=pltpu.CompilerParams(vmem_limit_bytes=VMEM),
    )(
        order,
        spots,
        w_fc1.reshape(blocks, rows, -1),
        *[w_qkv.reshape(blocks, rows, -1)] * 3,
        got,
    )
    return fc1.reshape(planes * height, own), qkv.reshape(planes * height, 3 * piece)


def place_columns(mine, other, order, spots, factor):
    blocks, rows, columns = mine.shape
    planes = spots.shape[0] - 2
    piece = columns // planes
    spec = pl.BlockSpec((None, rows, columns), lambda i, order, spots: (i, 0, 0))

    def kernel(order_ref, spots_ref, mine_ref, other_ref, out_ref):
        for e, ref in enumerate((mine_ref, other_ref)):
            for k in range(planes):
                column = (spots_ref[k] * CORES + spots_ref[planes + e]) * piece
                out_ref[:, pl.ds(pl.multiple_of(column, LANES), piece)] = (
                    ref[:, k * piece : (k + 1) * piece].astype(f32) * factor
                )

    return pl.pallas_call(
        kernel,
        grid_spec=pltpu.PrefetchScalarGridSpec(
            num_scalar_prefetch=2,
            grid=(blocks,),
            in_specs=[spec, spec],
            out_specs=pl.BlockSpec((rows, 2 * columns), lambda i, order, spots: (order[i], 0)),
        ),
        out_shape=jax.ShapeDtypeStruct((blocks * rows, 2 * columns), f32),
        cost_estimate=pl.CostEstimate(
            flops=blocks * rows * columns * 2,
            bytes_accessed=blocks * rows * columns * 12,
            transcendentals=0,
        ),
        compiler_params=pltpu.CompilerParams(vmem_limit_bytes=VMEM),
    )(order, spots, mine, other)


def place_mixed(mine, other, order, spots, shape, factor):
    A, B = shape
    J = A * B
    _, part, columns = mine.shape
    planes = spots.shape[0] - 2
    piece = columns // planes // 2
    aligned = part % LANES == 0
    first = pl.BlockSpec((None, part, columns), lambda i, order, spots: (i, 0, 0))
    second = pl.BlockSpec(
        (None, part, columns), lambda i, order, spots: (J + (i % B) * A + i // B, 0, 0)
    )

    def kernel(order_ref, spots_ref, m0_ref, m1_ref, o0_ref, o1_ref, qkv_ref, *rest):
        row = order_ref[pl.program_id(0)]
        for e, (f_ref, s_ref) in enumerate(((m0_ref, m1_ref), (o0_ref, o1_ref))):
            core = spots_ref[planes + e]
            for k in range(planes):
                for i in range(3):
                    ref = s_ref if i == 2 else f_ref
                    start = (2 * k + i % 2) * piece
                    column = ((i * planes + spots_ref[k]) * CORES + core) * piece
                    qkv_ref[:, pl.ds(pl.multiple_of(column, LANES), piece)] = (
                        ref[:, start : start + piece].astype(f32) * factor
                    )
                if aligned:
                    block = s_ref[:, (2 * k + 1) * piece : (2 * k + 2) * piece].astype(f32) * factor
                    rest[0][
                        pl.ds(pl.multiple_of(core * piece, LANES), piece),
                        pl.ds(pl.multiple_of((spots_ref[k] * J + row) * part, LANES), part),
                    ] = block.T

    out_shape = [jax.ShapeDtypeStruct((J * part, 3 * planes * CORES * piece), f32)]
    out_specs = [
        pl.BlockSpec((part, 3 * planes * CORES * piece), lambda i, order, spots: (order[i], 0))
    ]
    if aligned:
        out_shape.append(jax.ShapeDtypeStruct((CORES * piece, planes * J * part), f32))
        out_specs.append(
            pl.BlockSpec((CORES * piece, planes * J * part), lambda i, order, spots: (0, 0))
        )
    results = pl.pallas_call(
        kernel,
        grid_spec=pltpu.PrefetchScalarGridSpec(
            num_scalar_prefetch=2,
            grid=(J,),
            in_specs=[first, second, first, second],
            out_specs=out_specs,
        ),
        out_shape=out_shape,
        cost_estimate=pl.CostEstimate(
            flops=J * part * columns * 4,
            bytes_accessed=J * part * columns * 24,
            transcendentals=0,
        ),
        compiler_params=pltpu.CompilerParams(vmem_limit_bytes=VMEM),
    )(order, spots, mine, mine, other, other)
    if aligned:
        return results
    inverse = jnp.argsort(spots[:planes])
    rows_at = jnp.argsort(order)
    pair = jnp.stack([mine, other])[:, J:].reshape(2, B, A, part, planes, 2, piece)[..., 1, :]
    pair = jnp.swapaxes(pair, 1, 2).reshape(2, J, part, planes, piece)
    pair = jnp.take(jnp.take(pair, rows_at, axis=1), inverse, axis=3)
    pair = jnp.take(pair, jnp.argsort(spots[planes:]), axis=0)
    flipped = jnp.transpose(pair, (0, 4, 3, 1, 2)).reshape(CORES * piece, planes * J * part)
    return results[0], flipped.astype(f32) * factor


def place_rows(mine, other, order, factor):
    blocks, rows, columns = mine.shape

    def kernel(order_ref, mine_ref, other_ref, out_ref):
        here = pl.program_id(0)

        @pl.when(here < blocks)
        def _():
            out_ref[...] = mine_ref[...].astype(f32) * factor

        @pl.when(here >= blocks)
        def _():
            out_ref[...] = other_ref[...].astype(f32) * factor

    return pl.pallas_call(
        kernel,
        grid_spec=pltpu.PrefetchScalarGridSpec(
            num_scalar_prefetch=1,
            grid=(2 * blocks,),
            in_specs=[
                pl.BlockSpec(
                    (None, rows, columns), lambda i, order: (jnp.minimum(i, blocks - 1), 0, 0)
                ),
                pl.BlockSpec(
                    (None, rows, columns), lambda i, order: (jnp.maximum(i - blocks, 0), 0, 0)
                ),
            ],
            out_specs=pl.BlockSpec((rows, columns), lambda i, order: (order[i], 0)),
        ),
        out_shape=jax.ShapeDtypeStruct((2 * blocks * rows, columns), f32),
        cost_estimate=pl.CostEstimate(
            flops=blocks * rows * columns * 2,
            bytes_accessed=blocks * rows * columns * 12,
            transcendentals=0,
        ),
        compiler_params=pltpu.CompilerParams(vmem_limit_bytes=VMEM),
    )(order, mine, other)


def tie(x, *after):
    return lax.optimization_barrier((x, after))[0]


class Links:
    def __init__(self, planes, replicas):
        self.S = planes
        self.J = replicas // CORES
        self.B = 2 if self.J % 2 == 0 else 1
        self.A = self.J // self.B
        dp = lax.axis_index("dp")
        self.s = lax.axis_index("shard")
        self.c = dp % CORES
        self.j = dp // CORES
        self.b = self.j % self.B
        self.a = self.j // self.B
        self.size = {"a": self.A, "b": self.B, "c": CORES, "s": self.S}
        self.here = {"a": self.a, "b": self.b, "c": self.c, "s": self.s}

    def move(self, x, da=0, db=0, dc=0, ds=0):
        pairs = []
        for a in range(self.A):
            for b in range(self.B):
                for c in range(CORES):
                    for s in range(self.S):
                        to = ((a + da) % self.A, (b + db) % self.B, (c + dc) % CORES, (s + ds) % self.S)
                        pairs.append((self.flat(a, b, c, s), self.flat(*to)))
        return lax.ppermute(x, AXES, pairs)

    def flat(self, a, b, c, s):
        return ((a * self.B + b) * CORES + c) * self.S + s

    def line(self, x, axis, after=()):
        size = self.size[axis]
        sent = tie(x, *after)
        return [self.move(sent, **{"d" + axis: k}) for k in range(1, size)]

    def gather(self, pair, after=()):
        got = [self.line(pair[0], "b", after), self.line(pair[1], "a", after)]
        return [jnp.stack([x] + g) for x, g in zip(pair, got)], got

    def gather_more(self, pair, after=()):
        got = [self.line(pair[0], "a", after), self.line(pair[1], "b", after)]
        both = [jnp.stack([x] + g).reshape((self.J,) + x.shape[1:]) for x, g in zip(pair, got)]
        return jnp.concatenate(both), got

    def plane_order(self):
        a = (self.a - jnp.arange(self.A)) % self.A
        b = (self.b - jnp.arange(self.B)) % self.B
        first = (a[:, None] * self.B + b[None, :]).reshape(-1)
        second = (a[None, :] * self.B + b[:, None]).reshape(-1)
        return jnp.concatenate([first * 2, second * 2 + 1]).astype(jnp.int32)

    def spread(self, x, axis, dim, after=(), rider=None):
        size, here = self.size[axis], self.here[axis]
        own = pick(x, here, dim)
        got = []
        for k in range(1, size):
            sent = pick(x, (here + k) % size, dim)
            if rider is not None:
                sent = jnp.concatenate([sent.reshape(-1, sent.shape[-1]), twofold(rider)], axis=0)
            got.append(self.move(tie(sent, *after), **{"d" + axis: k}))

        def total():
            result, carried = own.astype(f32), rider
            for g in got:
                if rider is not None:
                    count = g.shape[0] - 2 * rider.shape[0]
                    carried = carried + onefold(g[count:])
                    g = g[:count].reshape(own.shape)
                result = result + g.astype(f32)
            return result.astype(bf16), carried

        return got, total


def twofold(x):
    high = lax.reduce_precision(x, 8, 7)
    return jnp.concatenate([high.astype(bf16), (x - high).astype(bf16)], axis=0)


def onefold(x):
    count = x.shape[0] // 2
    return x[:count].astype(f32) + x[count:].astype(f32)


def as_rows(vector, width, multiple):
    count = -(-vector.shape[0] // (width * multiple)) * multiple
    return jnp.pad(vector, (0, count * width - vector.shape[0])).reshape(count, width)


def pick(x, index, axis):
    return lax.dynamic_index_in_dim(x, index, axis, keepdims=False)


def in_order(held, here):
    size = len(held)
    backwards = jnp.stack(held[::-1])
    return lax.dynamic_slice_in_dim(
        jnp.concatenate([backwards, backwards]), size - 1 - here, size, 0
    )


def moments(x):
    average = jnp.mean(x, axis=1, keepdims=True)
    centred = x - average
    inverse = lax.rsqrt(jnp.mean(centred * centred, axis=1, keepdims=True) + epsilon)
    return average, inverse


def local(
    tokens,
    segments,
    ln_gain,
    ln_bias,
    w_qkv,
    b_qkv,
    w_out,
    b_out,
    w_fc1,
    b_fc1,
    w_fc2,
    b_fc2,
    cotangent,
):
    planes = lax.axis_size("shard")
    replicas = lax.axis_size("dp")
    net = Links(planes, replicas)
    S, J, A, B, c, j, s = net.S, net.J, net.A, net.B, net.c, net.j, net.s
    seqs, length, width = tokens.shape
    rows = seqs * length
    ff = w_fc1.shape[1]
    ff_own = ff // (S * CORES)
    mix_own = width // (S * CORES)
    height = width // S
    part = height // J
    members = S * CORES
    total = members * rows
    order = net.plane_order()
    order_rows = order[:J] // 2
    spots = jnp.concatenate([(s - jnp.arange(S)) % S, jnp.stack([c, 1 - c])]).astype(jnp.int32)

    own_tokens = tokens.reshape(rows, width)
    own_cot = cotangent.reshape(rows, width)
    tok = [own_tokens, net.move(own_tokens, ds=1)]
    cot = [own_cot]

    vectors = [ln_gain, ln_bias, b_qkv, b_out, b_fc1, b_fc2, segments.reshape(-1).astype(bf16)]
    small = jnp.concatenate(vectors)
    size = small.shape[0]
    packed = as_rows(small, ff_own + 3 * mix_own, 16)
    sent = [
        pack(w_fc1, w_qkv, packed, j, (s + k) % S * CORES + c, part, ff_own, mix_own)
        for k in range(1, S)
    ]
    sent = tie(sent, tok[1])
    got = [net.move(sent[k - 1], ds=k) for k in range(1, S)]

    held_small = [small] + [g[part:].reshape(-1)[:size] for g in got]
    marks = jnp.stack([v[size - rows :] for v in held_small])
    cut = part // 2
    halves = [jnp.stack([g[:cut] for g in got]), jnp.stack([g[cut:part] for g in got])]
    tok.append(net.move(tie(tok[-1], got), ds=1))
    cot.append(net.move(tie(cot[-1], got), ds=1))
    halves, arrived = net.gather(halves)
    other_marks = net.move(marks, dc=1)
    marks = jnp.stack([marks, other_marks], axis=1)
    blocks = None
    while len(cot) < S:
        after = (tok[-1], cot[-1], arrived)
        if len(tok) < S:
            tok.append(net.move(tie(tok[-1], after), ds=1))
        cot.append(net.move(tie(cot[-1], after), ds=1))
        if blocks is None:
            blocks, arrived = net.gather_more(halves, after)
    tables = rotary_tables(marks.reshape(members * seqs, length).astype(jnp.int32))
    small_all = in_order(held_small, s)
    whole = []
    start = 0
    for vector in vectors[:-1]:
        whole.append(small_all[:, start : start + vector.shape[0]].reshape(-1).astype(f32))
        start += vector.shape[0]
    gain_full, shift_full, qkv_bias, out_bias, fc1_bias, fc2_bias = whole
    fc1_bias = lax.dynamic_slice_in_dim(fc1_bias, (s * CORES + c) * ff_own, ff_own, 0)
    qkv_bias = lax.dynamic_slice_in_dim(
        qkv_bias.reshape(3, width), (s * CORES + c) * mix_own, mix_own, 1
    ).reshape(-1)

    mine = tie(jnp.stack(tok), (cot[:-1], arrived, tables))
    other = net.move(mine, dc=1)
    token_rows = jnp.stack([mine, other], axis=1).reshape(total, width)
    mine = jnp.stack(cot)
    other = net.move(mine, dc=1)
    cot_rows = jnp.stack([mine, other], axis=1).reshape(total, width)
    fc1_cols, qkv_cols = assemble(
        w_fc1,
        w_qkv,
        blocks,
        order,
        jnp.concatenate([spots[:S], (s * CORES + c)[None]]).astype(jnp.int32),
        ff_own,
        mix_own,
    )
    fc2_rows = lax.dynamic_slice_in_dim(w_fc2, c * ff_own, ff_own, 0)
    out_rows = lax.dynamic_slice_in_dim(w_out, c * mix_own, mix_own, 0)

    average, inverse = moments(token_rows.astype(f32))
    hidden_in = ((token_rows.astype(f32) - average) * inverse * gain_full + shift_full).astype(bf16)

    hidden = jnp.dot(hidden_in, fc1_cols, preferred_element_type=f32) + fc1_bias
    active, gelu_back = jax.vjp(lambda v: jax.nn.gelu(v, approximate=True), hidden)
    active = active.astype(bf16)
    fc2_term = jnp.einsum("tf,td->fd", active, cot_rows, preferred_element_type=f32).astype(bf16)

    by_rows = lambda x: [
        x.reshape(A, B, 2, x.shape[0] // (2 * J), x.shape[1])[:, :, i] for i in range(2)
    ]
    by_planes = lambda x: [
        x.reshape(2, S // 2, A, B, part, x.shape[1])[i] for i in range(2)
    ]

    fc2_halves = by_rows(fc2_term)
    got_0, sum_0 = net.spread(fc2_halves[0], "a", 0)
    got_1, sum_1 = net.spread(fc2_halves[1], "b", 1)
    arrived = (got_0, got_1)
    late_cot = tie(cot_rows, fc2_term)
    active_grad = jnp.einsum("td,fd->tf", late_cot, fc2_rows, preferred_element_type=f32)
    hidden_grad = gelu_back(active_grad)[0].astype(bf16)
    fc1_term = jnp.einsum("td,tf->df", hidden_in, hidden_grad, preferred_element_type=f32).astype(
        bf16
    )

    fc1_halves = by_planes(fc1_term)
    got_2, sum_2 = net.spread(fc1_halves[0], "a", 1, arrived)
    got_3, sum_3 = net.spread(fc1_halves[1], "b", 2, arrived)
    got_0, sum_0 = net.spread(sum_0()[0], "b", 0)
    got_1, sum_1 = net.spread(sum_1()[0], "a", 0)
    late_in, late_cot = tie((hidden_in, cot_rows), fc1_term, arrived)
    arrived = (got_0, got_1, got_2, got_3)
    mixed = jnp.dot(late_in, qkv_cols, preferred_element_type=f32) + qkv_bias
    context_grad = jnp.einsum("te,de->td", late_cot, out_rows, preferred_element_type=f32).astype(
        bf16
    )
    context, mixed_grad = attention(tables, mixed, context_grad, length)

    got_2, sum_2 = net.spread(sum_2()[0], "b", 1, arrived)
    got_3, sum_3 = net.spread(sum_3()[0], "a", 1, arrived)
    fc2_halves, got_4 = net.gather([sum_0()[0], sum_1()[0]], arrived)
    late_in, late_cot, late_mixed, late_context = tie(
        (hidden_in, cot_rows, mixed_grad, context), arrived
    )
    arrived = (got_2, got_3, got_4)
    transposed = lambda x, y: jnp.einsum("td,te->de", x, y, preferred_element_type=f32).astype(bf16)
    mixed_first = transposed(late_in, late_mixed[:, : 2 * mix_own])
    mixed_second = jnp.concatenate(
        [transposed(late_in, late_mixed[:, 2 * mix_own :]), transposed(late_cot, late_context)],
        axis=1,
    )

    def to_plane(term, after=(), rider=None):
        held = []
        for k in range(1, S):
            sent = pick(term, (s + k) % S, 0)
            if rider is not None:
                sent = jnp.concatenate([sent, rider((s + k) % S)], axis=0)
            held.append(net.move(tie(sent, *after), ds=k))
        return held

    fc1_sum = jnp.concatenate([sum_2()[0], sum_3()[0]])
    fc1_got = to_plane(fc1_sum, arrived)
    fc2_all, got_4 = net.gather_more(fc2_halves, arrived)
    late_context, late_active, late_grad, late_mixed = tie(
        (context, active, hidden_grad, mixed_grad), mixed_first, mixed_second, arrived
    )
    arrived = (fc1_got, got_4)
    back = jnp.einsum("te,de->td", late_mixed, qkv_cols, preferred_element_type=f32) + jnp.einsum(
        "tf,df->td", late_grad, fc1_cols, preferred_element_type=f32
    )
    branch = jnp.dot(late_context, out_rows, preferred_element_type=f32) + jnp.dot(
        late_active, fc2_rows, preferred_element_type=f32
    )
    normed = (token_rows.astype(f32) - average) * inverse
    sums = [
        jnp.sum(back * normed, axis=0),
        jnp.sum(back, axis=0),
        jnp.sum(mixed_grad, axis=0, dtype=f32),
        jnp.sum(hidden_grad, axis=0, dtype=f32),
        jnp.sum(cot_rows, axis=0, dtype=f32),
    ]
    sizes = [v.shape[0] for v in sums]
    rider = as_rows(jnp.concatenate(sums), 2 * mix_own, 16)

    fc1_part = jnp.concatenate([pick(fc1_sum, s, 0)] + fc1_got, axis=1)
    pair = lambda x: x.reshape(S, A, B, part, x.shape[1])
    got_0, sum_0 = net.spread(pair(mixed_first), "a", 1, arrived, rider)
    got_1, sum_1 = net.spread(pair(mixed_second), "b", 2, arrived)
    fc1_halves, got_2 = net.gather([fc1_part[:cut], fc1_part[cut:]], arrived)
    acts = jnp.stack([branch, back]).reshape(2, S, CORES, rows, width)
    acts_other = net.move(tie(acts[:, :, 1].astype(bf16), arrived), dc=1)
    arrived = (got_0, got_1, got_2, acts_other)

    acts = acts[:, :, 0] + acts_other.astype(f32)
    acts = jnp.swapaxes(in_order([acts[:, k].astype(bf16) for k in range(S)], s), 1, 2)
    acts = lax.psum_scatter(
        acts.reshape(S, rows, 2 * width), "shard", scatter_dimension=0, tiled=False
    ).reshape(rows, 2, width)
    mixed_0, rider = sum_0()
    got_0, sum_0 = net.spread(mixed_0, "b", 1, arrived, rider)
    got_1, sum_1 = net.spread(sum_1()[0], "a", 1, arrived)
    fc2_other = net.move(tie(fc2_all, arrived), dc=1)
    arrived = (got_0, got_1, fc2_other)

    mixed_0, rider = sum_0()
    mixed_1 = sum_1()[0]
    sums = []
    flat, start = rider.reshape(-1), 0
    for count in sizes:
        sums.append(flat[start : start + count])
        start += count
    norm_sums = jnp.stack(sums[:2])

    def riding(plane):
        own = lax.dynamic_slice_in_dim(norm_sums, plane * height, height, 1).reshape(-1)
        return twofold(as_rows(jnp.concatenate([own, sums[2]]), 3 * mix_own, 8))

    mixed_sum = jnp.concatenate([mixed_0, mixed_1[:, :, :mix_own]], axis=2)
    mixed_got = to_plane(mixed_sum, arrived, riding)
    fc1_all, got_2 = net.gather_more(fc1_halves, arrived)
    factor = 1.0 / math.sqrt(rows * planes * replicas)
    row_order = jnp.concatenate([c * 2 * J + order, (1 - c) * 2 * J + order]).astype(jnp.int32)
    fc2_all, fc2_other = tie((fc2_all, fc2_other), arrived)
    fc2_own = place_rows(fc2_all, fc2_other, row_order, factor)
    arrived = (mixed_got, got_2)

    held = [pick(mixed_sum, s, 0)] + [g[:part] for g in mixed_got]
    first = jnp.concatenate([x[:, : 2 * mix_own] for x in held], axis=1)
    second = jnp.concatenate(
        [
            x
            for k in range(S)
            for x in (held[k][:, 2 * mix_own :], pick(mixed_1, (s - k) % S, 0)[:, mix_own:])
        ],
        axis=1,
    )
    mixed_halves, got_0 = net.gather([first, second], arrived)
    fc1_other = net.move(tie(fc1_all, arrived), dc=1)
    ridden = [onefold(riding(s))] + [onefold(g[part:]) for g in mixed_got]
    ridden = [r.reshape(-1)[: 2 * height + 3 * mix_own] for r in ridden]
    ridden = jnp.concatenate(
        [sum(r[: 2 * height] for r in ridden), sums[3]] + [r[2 * height :] for r in ridden]
    )
    ridden_other = net.move(tie(ridden, arrived), dc=1)
    arrived = (got_0, fc1_other, ridden_other)

    mixed_all, got_0 = net.gather_more(mixed_halves, arrived)
    fc1_all, fc1_other = tie((fc1_all, fc1_other), arrived, fc2_own)
    fc1_own = place_columns(fc1_all, fc1_other, order, spots, factor)

    mixed_other = net.move(tie(mixed_all, fc1_own), dc=1)
    qkv_own, out_own = place_mixed(mixed_all, mixed_other, order_rows, spots, (A, B), factor)

    own_inputs = tokens.reshape(rows, width).astype(f32)
    output = (own_inputs + acts[:, 0].astype(f32) + (out_bias + fc2_bias)).astype(bf16)
    average, inverse = moments(own_inputs)
    normed = (own_inputs - average) * inverse
    scaled = acts[:, 1].astype(f32) * gain_full
    input_grad = own_cot.astype(f32) + inverse * (
        scaled
        - jnp.mean(scaled, axis=1, keepdims=True)
        - normed * jnp.mean(scaled * normed, axis=1, keepdims=True)
    )

    gain_own = (ridden[:height] + ridden_other[:height]) * factor
    shift_own = (ridden[height : 2 * height] + ridden_other[height : 2 * height]) * factor
    both = jnp.where(
        c == 0, jnp.stack([ridden, ridden_other]), jnp.stack([ridden_other, ridden])
    )[:, 2 * height :]
    fc1_bias_own = both[:, :ff_own].reshape(-1) * factor
    mixed_sums = both[:, ff_own:].reshape(CORES, S, 3, mix_own)
    mixed_sums = in_order([mixed_sums[:, k] for k in range(S)], s)
    mixed_sums = jnp.transpose(mixed_sums, (2, 0, 1, 3)).reshape(S, -1)
    qkv_bias_own = pick(mixed_sums, s, 0) * factor
    bias_own = pick(sums[4].reshape(S, height), s, 0) * factor
    return (
        output.reshape(tokens.shape),
        input_grad.reshape(tokens.shape),
        gain_own,
        shift_own,
        qkv_own,
        qkv_bias_own,
        out_own,
        bias_own,
        fc1_own,
        fc1_bias_own,
        fc2_own,
        bias_own,
    )


def solution(mesh):
    return jax.shard_map(
        local,
        mesh=mesh,
        in_specs=(
            P(("dp", "shard"), None, None),
            P(("dp", "shard"), None),
            P("shard"),
            P("shard"),
            P("shard", None),
            P("shard"),
            P("shard", None),
            P("shard"),
            P("shard", None),
            P("shard"),
            P("shard", None),
            P("shard"),
            P(("dp", "shard"), None, None),
        ),
        out_specs=(
            P(("dp", "shard"), None, None),
            P(("dp", "shard"), None, None),
            P("shard"),
            P("shard"),
            P("shard", None),
            P("shard"),
            P("shard", None),
            P("shard"),
            P("shard", None),
            P("shard"),
            P("shard", None),
            P("shard"),
        ),
        check_vma=False,
    )
```

```python
import math

import jax
import jax.numpy as jnp
from jax import lax
from jax.experimental import pallas as pl
from jax.experimental.pallas import tpu as pltpu
from jax.experimental.layout import Layout, with_layout_constraint
from jax.sharding import PartitionSpec as P

HEADS = 32
HEAD_DIM = 64
ROT = 32
CORES = 2
LANES = 128

epsilon = 1e-05
masked_value = -1e30
AXES = ("dp", "shard")
f32 = jnp.float32
bf16 = jnp.bfloat16
VMEM = 48 * 1024 * 1024


def rotary_tables(segments):
    seqs, length = segments.shape
    positions = jnp.broadcast_to(jnp.arange(length, dtype=jnp.int32), segments.shape)
    change = jnp.concatenate(
        [jnp.ones((seqs, 1), dtype=bool), segments[:, 1:] != segments[:, :-1]], axis=1
    )
    run_start = lax.cummax(jnp.where(change, positions, 0), axis=1)
    distance = (positions - run_start).astype(f32).reshape(-1, 1)
    lane = jnp.arange(LANES, dtype=jnp.int32) % HEAD_DIM
    half = ROT // 2
    frequency = jnp.exp((lane % half).astype(f32) * (-2.0 * math.log(10000.0) / ROT))
    angles = distance * frequency[None, :]
    sines = jnp.sin(angles)
    cos_table = jnp.where(lane < ROT, jnp.cos(angles), 1.0)
    low_table = jnp.where(lane < half, -sines, 0.0)
    high_table = jnp.where((lane >= half) & (lane < ROT), sines, 0.0)
    starts = jnp.broadcast_to(run_start.reshape(-1, 1), (seqs * length, LANES))
    return starts, cos_table, low_table, high_table


def attention_kernel(
    starts_ref, cos_ref, low_ref, high_ref, mixed_ref, outer_ref, context_ref, grad_ref
):
    length, width = outer_ref.shape
    half = ROT // 2
    scale = HEAD_DIM ** (-0.5)

    def wide(table):
        return jnp.concatenate([table[...]] * (width // LANES), axis=1)

    cos_table, low_table, high_table = wide(cos_ref), wide(low_ref), wide(high_ref)

    def rotate(v, sign):
        turned = pltpu.roll(v, width - half, 1) * low_table + pltpu.roll(v, half, 1) * high_table
        return v * cos_table + sign * turned

    queries = rotate(mixed_ref[:, :width], 1.0).astype(bf16)
    key_rows = rotate(mixed_ref[:, width : 2 * width], 1.0).astype(bf16)
    values = mixed_ref[:, 2 * width :].astype(bf16)
    outer = outer_ref[...]
    row = lax.broadcasted_iota(jnp.int32, (length, length), 0)
    column = lax.broadcasted_iota(jnp.int32, (length, length), 1)
    allowed = (column <= row) & (column >= starts_ref[...])
    spans = [slice(h * HEAD_DIM, (h + 1) * HEAD_DIM) for h in range(width // HEAD_DIM)]
    block = lambda x, h: x[h * length : (h + 1) * length]
    heads = range(len(spans))
    allowed = jnp.concatenate([allowed] * len(spans), axis=0)
    scores = jnp.concatenate([dot(queries[:, p], key_rows[:, p], ((1,), (1,))) for p in spans], axis=0)
    scores = jnp.where(allowed, scores * scale, masked_value)
    weights = jnp.exp(scores - jnp.max(scores, axis=1, keepdims=True))
    probs = weights / jnp.sum(weights, axis=1, keepdims=True)
    low = probs.astype(bf16)
    prob_grad = jnp.concatenate([dot(outer[:, p], values[:, p], ((1,), (1,))) for p in spans], axis=0)
    inner = jnp.sum(prob_grad * probs, axis=1, keepdims=True)
    score_grad = (probs * (prob_grad - inner)).astype(bf16)
    context = [dot(block(low, h), values[:, spans[h]], ((1,), (0,))) for h in heads]
    value_grad = [dot(block(low, h), outer[:, spans[h]], ((0,), (0,))) for h in heads]
    query_grad = [dot(block(score_grad, h), key_rows[:, spans[h]], ((1,), (0,))) for h in heads]
    key_grad = [dot(block(score_grad, h), queries[:, spans[h]], ((0,), (0,))) for h in heads]
    side = lambda x: jnp.concatenate(x, axis=1)
    context_ref[...] = side(context).astype(bf16)
    grad_ref[:, :width] = rotate(side(query_grad) * scale, -1.0).astype(bf16)
    grad_ref[:, width : 2 * width] = rotate(side(key_grad) * scale, -1.0).astype(bf16)
    grad_ref[:, 2 * width :] = side(value_grad).astype(bf16)


def attention(tables, mixed, outer, length):
    rows, width = outer.shape
    wide = lambda columns: pl.BlockSpec((length, columns), lambda i: (i, 0))
    return pl.pallas_call(
        attention_kernel,
        grid=(rows // length,),
        in_specs=[wide(LANES)] * 4 + [wide(3 * width), wide(width)],
        out_specs=[wide(width), wide(3 * width)],
        out_shape=[
            jax.ShapeDtypeStruct((rows, width), bf16),
            jax.ShapeDtypeStruct((rows, 3 * width), bf16),
        ],
        cost_estimate=pl.CostEstimate(flops=4 * 10**9, bytes_accessed=0, transcendentals=0),
        compiler_params=pltpu.CompilerParams(vmem_limit_bytes=VMEM),
    )(*tables, mixed, outer)


def call(kernel, grid, in_specs, out_specs, out_shape, scalars=0, us=0, **more):
    return pl.pallas_call(
        kernel,
        grid_spec=pltpu.PrefetchScalarGridSpec(
            num_scalar_prefetch=scalars, grid=grid, in_specs=in_specs, out_specs=out_specs
        ),
        out_shape=out_shape,
        cost_estimate=pl.CostEstimate(flops=us * 10**9 // 3, bytes_accessed=0, transcendentals=0),
        compiler_params=pltpu.CompilerParams(vmem_limit_bytes=VMEM),
        **more,
    )


def dot(a, b, dims):
    return lax.dot_general(a, b, (dims, ((), ())), preferred_element_type=f32)


def pack(w_fc1, w_qkv, row, core, planes, part, own, piece):
    third = w_qkv.shape[1] // 3 // piece
    cols = own + 3 * piece
    spots = jnp.stack([row, core]).astype(jnp.int32)

    def kernel(spots_ref, fc1_ref, q_ref, k_ref, v_ref, out_ref):
        out_ref[:, :own] = fc1_ref[...]
        for i, ref in enumerate((q_ref, k_ref, v_ref)):
            out_ref[:, own + i * piece : own + (i + 1) * piece] = ref[...]

    cut = lambda i: pl.BlockSpec(
        (part, piece), lambda p, spots: (spots[0], i * third + p * CORES + spots[1])
    )
    return call(
        kernel,
        (planes,),
        [
            pl.BlockSpec((part, own), lambda p, spots: (spots[0], p * CORES + spots[1])),
            cut(0),
            cut(1),
            cut(2),
        ],
        pl.BlockSpec((None, part, cols), lambda p, spots: (p, 0, 0)),
        jax.ShapeDtypeStruct((planes, part, cols), bf16),
        scalars=1,
    )(spots, w_fc1, w_qkv, w_qkv, w_qkv)


def assemble(w_fc1, w_qkv, arrays, order, spots, own, piece, blocks, before=None):
    others, rows, cols = arrays[0].shape
    planes = others + 1
    height = w_fc1.shape[0]
    third = w_qkv.shape[1] // 3 // piece

    def kernel(order_ref, spots_ref, fc1_ref, q_ref, k_ref, v_ref, *refs):
        fc1_out, qkv_out = refs[-2:]
        here = spots_ref[0]
        fc1_out[here] = fc1_ref[...]
        for i, ref in enumerate((q_ref, k_ref, v_ref)):
            qkv_out[here, :, i * piece : (i + 1) * piece] = ref[...]
        for n in range(len(arrays)):

            @pl.when(pl.program_id(0) == n)
            def _(ref=refs[n]):
                for k in range(1, planes):
                    there = spots_ref[k]
                    fc1_out[there] = ref[k - 1, :, :own]
                    qkv_out[there] = ref[k - 1, :, own:]

    cut = lambda i: pl.BlockSpec(
        (None, rows, piece), lambda n, order, spots: (order[n], 0, i * third + spots[planes])
    )
    result = lambda size: pl.BlockSpec(
        (planes, None, rows, size), lambda n, order, spots: (0, order[n], 0, 0)
    )
    more = {}
    if before is not None:
        first = 6 + len(arrays)
        more["input_output_aliases"] = {first: 0, first + 1: 1}
    return call(
        kernel,
        (len(arrays),),
        [
            pl.BlockSpec((None, rows, own), lambda n, order, spots: (order[n], 0, spots[planes])),
            cut(0),
            cut(1),
            cut(2),
        ]
        + [pl.BlockSpec(x.shape, lambda n, order, spots: (0, 0, 0)) for x in arrays]
        + [pl.BlockSpec(memory_space=pl.ANY)] * (0 if before is None else 2),
        [result(own), result(3 * piece)],
        [
            jax.ShapeDtypeStruct((planes, blocks, rows, own), bf16),
            jax.ShapeDtypeStruct((planes, blocks, rows, 3 * piece), bf16),
        ],
        scalars=2,
        **more,
    )(
        order,
        spots,
        w_fc1.reshape(blocks, rows, -1),
        *[w_qkv.reshape(blocks, rows, -1)] * 3,
        *arrays,
        *(before or ()),
    )


def norm(arrays, places, gain, shift, blocks, before=None):
    rows, width = arrays[0].shape[0] // 2, arrays[0].shape[1]

    def kernel(places_ref, gain_ref, shift_ref, *refs):
        out_ref, tokens_ref, cot_ref, mean_ref, inverse_ref = refs[-5:]
        for n in range(len(arrays)):

            @pl.when(pl.program_id(0) == n)
            def _(ref=refs[n]):
                tokens_ref[...] = ref[:rows]
                cot_ref[...] = ref[rows:]
                x = ref[:rows].astype(f32)
                mean = jnp.mean(x, axis=1, keepdims=True)
                centred = x - mean
                inverse = lax.rsqrt(jnp.mean(centred * centred, axis=1, keepdims=True) + epsilon)
                out_ref[...] = (centred * inverse * gain_ref[...] + shift_ref[...]).astype(bf16)
                mean_ref[...] = jnp.broadcast_to(mean, mean_ref.shape)
                inverse_ref[...] = jnp.broadcast_to(inverse, inverse_ref.shape)

    line = pl.BlockSpec((1, width), lambda i, places: (0, 0))
    wide = pl.BlockSpec((rows, width), lambda i, places: (places[i], 0))
    slim = pl.BlockSpec((rows, LANES), lambda i, places: (places[i], 0))
    more = {}
    if before is not None:
        more["input_output_aliases"] = {3 + len(arrays) + i: i for i in range(5)}
    return call(
        kernel,
        (len(arrays),),
        [line, line]
        + [pl.BlockSpec(x.shape, lambda i, places: (0, 0)) for x in arrays]
        + [pl.BlockSpec(memory_space=pl.ANY)] * (0 if before is None else 5),
        [wide, wide, wide, slim, slim],
        [jax.ShapeDtypeStruct((blocks * rows, width), bf16)] * 3
        + [jax.ShapeDtypeStruct((blocks * rows, LANES), f32)] * 2,
        scalars=1,
        **more,
    )(
        jnp.asarray(places, jnp.int32),
        gain.reshape(1, width),
        shift.reshape(1, width),
        *arrays,
        *(before or ()),
    )


def join(*lists):
    shape = lists[0][0].shape[1:]
    spans, arrays, total = [], [], 0
    for some in lists:
        start = total
        for x in some:
            arrays.append((total, x))
            total += x.shape[0]
        spans.append((start, total - start))

    def kernel(*refs):
        here = pl.program_id(0)
        for n, (start, x) in enumerate(arrays):
            for out, (first, count) in zip(refs[len(arrays) :], spans):
                if first <= start < first + count:

                    @pl.when((here >= start) & (here < start + x.shape[0]))
                    def _(ref=refs[n], out=out):
                        out[...] = ref[...]

    def spec(first, count):
        return pl.BlockSpec(
            (None,) + shape,
            lambda i: (jnp.clip(i - first, 0, count - 1),) + (0,) * len(shape),
        )

    results = call(
        kernel,
        (total,),
        [spec(start, x.shape[0]) for start, x in arrays],
        [spec(*span) for span in spans],
        [jax.ShapeDtypeStruct((count,) + shape, arrays[0][1].dtype) for _, count in spans],
        us=3,
    )(*[x for _, x in arrays])
    return results if len(lists) > 1 else results[0]


def add_in_order(mine, came, order):
    count = order.shape[0]
    rows, width = mine.shape[0] // count, mine.shape[1]

    def kernel(order_ref, mine_ref, came_ref, out_ref):
        out_ref[...] = (mine_ref[...] + came_ref[...].astype(f32)).astype(bf16)

    block = pl.BlockSpec((rows, width), lambda i, order: (i, 0))
    return call(
        kernel,
        (count,),
        [block, block],
        pl.BlockSpec((None, rows, width), lambda i, order: (order[i], 0, 0)),
        jax.ShapeDtypeStruct((count, rows, width), bf16),
        scalars=1,
        us=5,
    )(order, mine, came)


def branches(context, out_rows, active, fc2_rows):
    total, width = context.shape[0], out_rows.shape[1]
    half, block = total // 2, 256

    def kernel(context_ref, out_ref, active_ref, fc2_ref, mine_ref, other_ref):
        y = dot(context_ref[...], out_ref[...], ((1,), (0,)))
        y = y + dot(active_ref[...], fc2_ref[...], ((1,), (0,)))
        mine_ref[...] = y[:half]
        other_ref[...] = y[half:].astype(bf16)

    whole = lambda x: pl.BlockSpec(x.shape, lambda i: (0, 0))
    part = lambda rows: pl.BlockSpec((rows, block), lambda i: (0, i))
    return call(
        kernel,
        (width // block,),
        [whole(context), part(out_rows.shape[0]), whole(active), part(fc2_rows.shape[0])],
        [part(half), part(half)],
        [jax.ShapeDtypeStruct((half, width), f32), jax.ShapeDtypeStruct((half, width), bf16)],
        us=10,
    )(context, out_rows, active, fc2_rows)


def backs(hidden_grad, fc1_cols, mixed_grad, qkv_cols, tokens, mean, inverse):
    total, width = mean.shape[0], fc1_cols.shape[0]
    half, block = total // 2, 256

    def kernel(
        hidden_ref, fc1_ref, mixed_ref, qkv_ref, tokens_ref, mean_ref, inverse_ref,
        first_ref, second_ref, sums_ref,
    ):
        y = dot(hidden_ref[...], fc1_ref[...], ((1,), (1,)))
        y = y + dot(mixed_ref[...], qkv_ref[...], ((1,), (1,)))
        first_ref[...] = y[:half]
        second_ref[...] = y[half:].astype(bf16)
        normed = (tokens_ref[...].astype(f32) - mean_ref[:, :1]) * inverse_ref[:, :1]
        sums_ref[0:1, :] = jnp.sum(y * normed, axis=0, keepdims=True)
        sums_ref[1:2, :] = jnp.sum(y, axis=0, keepdims=True)
        sums_ref[2:8, :] = jnp.zeros((6, block), f32)

    whole = lambda x: pl.BlockSpec(x.shape, lambda i: (0, 0))
    part = lambda rows: pl.BlockSpec((rows, block), lambda i: (0, i))
    rhs = lambda x: pl.BlockSpec((block, x.shape[1]), lambda i: (i, 0))
    return call(
        kernel,
        (width // block,),
        [
            whole(hidden_grad),
            rhs(fc1_cols),
            whole(mixed_grad),
            rhs(qkv_cols),
            part(total),
            whole(mean),
            whole(inverse),
        ],
        [part(half), part(half), part(8)],
        [
            jax.ShapeDtypeStruct((half, width), f32),
            jax.ShapeDtypeStruct((half, width), bf16),
            jax.ShapeDtypeStruct((8, width), f32),
        ],
        us=14,
    )(hidden_grad, fc1_cols, mixed_grad, qkv_cols, tokens, mean, inverse)


def place_columns(net, mine, other, factor):
    J, planes = net.J, net.S
    _, rows, columns = mine[0].shape
    piece = columns // planes
    spots = jnp.concatenate([net.order(), jnp.stack([net.c, 1 - net.c])]).astype(jnp.int32)
    high = rows // 2

    def kernel(spots_ref, m0_ref, m1_ref, o0_ref, o1_ref, out_ref):
        here = pl.program_id(0)
        for e, (place, refs) in enumerate(
            ((net.mine, (m0_ref, m1_ref)), (net.theirs, (o0_ref, o1_ref)))
        ):
            last, _ = place(here)
            for ref, chosen in zip(refs, (jnp.logical_not(last), last)):

                @pl.when(chosen)
                def _(e=e, ref=ref):
                    for k in range(planes):
                        column = (k * CORES + spots_ref[J + e]) * piece
                        out_ref[:, pl.ds(pl.multiple_of(column, LANES), piece)] = (
                            ref[:, k * piece : (k + 1) * piece].astype(f32) * factor
                        )

    return call(
        kernel,
        (J, 2),
        [
            pl.BlockSpec(
                (None, high, columns), lambda i, h, spots, place=place, n=n: (place(i)[1][n], h, 0)
            )
            for place in (net.mine, net.theirs)
            for n in range(2)
        ],
        pl.BlockSpec((high, 2 * columns), lambda i, h, spots: (spots[i] * 2 + h, 0)),
        jax.ShapeDtypeStruct((J * rows, 2 * columns), f32),
        scalars=1,
        us=11,
    )(spots, *mine, *other)


def place_mixed(net, mine, other, factor):
    J, planes = net.J, net.S
    _, part, columns = mine[0].shape
    piece = columns // planes // 4
    width = planes * CORES * piece
    spots = jnp.concatenate([net.order(), jnp.stack([net.c, 1 - net.c])]).astype(jnp.int32)

    def kernel(spots_ref, m0_ref, m1_ref, o0_ref, o1_ref, qkv_ref, out_ref):
        here = pl.program_id(0)
        for e, (place, refs) in enumerate(
            ((net.mine, (m0_ref, m1_ref)), (net.theirs, (o0_ref, o1_ref)))
        ):
            last, _ = place(here)
            core = spots_ref[J + e]
            for ref, chosen in zip(refs, (jnp.logical_not(last), last)):
                for k in range(planes):

                    @pl.when(chosen & (pl.program_id(1) == k))
                    def _(k=k, core=core, ref=ref):
                        for i in range(3):
                            start = (4 * k + i) * piece
                            column = ((i * planes + k) * CORES + core) * piece
                            qkv_ref[:, pl.ds(pl.multiple_of(column, LANES), piece)] = (
                                ref[:, start : start + piece].astype(f32) * factor
                            )
                        block = ref[:, (4 * k + 3) * piece : (4 * k + 4) * piece].astype(f32)
                        out_ref[pl.ds(pl.multiple_of(core * piece, LANES), piece), :] = (
                            block * factor
                        ).T

    if part % LANES == 0:
        out_shape = (CORES * piece, planes * J * part)
        out_spec = pl.BlockSpec((CORES * piece, part), lambda i, k, spots: (0, k * J + spots[i]))
    else:
        out_shape = (planes, J, CORES * piece, part)
        out_spec = pl.BlockSpec(
            (None, None, CORES * piece, part), lambda i, k, spots: (k, spots[i], 0, 0)
        )
    return call(
        kernel,
        (J, planes),
        [
            pl.BlockSpec(
                (None, part, columns), lambda i, k, spots, place=place, n=n: (place(i)[1][n], 0, 0)
            )
            for place in (net.mine, net.theirs)
            for n in range(2)
        ],
        [pl.BlockSpec((part, 3 * width), lambda i, k, spots: (spots[i], 0)), out_spec],
        [
            jax.ShapeDtypeStruct((width // planes, 3 * width), f32),
            jax.ShapeDtypeStruct(out_shape, f32),
        ],
        scalars=1,
        us=16,
    )(spots, *mine, *other)


def place_rows(net, mine, other, factor):
    J = net.J
    _, rows, columns = mine[0].shape
    spots = jnp.concatenate([net.c * J + net.order(), (1 - net.c) * J + net.order(other=True)])
    arrays = (*mine, *other) if net.square else (mine[0], other[0])
    starts = [sum(x.shape[0] for x in arrays[:n]) for n in range(len(arrays))]

    def kernel(spots_ref, *refs):
        here = pl.program_id(0)
        for start, x, ref in zip(starts, arrays, refs):

            @pl.when((here >= start) & (here < start + x.shape[0]))
            def _(ref=ref):
                refs[-1][...] = ref[...].astype(f32) * factor

    def spec(start, count):
        return pl.BlockSpec(
            (None, rows, columns), lambda i, spots: (jnp.clip(i - start, 0, count - 1), 0, 0)
        )

    return call(
        kernel,
        (2 * J,),
        [spec(start, x.shape[0]) for start, x in zip(starts, arrays)],
        pl.BlockSpec((rows, columns), lambda i, spots: (spots[i], 0)),
        jax.ShapeDtypeStruct((2 * J * rows, columns), f32),
        scalars=1,
        us=12,
    )(spots.astype(jnp.int32), *arrays)


def tie(x, *after):
    return lax.optimization_barrier((x, after))[0]


class Links:
    def __init__(self, planes, replicas):
        self.S = planes
        self.J = replicas // CORES
        self.square = self.J == 4
        dp = lax.axis_index("dp")
        self.s = lax.axis_index("shard")
        self.c = dp % CORES
        self.j = dp // CORES
        self.first = jnp.where(self.c == 0, 2, 1)

    def move(self, x, ds=0, dc=0, steps=None):
        pairs = []
        for j in range(self.J):
            for c in range(CORES):
                for s in range(self.S):
                    turn = 0 if steps is None else (2, 1)[(c + steps) % 2]
                    to = ((j ^ turn) * CORES + (c + dc) % CORES) * self.S + (s + ds) % self.S
                    pairs.append(((j * CORES + c) * self.S + s, to))
        return lax.ppermute(x, AXES, pairs)

    def groups(self):
        return [[j * CORES + c for j in range(self.J)] for c in range(CORES)]

    def order(self, other=False):
        if not self.square:
            return jnp.arange(self.J)
        turn = 3 - self.first if other else self.first
        return jnp.stack([self.j, self.j ^ turn, self.j ^ 3 ^ turn, self.j ^ 3])

    def mine(self, i):
        return (i >= 2, (jnp.minimum(i, 1), jnp.maximum(i - 2, 0))) if self.square else (i < 0, (i, 0))

    def theirs(self, i):
        return (i % 2 == 1, (i // 2, i // 2)) if self.square else (i < 0, (i, 0))

    def gather(self, x):
        return self.move(x, steps=0) if self.square else None

    def gather_more(self, stack):
        return self.move(stack, steps=1) if self.square else None

    def spread(self, x):
        if not self.square:
            return x
        other = self.j ^ self.first
        return jnp.stack([pick(x, other, 1), pick(x, other ^ 3 ^ self.first, 1)])

    def spread_sum(self, x, got):
        if not self.square:
            return x, x
        mine = pick(x, self.j, 1), pick(x, self.j ^ 3 ^ self.first, 1)
        return [(m.astype(f32) + g.astype(f32)).astype(bf16) for m, g in zip(mine, got)]

    def spread_last(self, own, got):
        if not self.square:
            return lax.psum_scatter(
                own.astype(f32),
                "dp",
                scatter_dimension=1,
                axis_index_groups=self.groups(),
                tiled=False,
            ).astype(bf16)
        return (own.astype(f32) + got.astype(f32)).astype(bf16)

    def plane_sum(self, x, step):
        if not self.square:
            return lax.psum(x, "dp", axis_index_groups=self.groups()) if step else x
        return x + self.move(x, steps=step)


def swap(x, after=()):
    return lax.all_to_all(tie(x, *after), "shard", 0, 0, tiled=True)


def twofold(x, axis):
    high = lax.reduce_precision(x, 8, 7)
    return jnp.concatenate([high.astype(bf16), (x - high).astype(bf16)], axis=axis)


def as_rows(vector, width, multiple):
    count = -(-vector.shape[0] // (width * multiple)) * multiple
    return jnp.pad(vector, (0, count * width - vector.shape[0])).reshape(count, width)


def pick(x, index, axis):
    return lax.dynamic_index_in_dim(x, index, axis, keepdims=False)


def in_order(held, here):
    size = len(held)
    backwards = jnp.stack(held[::-1])
    return lax.dynamic_slice_in_dim(
        jnp.concatenate([backwards, backwards]), size - 1 - here, size, 0
    )


def local(
    tokens,
    segments,
    ln_gain,
    ln_bias,
    w_qkv,
    b_qkv,
    w_out,
    b_out,
    w_fc1,
    b_fc1,
    w_fc2,
    b_fc2,
    cotangent,
):
    planes = lax.axis_size("shard")
    replicas = lax.axis_size("dp")
    net = Links(planes, replicas)
    S, J, c, j, s = net.S, net.J, net.c, net.j, net.s
    seqs, length, width = tokens.shape
    rows = seqs * length
    ff = w_fc1.shape[1]
    ff_own = ff // (S * CORES)
    mix_own = width // (S * CORES)
    height = width // S
    part = height // J
    total = S * CORES * rows
    back_planes = (s - jnp.arange(S)) % S
    factor = 1.0 / math.sqrt(rows * planes * replicas)

    own_tokens = tokens.reshape(rows, width)
    own_cot = cotangent.reshape(rows, width)
    hops = [jnp.concatenate([own_tokens, own_cot])]
    hops.append(net.move(hops[0], ds=1))

    vectors = [ln_gain, ln_bias, b_qkv, b_out, b_fc1, b_fc2, segments.reshape(-1).astype(bf16)]
    small = jnp.concatenate(vectors)
    size = small.shape[0]
    held = [small] + [net.move(small, ds=k) for k in range(1, S)]

    got = swap(pack(w_fc1, w_qkv, j, c, S, part, ff_own, mix_own))
    others = [net.move(tie(hops[0], hops[1], held), dc=1), net.move(hops[1], dc=1)]
    fc2_rows = lax.dynamic_slice_in_dim(w_fc2, c * ff_own, ff_own, 0)
    out_rows = lax.dynamic_slice_in_dim(w_out, c * mix_own, mix_own, 0)
    marks = jnp.stack([v[size - rows :] for v in held])
    small_all = in_order(held, s)
    whole = []
    start = 0
    for vector in vectors[:-1]:
        whole.append(small_all[:, start : start + vector.shape[0]].reshape(-1).astype(f32))
        start += vector.shape[0]
    gain_full, shift_full, qkv_bias, out_bias, fc1_bias, fc2_bias = whole
    fc1_bias = lax.dynamic_slice_in_dim(fc1_bias, (s * CORES + c) * ff_own, ff_own, 0)
    qkv_bias = lax.dynamic_slice_in_dim(
        qkv_bias.reshape(3, width), (s * CORES + c) * mix_own, mix_own, 1
    ).reshape(-1)
    marks = jnp.stack([marks, net.move(tie(marks, hops[1], held), dc=1)])
    tables = rotary_tables(marks.reshape(-1, length).astype(jnp.int32))
    ready = tie((hops[1], others, fc2_rows, out_rows, tables, gain_full, fc1_bias, qkv_bias), hops[1])
    hop, others, fc2_rows, out_rows, tables, gain_full, fc1_bias, qkv_bias = ready

    got = tie(got, hop, others, fc2_rows, out_rows, tables, gain_full, fc1_bias, qkv_bias)
    block = jnp.concatenate([pick(got, back_planes[k], 0) for k in range(1, S)])[None]
    hops.append(net.move(tie(hop, got), ds=1))
    came = net.gather(block)
    if net.square:
        blocks = tie(join([block, came]))
    else:
        blocks = lax.all_gather(block[0], "dp", axis_index_groups=net.groups())
    came = net.gather_more(blocks)
    while len(hops) < S:
        hops.append(net.move(tie(hops[-1], blocks), ds=1))
        others.append(net.move(tie(hops[-2], blocks), dc=1))
    places = [e * S + k for k in range(S) for e in range(CORES)]
    early = [x for pair in zip(hops[: S - 1], others[: S - 1]) for x in pair]
    early = tie(early, blocks)
    normed_rows = norm(early, places[:-CORES], gain_full, shift_full, S * CORES)
    last = tie(hops[-1], normed_rows)
    others.append(net.move(last, dc=1))
    blocks = tie(blocks, normed_rows)
    spots_w = jnp.concatenate([back_planes, (s * CORES + c)[None]]).astype(jnp.int32)
    chips = net.order()
    weights = lambda x, order, *before: assemble(
        w_fc1,
        w_qkv,
        [y.reshape(S - 1, part, -1) for y in x],
        order.astype(jnp.int32),
        spots_w,
        ff_own,
        mix_own,
        J,
        *before,
    )
    weight_cols = weights(blocks, chips[: blocks.shape[0]])
    last, other = tie((last, others[-1]), weight_cols)
    hidden_in, tok_rows, cot_rows, mean, inverse = norm(
        [last, other], places[-CORES:], gain_full, shift_full, S * CORES, normed_rows
    )
    if net.square:
        weight_cols, came = tie((weight_cols, came), hidden_in)
        weight_cols = weights(came, chips[2:], weight_cols)
    fc1_cols = weight_cols[0].reshape(width, ff_own)
    qkv_cols = weight_cols[1].reshape(width, 3 * mix_own)

    hidden = jnp.dot(hidden_in, fc1_cols, preferred_element_type=f32) + fc1_bias
    active, gelu_back = jax.vjp(lambda v: jax.nn.gelu(v, approximate=True), hidden)
    active = active.astype(bf16)
    transposed = lambda x, y: jnp.einsum("td,te->de", x, y, preferred_element_type=f32).astype(bf16)
    fc2_term = transposed(active, cot_rows)

    mark = []

    def step(x, *made):
        nonlocal mark
        if not made:
            return tie(x, mark)
        mark = list(made)
        return x

    def first_sum(x):
        sent = tie(net.spread(x))
        step(None, sent)
        return x, net.gather(sent)

    def second_sum(x, got):
        x, got = step((x, got))
        own, sent = tie(net.spread_sum(x, got))
        step(None, own, sent)
        return own, net.gather_more(sent)

    def last_sum(own, got):
        part = tie(net.spread_last(*step((own, got))))
        step(None, part)
        return part

    def second_gather(part, came):
        part, came = step((part, came))
        if net.square:
            stack = join([part[None], came[None]])
        else:
            stack = lax.all_gather(part, "dp", axis_index_groups=net.groups())
        stack = tie(stack)
        step(None, stack)
        return stack, net.gather_more(stack)

    def to_other(x):
        return net.move(step(x), dc=1) if net.square else x

    fc2_own, fc2_got = first_sum(fc2_term.reshape(1, J, ff_own // J, width))
    late_cot = step(cot_rows)
    active_grad = jnp.einsum("td,fd->tf", late_cot, fc2_rows, preferred_element_type=f32)
    hidden_grad = gelu_back(active_grad)[0].astype(bf16)
    fc1_term = transposed(hidden_in, hidden_grad)
    fc1_own, fc1_got = first_sum(fc1_term.reshape(S, J, part, ff_own))
    fc2_own, fc2_got = second_sum(fc2_own, fc2_got)
    late_in, late_cot = step((hidden_in, cot_rows))
    mixed = jnp.dot(late_in, qkv_cols, preferred_element_type=f32) + qkv_bias
    context_grad = jnp.einsum("te,de->td", late_cot, out_rows, preferred_element_type=f32).astype(
        bf16
    )
    context, mixed_grad = attention(tables, mixed, context_grad, length)
    step(None, context, mixed_grad)
    fc1_own, fc1_got = second_sum(fc1_own, fc1_got)
    fc2_part = last_sum(fc2_own, fc2_got)[0]
    fc2_came = net.gather(fc2_part)
    late_in, late_cot, late_mixed, late_context = step((hidden_in, cot_rows, mixed_grad, context))
    mixed_term = with_layout_constraint(
        jnp.concatenate(
            [transposed(late_in, late_mixed), transposed(late_cot, late_context)], axis=1
        ),
        Layout((0, 1)),
    )
    mixed_own, mixed_got = first_sum(mixed_term.reshape(S, J, part, 4 * mix_own))
    fc1_part = last_sum(fc1_own, fc1_got)
    fc1_part = swap(fc1_part)
    fc2_part, fc2_came = second_gather(fc2_part, fc2_came)
    fc2_other = net.move(fc2_part, dc=1)
    late_context, late_active = step((context, active))
    branch, branch_other = branches(late_context, out_rows, late_active, fc2_rows)
    step(None, branch, branch_other)
    branch_came = net.move(branch_other, dc=1)
    late_mixed, late_grad = step((mixed_grad, hidden_grad))
    back, back_other, norm_sums = backs(
        late_grad, fc1_cols, late_mixed, qkv_cols, tok_rows, mean, inverse
    )
    step(None, back, back_other, norm_sums)
    back_came = net.move(back_other, dc=1)
    scatter = lambda x: lax.psum_scatter(x, "shard", scatter_dimension=0, tiled=True)[0]
    late_grad, late_mixed, late_cot, norm_sums = step((hidden_grad, mixed_grad, cot_rows, norm_sums))
    mixed_sums = jnp.sum(late_mixed, axis=0, dtype=f32)
    norm_sums = jnp.swapaxes(norm_sums[:2].reshape(2, S, height), 0, 1).reshape(S, -1)
    riders = jnp.concatenate([norm_sums, jnp.broadcast_to(mixed_sums, (S, 3 * mix_own))], axis=1)
    riding = riders.shape[1]
    riders = jnp.pad(riders, ((0, 0), (0, -riding % (24 * mix_own))))
    riders = twofold(riders.reshape(S, -1, 3 * mix_own), 1)
    column_sums = jnp.concatenate(
        [
            jnp.sum(late_grad, axis=0, dtype=f32),
            pick(jnp.sum(late_cot, axis=0, dtype=f32).reshape(S, height), s, 0),
        ]
    )
    riders, column_sums = tie((riders, column_sums))
    step(None, riders, column_sums)
    mixed_own, mixed_got = second_sum(mixed_own, mixed_got)
    fc1_part, fc2_came = step((fc1_part, fc2_came))
    fc1_part = tie(jnp.swapaxes(fc1_part, 0, 1).reshape(part, S * ff_own))
    step(None, fc1_part)
    fc1_came = net.gather(fc1_part)
    branch_acts = add_in_order(*step((branch, branch_came)), back_planes.astype(jnp.int32))
    back_acts = add_in_order(*step((back, back_came)), back_planes.astype(jnp.int32))
    mark += [branch_acts, back_acts]
    fc1_part, fc1_came = second_gather(fc1_part, fc1_came)
    branch_sum, back_sum = scatter(branch_acts), scatter(back_acts)
    mixed_part = last_sum(mixed_own, mixed_got)
    out_part = mixed_part[:, :, 3 * mix_own :]
    mixed_part = tie(jnp.concatenate([mixed_part[:, :, : 3 * mix_own], riders], axis=1))
    step(None, mixed_part)
    mixed_part = swap(mixed_part)
    fc1_other = net.move(step(fc1_part), dc=1)
    if net.square:
        fc2_last = net.move(step(fc2_came), dc=1)
        fc1_came = step(fc1_came)
        mark += [fc1_came]
    mixed_part = step(mixed_part)
    riders = mixed_part[:, part:].astype(f32)
    mixed_part = jnp.concatenate([mixed_part[:, :part], out_part], axis=2)
    mixed_part = tie(jnp.swapaxes(mixed_part, 0, 1).reshape(part, S * 4 * mix_own))
    step(None, mixed_part)
    mixed_came = net.gather(mixed_part)
    if net.square:
        fc1_last = net.move(step(fc1_came), dc=1)
        fc2_mine, fc2_other = (fc2_part, fc2_came), (fc2_other, fc2_last)
    else:
        fc2_mine, fc2_other = (fc2_part, fc2_part), (fc2_other, fc2_other)
    count = riders.shape[1] // 2
    riders = step(riders)
    riders = (riders[:, :count] + riders[:, count:]).reshape(S, -1)[:, :riding]
    sums = jnp.concatenate(
        [
            jnp.sum(riders[:, : 2 * height], axis=0),
            column_sums[:ff_own],
            riders[:, 2 * height :].reshape(-1),
            column_sums[ff_own:],
        ]
    )
    sums = tie(sums)
    step(None, sums)
    sums = net.plane_sum(sums, 0)
    fc2_own = place_rows(net, *step((fc2_mine, fc2_other)), factor)
    step(None, fc2_own)
    mixed_part, mixed_came = second_gather(mixed_part, mixed_came)
    mixed_other = net.move(mixed_part, dc=1)
    if net.square:
        fc1_mine, fc1_other = (fc1_part, fc1_came), (fc1_other, fc1_last)
    else:
        fc1_mine, fc1_other = (fc1_part, fc1_part), (fc1_other, fc1_other)
    fc1_own = place_columns(net, *step((fc1_mine, fc1_other)), factor)
    step(None, fc1_own)
    if net.square:
        mixed_came = tie(step(mixed_came))
        mixed_last = net.move(mixed_came, dc=1)
        mixed_mine, mixed_other = (mixed_part, mixed_came), (mixed_other, mixed_last)
    else:
        mixed_mine, mixed_other = (mixed_part, mixed_part), (mixed_other, mixed_other)
    sums = net.plane_sum(tie(sums, mixed_mine), 1)
    sums_came = net.move(sums, dc=1)
    qkv_own, out_own = place_mixed(net, mixed_mine, mixed_other, factor)
    if out_own.ndim == 4:
        out_own = jnp.transpose(out_own, (2, 0, 1, 3)).reshape(height, width)

    own_inputs = own_tokens.astype(f32)
    output = (own_inputs + branch_sum.astype(f32) + (out_bias + fc2_bias)).astype(bf16)
    normed = (own_inputs - mean[:rows, :1]) * inverse[:rows, :1]
    scaled = back_sum.astype(f32) * gain_full
    input_grad = own_cot.astype(f32) + inverse[:rows, :1] * (
        scaled
        - jnp.mean(scaled, axis=1, keepdims=True)
        - normed * jnp.mean(scaled * normed, axis=1, keepdims=True)
    )

    gain_own = (sums[:height] + sums_came[:height]) * factor
    shift_own = (sums[height : 2 * height] + sums_came[height : 2 * height]) * factor
    bias_own = sums[-height:] * factor
    pairs = jnp.where(c == 0, jnp.stack([sums, sums_came]), jnp.stack([sums_came, sums]))
    pairs = pairs[:, 2 * height : -height]
    fc1_bias_own = pairs[:, :ff_own].reshape(-1) * factor
    mixed_sums = jnp.transpose(pairs[:, ff_own:].reshape(CORES, S, 3, mix_own), (2, 1, 0, 3))
    qkv_bias_own = pick(mixed_sums.reshape(S, -1), s, 0) * factor
    return (
        output.reshape(tokens.shape),
        input_grad.reshape(tokens.shape),
        gain_own,
        shift_own,
        qkv_own,
        qkv_bias_own,
        out_own,
        bias_own,
        fc1_own,
        fc1_bias_own,
        fc2_own,
        bias_own,
    )


def solution(mesh):
    return jax.shard_map(
        local,
        mesh=mesh,
        in_specs=(
            P(("dp", "shard"), None, None),
            P(("dp", "shard"), None),
            P("shard"),
            P("shard"),
            P("shard", None),
            P("shard"),
            P("shard", None),
            P("shard"),
            P("shard", None),
            P("shard"),
            P("shard", None),
            P("shard"),
            P(("dp", "shard"), None, None),
        ),
        out_specs=(
            P(("dp", "shard"), None, None),
            P(("dp", "shard"), None, None),
            P("shard"),
            P("shard"),
            P("shard", None),
            P("shard"),
            P("shard", None),
            P("shard"),
            P("shard", None),
            P("shard"),
            P("shard", None),
            P("shard"),
        ),
        check_vma=False,
    )
```

```python
import math

import jax
import jax.numpy as jnp
from jax import lax
from jax.experimental import pallas as pl
from jax.experimental.pallas import tpu as pltpu
from jax.experimental.layout import Layout, with_layout_constraint
from jax.sharding import PartitionSpec as P

HEADS = 32
HEAD_DIM = 64
ROT = 32
CORES = 2
LANES = 128

epsilon = 1e-05
masked_value = -1e30
AXES = ("dp", "shard")
f32 = jnp.float32
bf16 = jnp.bfloat16
VMEM = 48 * 1024 * 1024


def rotary_tables(segments):
    seqs, length = segments.shape
    positions = jnp.broadcast_to(jnp.arange(length, dtype=jnp.int32), segments.shape)
    change = jnp.concatenate(
        [jnp.ones((seqs, 1), dtype=bool), segments[:, 1:] != segments[:, :-1]], axis=1
    )
    run_start = lax.cummax(jnp.where(change, positions, 0), axis=1)
    distance = (positions - run_start).astype(f32).reshape(-1, 1)
    lane = jnp.arange(LANES, dtype=jnp.int32) % HEAD_DIM
    half = ROT // 2
    frequency = jnp.exp((lane % half).astype(f32) * (-2.0 * math.log(10000.0) / ROT))
    angles = distance * frequency[None, :]
    sines = jnp.sin(angles)
    cos_table = jnp.where(lane < ROT, jnp.cos(angles), 1.0)
    low_table = jnp.where(lane < half, -sines, 0.0)
    high_table = jnp.where((lane >= half) & (lane < ROT), sines, 0.0)
    starts = jnp.broadcast_to(run_start.reshape(-1, 1), (seqs * length, LANES))
    return starts, cos_table, low_table, high_table


def attention_kernel(
    starts_ref, cos_ref, low_ref, high_ref, mixed_ref, outer_ref, context_ref, grad_ref
):
    length, width = outer_ref.shape
    half = ROT // 2
    scale = HEAD_DIM ** (-0.5)

    def wide(table):
        return jnp.concatenate([table[...]] * (width // LANES), axis=1)

    cos_table, low_table, high_table = wide(cos_ref), wide(low_ref), wide(high_ref)

    def rotate(v, sign):
        turned = pltpu.roll(v, width - half, 1) * low_table + pltpu.roll(v, half, 1) * high_table
        return v * cos_table + sign * turned

    queries = rotate(mixed_ref[:, :width], 1.0).astype(bf16)
    key_rows = rotate(mixed_ref[:, width : 2 * width], 1.0).astype(bf16)
    values = mixed_ref[:, 2 * width :].astype(bf16)
    outer = outer_ref[...]
    row = lax.broadcasted_iota(jnp.int32, (length, length), 0)
    column = lax.broadcasted_iota(jnp.int32, (length, length), 1)
    allowed = (column <= row) & (column >= starts_ref[...])
    spans = [slice(h * HEAD_DIM, (h + 1) * HEAD_DIM) for h in range(width // HEAD_DIM)]
    block = lambda x, h: x[h * length : (h + 1) * length]
    heads = range(len(spans))
    allowed = jnp.concatenate([allowed] * len(spans), axis=0)
    scores = jnp.concatenate([dot(queries[:, p], key_rows[:, p], ((1,), (1,))) for p in spans], axis=0)
    scores = jnp.where(allowed, scores * scale, masked_value)
    weights = jnp.exp(scores - jnp.max(scores, axis=1, keepdims=True))
    probs = weights / jnp.sum(weights, axis=1, keepdims=True)
    low = probs.astype(bf16)
    prob_grad = jnp.concatenate([dot(outer[:, p], values[:, p], ((1,), (1,))) for p in spans], axis=0)
    inner = jnp.sum(prob_grad * probs, axis=1, keepdims=True)
    score_grad = (probs * (prob_grad - inner)).astype(bf16)
    context = [dot(block(low, h), values[:, spans[h]], ((1,), (0,))) for h in heads]
    value_grad = [dot(block(low, h), outer[:, spans[h]], ((0,), (0,))) for h in heads]
    query_grad = [dot(block(score_grad, h), key_rows[:, spans[h]], ((1,), (0,))) for h in heads]
    key_grad = [dot(block(score_grad, h), queries[:, spans[h]], ((0,), (0,))) for h in heads]
    side = lambda x: jnp.concatenate(x, axis=1)
    context_ref[...] = side(context).astype(bf16)
    grad_ref[:, :width] = rotate(side(query_grad) * scale, -1.0).astype(bf16)
    grad_ref[:, width : 2 * width] = rotate(side(key_grad) * scale, -1.0).astype(bf16)
    grad_ref[:, 2 * width :] = side(value_grad).astype(bf16)


def attention(tables, mixed, outer, length):
    rows, width = outer.shape
    wide = lambda columns: pl.BlockSpec((length, columns), lambda i: (i, 0))
    return pl.pallas_call(
        attention_kernel,
        grid=(rows // length,),
        in_specs=[wide(LANES)] * 4 + [wide(3 * width), wide(width)],
        out_specs=[wide(width), wide(3 * width)],
        out_shape=[
            jax.ShapeDtypeStruct((rows, width), bf16),
            jax.ShapeDtypeStruct((rows, 3 * width), bf16),
        ],
        cost_estimate=pl.CostEstimate(flops=4 * 10**9, bytes_accessed=0, transcendentals=0),
        compiler_params=pltpu.CompilerParams(vmem_limit_bytes=VMEM),
    )(*tables, mixed, outer)


def call(kernel, grid, in_specs, out_specs, out_shape, scalars=0, us=0, **more):
    return pl.pallas_call(
        kernel,
        grid_spec=pltpu.PrefetchScalarGridSpec(
            num_scalar_prefetch=scalars, grid=grid, in_specs=in_specs, out_specs=out_specs
        ),
        out_shape=out_shape,
        cost_estimate=pl.CostEstimate(flops=us * 10**9 // 3, bytes_accessed=0, transcendentals=0),
        compiler_params=pltpu.CompilerParams(vmem_limit_bytes=VMEM),
        **more,
    )


def dot(a, b, dims):
    return lax.dot_general(a, b, (dims, ((), ())), preferred_element_type=f32)


def pack(w_fc1, w_qkv, row, core, planes, part, own, piece):
    third = w_qkv.shape[1] // 3 // piece
    cols = own + 3 * piece
    spots = jnp.stack([row, core]).astype(jnp.int32)

    def kernel(spots_ref, fc1_ref, q_ref, k_ref, v_ref, out_ref):
        out_ref[:, :own] = fc1_ref[...]
        for i, ref in enumerate((q_ref, k_ref, v_ref)):
            out_ref[:, own + i * piece : own + (i + 1) * piece] = ref[...]

    cut = lambda i: pl.BlockSpec(
        (part, piece), lambda p, spots: (spots[0], i * third + p * CORES + spots[1])
    )
    return call(
        kernel,
        (planes,),
        [
            pl.BlockSpec((part, own), lambda p, spots: (spots[0], p * CORES + spots[1])),
            cut(0),
            cut(1),
            cut(2),
        ],
        pl.BlockSpec((None, part, cols), lambda p, spots: (p, 0, 0)),
        jax.ShapeDtypeStruct((planes, part, cols), bf16),
        scalars=1,
    )(spots, w_fc1, w_qkv, w_qkv, w_qkv)


def assemble(w_fc1, w_qkv, arrays, order, spots, own, piece, blocks, before=None):
    _, others, rows, cols = arrays[0].shape
    planes = others + 1
    height = w_fc1.shape[0]
    third = w_qkv.shape[1] // 3 // piece

    def kernel(order_ref, spots_ref, fc1_ref, q_ref, k_ref, v_ref, *refs):
        fc1_out, qkv_out = refs[-2:]
        here = spots_ref[0]
        fc1_out[here] = fc1_ref[...]
        for i, ref in enumerate((q_ref, k_ref, v_ref)):
            qkv_out[here, :, i * piece : (i + 1) * piece] = ref[...]
        places = [(ref, m) for ref in refs[: len(arrays)] for m in range(ref.shape[0])]
        for n, (ref, m) in enumerate(places):

            @pl.when(pl.program_id(0) == n)
            def _(ref=ref, m=m):
                for k in range(1, planes):
                    there = spots_ref[k]
                    fc1_out[there] = ref[m, k - 1, :, :own]
                    qkv_out[there] = ref[m, k - 1, :, own:]

    cut = lambda i: pl.BlockSpec(
        (None, rows, piece), lambda n, order, spots: (order[n], 0, i * third + spots[planes])
    )
    result = lambda size: pl.BlockSpec(
        (planes, None, rows, size), lambda n, order, spots: (0, order[n], 0, 0)
    )
    more = {}
    if before is not None:
        first = 6 + len(arrays)
        more["input_output_aliases"] = {first: 0, first + 1: 1}
    return call(
        kernel,
        (sum(x.shape[0] for x in arrays),),
        [
            pl.BlockSpec((None, rows, own), lambda n, order, spots: (order[n], 0, spots[planes])),
            cut(0),
            cut(1),
            cut(2),
        ]
        + [pl.BlockSpec(x.shape, lambda n, order, spots: (0, 0, 0, 0)) for x in arrays]
        + [pl.BlockSpec(memory_space=pl.ANY)] * (0 if before is None else 2),
        [result(own), result(3 * piece)],
        [
            jax.ShapeDtypeStruct((planes, blocks, rows, own), bf16),
            jax.ShapeDtypeStruct((planes, blocks, rows, 3 * piece), bf16),
        ],
        scalars=2,
        **more,
    )(
        order,
        spots,
        w_fc1.reshape(blocks, rows, -1),
        *[w_qkv.reshape(blocks, rows, -1)] * 3,
        *arrays,
        *(before or ()),
    )


def norm(arrays, places, gain, shift, blocks, before=None):
    rows, width = arrays[0].shape[0] // 2, arrays[0].shape[1]

    def kernel(places_ref, gain_ref, shift_ref, *refs):
        out_ref, tokens_ref, cot_ref, mean_ref, inverse_ref = refs[-5:]
        for n in range(len(arrays)):

            @pl.when(pl.program_id(0) == n)
            def _(ref=refs[n]):
                tokens_ref[...] = ref[:rows]
                cot_ref[...] = ref[rows:]
                x = ref[:rows].astype(f32)
                mean = jnp.mean(x, axis=1, keepdims=True)
                centred = x - mean
                inverse = lax.rsqrt(jnp.mean(centred * centred, axis=1, keepdims=True) + epsilon)
                out_ref[...] = (centred * inverse * gain_ref[...] + shift_ref[...]).astype(bf16)
                mean_ref[...] = jnp.broadcast_to(mean, mean_ref.shape)
                inverse_ref[...] = jnp.broadcast_to(inverse, inverse_ref.shape)

    line = pl.BlockSpec((1, width), lambda i, places: (0, 0))
    wide = pl.BlockSpec((rows, width), lambda i, places: (places[i], 0))
    slim = pl.BlockSpec((rows, LANES), lambda i, places: (places[i], 0))
    more = {}
    if before is not None:
        more["input_output_aliases"] = {3 + len(arrays) + i: i for i in range(5)}
    return call(
        kernel,
        (len(arrays),),
        [line, line]
        + [pl.BlockSpec(x.shape, lambda i, places: (0, 0)) for x in arrays]
        + [pl.BlockSpec(memory_space=pl.ANY)] * (0 if before is None else 5),
        [wide, wide, wide, slim, slim],
        [jax.ShapeDtypeStruct((blocks * rows, width), bf16)] * 3
        + [jax.ShapeDtypeStruct((blocks * rows, LANES), f32)] * 2,
        scalars=1,
        **more,
    )(
        jnp.asarray(places, jnp.int32),
        gain.reshape(1, width),
        shift.reshape(1, width),
        *arrays,
        *(before or ()),
    )


def join(*lists):
    shape = lists[0][0].shape[1:]
    spans, arrays, total = [], [], 0
    for some in lists:
        start = total
        for x in some:
            arrays.append((total, x))
            total += x.shape[0]
        spans.append((start, total - start))

    def kernel(*refs):
        here = pl.program_id(0)
        for n, (start, x) in enumerate(arrays):
            for out, (first, count) in zip(refs[len(arrays) :], spans):
                if first <= start < first + count:

                    @pl.when((here >= start) & (here < start + x.shape[0]))
                    def _(ref=refs[n], out=out):
                        out[...] = ref[...]

    def spec(first, count):
        return pl.BlockSpec(
            (None,) + shape,
            lambda i: (jnp.clip(i - first, 0, count - 1),) + (0,) * len(shape),
        )

    results = call(
        kernel,
        (total,),
        [spec(start, x.shape[0]) for start, x in arrays],
        [spec(*span) for span in spans],
        [jax.ShapeDtypeStruct((count,) + shape, arrays[0][1].dtype) for _, count in spans],
        us=3,
    )(*[x for _, x in arrays])
    return results if len(lists) > 1 else results[0]


def add_in_order(mine, came, order):
    count = order.shape[0]
    rows, width = mine.shape[0] // count, mine.shape[1]

    def kernel(order_ref, mine_ref, came_ref, out_ref):
        out_ref[...] = (mine_ref[...] + came_ref[...].astype(f32)).astype(bf16)

    block = pl.BlockSpec((rows, width), lambda i, order: (i, 0))
    return call(
        kernel,
        (count,),
        [block, block],
        pl.BlockSpec((None, rows, width), lambda i, order: (order[i], 0, 0)),
        jax.ShapeDtypeStruct((count, rows, width), bf16),
        scalars=1,
    )(order, mine, came)


def branches(context, out_rows, active, fc2_rows):
    total, width = context.shape[0], out_rows.shape[1]
    half, block = total // 2, 256

    def kernel(context_ref, out_ref, active_ref, fc2_ref, mine_ref, other_ref):
        y = dot(context_ref[...], out_ref[...], ((1,), (0,)))
        y = y + dot(active_ref[...], fc2_ref[...], ((1,), (0,)))
        mine_ref[...] = y[:half]
        other_ref[...] = y[half:].astype(bf16)

    whole = lambda x: pl.BlockSpec(x.shape, lambda i: (0, 0))
    part = lambda rows: pl.BlockSpec((rows, block), lambda i: (0, i))
    return call(
        kernel,
        (width // block,),
        [whole(context), part(out_rows.shape[0]), whole(active), part(fc2_rows.shape[0])],
        [part(half), part(half)],
        [jax.ShapeDtypeStruct((half, width), f32), jax.ShapeDtypeStruct((half, width), bf16)],
        us=10,
    )(context, out_rows, active, fc2_rows)


def backs(hidden_grad, fc1_cols, mixed_grad, qkv_cols, tokens, mean, inverse):
    total, width = mean.shape[0], fc1_cols.shape[0]
    half, block = total // 2, 256

    def kernel(
        hidden_ref, fc1_ref, mixed_ref, qkv_ref, tokens_ref, mean_ref, inverse_ref,
        first_ref, second_ref, sums_ref,
    ):
        y = dot(hidden_ref[...], fc1_ref[...], ((1,), (1,)))
        y = y + dot(mixed_ref[...], qkv_ref[...], ((1,), (1,)))
        first_ref[...] = y[:half]
        second_ref[...] = y[half:].astype(bf16)
        normed = (tokens_ref[...].astype(f32) - mean_ref[:, :1]) * inverse_ref[:, :1]
        sums_ref[0:1, :] = jnp.sum(y * normed, axis=0, keepdims=True)
        sums_ref[1:2, :] = jnp.sum(y, axis=0, keepdims=True)
        sums_ref[2:8, :] = jnp.zeros((6, block), f32)

    whole = lambda x: pl.BlockSpec(x.shape, lambda i: (0, 0))
    part = lambda rows: pl.BlockSpec((rows, block), lambda i: (0, i))
    rhs = lambda x: pl.BlockSpec((block, x.shape[1]), lambda i: (i, 0))
    return call(
        kernel,
        (width // block,),
        [
            whole(hidden_grad),
            rhs(fc1_cols),
            whole(mixed_grad),
            rhs(qkv_cols),
            part(total),
            whole(mean),
            whole(inverse),
        ],
        [part(half), part(half), part(8)],
        [
            jax.ShapeDtypeStruct((half, width), f32),
            jax.ShapeDtypeStruct((half, width), bf16),
            jax.ShapeDtypeStruct((8, width), f32),
        ],
        us=14,
    )(hidden_grad, fc1_cols, mixed_grad, qkv_cols, tokens, mean, inverse)


def place_columns(net, mine, other, factor):
    J, planes = net.J, net.S
    _, rows, columns = mine[0].shape
    piece = columns // planes
    spots = jnp.concatenate([net.order(), jnp.stack([net.c, 1 - net.c])]).astype(jnp.int32)
    high = rows // 2

    def kernel(spots_ref, m0_ref, m1_ref, o0_ref, o1_ref, out_ref):
        here = pl.program_id(0)
        for e, (place, refs) in enumerate(
            ((net.mine, (m0_ref, m1_ref)), (net.theirs, (o0_ref, o1_ref)))
        ):
            last, _ = place(here)
            for ref, chosen in zip(refs, (jnp.logical_not(last), last)):

                @pl.when(chosen)
                def _(e=e, ref=ref):
                    for k in range(planes):
                        column = (k * CORES + spots_ref[J + e]) * piece
                        out_ref[:, pl.ds(pl.multiple_of(column, LANES), piece)] = (
                            ref[:, k * piece : (k + 1) * piece].astype(f32) * factor
                        )

    return call(
        kernel,
        (J, 2),
        [
            pl.BlockSpec(
                (None, high, columns), lambda i, h, spots, place=place, n=n: (place(i)[1][n], h, 0)
            )
            for place in (net.mine, net.theirs)
            for n in range(2)
        ],
        pl.BlockSpec((high, 2 * columns), lambda i, h, spots: (spots[i] * 2 + h, 0)),
        jax.ShapeDtypeStruct((J * rows, 2 * columns), f32),
        scalars=1,
    )(spots, *mine, *other)


def place_mixed(net, mine, other, start, factor, before=None):
    J, planes = net.J, net.S
    count, part, columns = mine.shape
    piece = columns // planes // 4
    width = planes * CORES * piece
    chips = net.order()[start : start + count]
    spots = jnp.concatenate([chips, jnp.stack([net.c, 1 - net.c])]).astype(jnp.int32)

    def kernel(spots_ref, mine_ref, other_ref, *refs):
        qkv_ref, out_ref = refs[-2:]
        for e, ref in enumerate((mine_ref, other_ref)):
            core = spots_ref[count + e]
            for k in range(planes):

                @pl.when(pl.program_id(1) == k)
                def _(k=k, core=core, ref=ref):
                    for i in range(3):
                        start = (4 * k + i) * piece
                        column = ((i * planes + k) * CORES + core) * piece
                        qkv_ref[:, pl.ds(pl.multiple_of(column, LANES), piece)] = (
                            ref[:, start : start + piece].astype(f32) * factor
                        )
                    block = ref[:, (4 * k + 3) * piece : (4 * k + 4) * piece].astype(f32)
                    out_ref[pl.ds(pl.multiple_of(core * piece, LANES), piece), :] = (
                        block * factor
                    ).T

    if part % LANES == 0:
        out_shape = (CORES * piece, planes * J * part)
        out_spec = pl.BlockSpec((CORES * piece, part), lambda i, k, spots: (0, k * J + spots[i]))
    else:
        out_shape = (planes, J, CORES * piece, part)
        out_spec = pl.BlockSpec(
            (None, None, CORES * piece, part), lambda i, k, spots: (k, spots[i], 0, 0)
        )
    before = before or ()
    return call(
        kernel,
        (count, planes),
        [
            pl.BlockSpec((None, part, columns), lambda i, k, spots: (i, 0, 0)),
            pl.BlockSpec((None, part, columns), lambda i, k, spots: (i, 0, 0)),
        ]
        + [pl.BlockSpec(memory_space=pl.ANY)] * len(before),
        [pl.BlockSpec((part, 3 * width), lambda i, k, spots: (spots[i], 0)), out_spec],
        [
            jax.ShapeDtypeStruct((width // planes, 3 * width), f32),
            jax.ShapeDtypeStruct(out_shape, f32),
        ],
        scalars=1,
        input_output_aliases={3 + i: i for i in range(len(before))},
    )(spots, mine, other, *before)


def place_rows(net, mine, other, factor):
    J = net.J
    _, rows, columns = mine[0].shape
    spots = jnp.concatenate([net.c * J + net.order(), (1 - net.c) * J + net.order(other=True)])
    arrays = (*mine, *other) if net.square else (mine[0], other[0])
    starts = [sum(x.shape[0] for x in arrays[:n]) for n in range(len(arrays))]

    def kernel(spots_ref, *refs):
        here = pl.program_id(0)
        for start, x, ref in zip(starts, arrays, refs):

            @pl.when((here >= start) & (here < start + x.shape[0]))
            def _(ref=ref):
                refs[-1][...] = ref[...].astype(f32) * factor

    def spec(start, count):
        return pl.BlockSpec(
            (None, rows, columns), lambda i, spots: (jnp.clip(i - start, 0, count - 1), 0, 0)
        )

    return call(
        kernel,
        (2 * J,),
        [spec(start, x.shape[0]) for start, x in zip(starts, arrays)],
        pl.BlockSpec((rows, columns), lambda i, spots: (spots[i], 0)),
        jax.ShapeDtypeStruct((2 * J * rows, columns), f32),
        scalars=1,
    )(spots.astype(jnp.int32), *arrays)


def tie(x, *after):
    return lax.optimization_barrier((x, after))[0]


class Links:
    def __init__(self, planes, replicas):
        self.S = planes
        self.J = replicas // CORES
        self.square = self.J == 4
        dp = lax.axis_index("dp")
        self.s = lax.axis_index("shard")
        self.c = dp % CORES
        self.j = dp // CORES
        self.first = jnp.where(self.c == 0, 2, 1)

    def move(self, x, ds=0, dc=0, steps=None):
        pairs = []
        for j in range(self.J):
            for c in range(CORES):
                for s in range(self.S):
                    turn = 0 if steps is None else (2, 1)[(c + steps) % 2]
                    to = ((j ^ turn) * CORES + (c + dc) % CORES) * self.S + (s + ds) % self.S
                    pairs.append(((j * CORES + c) * self.S + s, to))
        return lax.ppermute(x, AXES, pairs)

    def groups(self):
        return [[j * CORES + c for j in range(self.J)] for c in range(CORES)]

    def order(self, other=False):
        if not self.square:
            return jnp.arange(self.J)
        turn = 3 - self.first if other else self.first
        return jnp.stack([self.j, self.j ^ turn, self.j ^ 3 ^ turn, self.j ^ 3])

    def mine(self, i):
        return (i >= 2, (jnp.minimum(i, 1), jnp.maximum(i - 2, 0))) if self.square else (i < 0, (i, 0))

    def theirs(self, i):
        return (i % 2 == 1, (i // 2, i // 2)) if self.square else (i < 0, (i, 0))

    def gather(self, x):
        return self.move(x, steps=0) if self.square else None

    def gather_more(self, stack):
        return self.move(stack, steps=1) if self.square else None

    def spread(self, x):
        if not self.square:
            return x
        other = self.j ^ self.first
        return jnp.stack([pick(x, other, 1), pick(x, other ^ 3 ^ self.first, 1)])

    def spread_sum(self, x, got):
        if not self.square:
            return x, x
        mine = pick(x, self.j, 1), pick(x, self.j ^ 3 ^ self.first, 1)
        return [(m.astype(f32) + g.astype(f32)).astype(bf16) for m, g in zip(mine, got)]

    def spread_last(self, own, got):
        if not self.square:
            return lax.psum_scatter(
                own.astype(f32),
                "dp",
                scatter_dimension=1,
                axis_index_groups=self.groups(),
                tiled=False,
            ).astype(bf16)
        return (own.astype(f32) + got.astype(f32)).astype(bf16)

    def plane_sum(self, x, step):
        if not self.square:
            return lax.psum(x, "dp", axis_index_groups=self.groups()) if step else x
        return x + self.move(x, steps=step)


def swap(x, after=()):
    return lax.all_to_all(tie(x, *after), "shard", 0, 0, tiled=True)


def twofold(x, axis):
    high = lax.reduce_precision(x, 8, 7)
    return jnp.concatenate([high.astype(bf16), (x - high).astype(bf16)], axis=axis)


def as_rows(vector, width, multiple):
    count = -(-vector.shape[0] // (width * multiple)) * multiple
    return jnp.pad(vector, (0, count * width - vector.shape[0])).reshape(count, width)


def pick(x, index, axis):
    return lax.dynamic_index_in_dim(x, index, axis, keepdims=False)


def in_order(held, here):
    size = len(held)
    backwards = jnp.stack(held[::-1])
    return lax.dynamic_slice_in_dim(
        jnp.concatenate([backwards, backwards]), size - 1 - here, size, 0
    )


def local(
    tokens,
    segments,
    ln_gain,
    ln_bias,
    w_qkv,
    b_qkv,
    w_out,
    b_out,
    w_fc1,
    b_fc1,
    w_fc2,
    b_fc2,
    cotangent,
):
    planes = lax.axis_size("shard")
    replicas = lax.axis_size("dp")
    net = Links(planes, replicas)
    S, J, c, j, s = net.S, net.J, net.c, net.j, net.s
    seqs, length, width = tokens.shape
    rows = seqs * length
    ff = w_fc1.shape[1]
    ff_own = ff // (S * CORES)
    mix_own = width // (S * CORES)
    height = width // S
    part = height // J
    total = S * CORES * rows
    back_planes = (s - jnp.arange(S)) % S
    factor = 1.0 / math.sqrt(rows * planes * replicas)

    own_tokens = tokens.reshape(rows, width)
    own_cot = cotangent.reshape(rows, width)
    hops = [jnp.concatenate([own_tokens, own_cot])]
    hops.append(net.move(hops[0], ds=1))

    vectors = [ln_gain, ln_bias, b_qkv, b_out, b_fc1, b_fc2, segments.reshape(-1).astype(bf16)]
    small = jnp.concatenate(vectors)
    size = small.shape[0]
    held = [small] + [net.move(small, ds=k) for k in range(1, S)]

    got = swap(pack(w_fc1, w_qkv, j, c, S, part, ff_own, mix_own))
    others = [net.move(tie(hops[0], hops[1], held), dc=1), net.move(hops[1], dc=1)]
    fc2_rows = lax.dynamic_slice_in_dim(w_fc2, c * ff_own, ff_own, 0)
    out_rows = lax.dynamic_slice_in_dim(w_out, c * mix_own, mix_own, 0)
    marks = jnp.stack([v[size - rows :] for v in held])
    small_all = in_order(held, s)
    whole = []
    start = 0
    for vector in vectors[:-1]:
        whole.append(small_all[:, start : start + vector.shape[0]].reshape(-1).astype(f32))
        start += vector.shape[0]
    gain_full, shift_full, qkv_bias, out_bias, fc1_bias, fc2_bias = whole
    fc1_bias = lax.dynamic_slice_in_dim(fc1_bias, (s * CORES + c) * ff_own, ff_own, 0)
    qkv_bias = lax.dynamic_slice_in_dim(
        qkv_bias.reshape(3, width), (s * CORES + c) * mix_own, mix_own, 1
    ).reshape(-1)
    marks = jnp.stack([marks, net.move(tie(marks, hops[1], held), dc=1)])
    tables = rotary_tables(marks.reshape(-1, length).astype(jnp.int32))
    ready = tie((hops[1], others, fc2_rows, out_rows, tables, gain_full, fc1_bias, qkv_bias), hops[1])
    hop, others, fc2_rows, out_rows, tables, gain_full, fc1_bias, qkv_bias = ready

    got = tie(got, hop, others, fc2_rows, out_rows, tables, gain_full, fc1_bias, qkv_bias)
    block = jnp.concatenate([pick(got, back_planes[k], 0) for k in range(1, S)])[None]
    hops.append(net.move(tie(hop, got), ds=1))
    came = net.gather(block)
    if net.square:
        blocks = tie(join([block, came]))
    else:
        blocks = lax.all_gather(block[0], "dp", axis_index_groups=net.groups())
    came = net.gather_more(blocks)
    while len(hops) < S:
        hops.append(net.move(tie(hops[-1], blocks), ds=1))
        others.append(net.move(tie(hops[-2], blocks), dc=1))
    places = [e * S + k for k in range(S) for e in range(CORES)]
    early = [x for pair in zip(hops[: S - 1], others[: S - 1]) for x in pair]
    early = tie(early, blocks)
    normed_rows = norm(early, places[:-CORES], gain_full, shift_full, S * CORES)
    blocks = tie(blocks, normed_rows)
    spots_w = jnp.concatenate([back_planes, (s * CORES + c)[None]]).astype(jnp.int32)
    chips = net.order()
    weights = lambda x, order, *before: assemble(
        w_fc1,
        w_qkv,
        [x.reshape(-1, S - 1, part, x.shape[-1])],
        order.astype(jnp.int32),
        spots_w,
        ff_own,
        mix_own,
        J,
        *before,
    )
    weight_cols = weights(blocks, chips[: blocks.shape[0]])
    last = tie(hops[-1], weight_cols)
    other = net.move(last, dc=1)
    if net.square:
        weight_cols, came = tie((weight_cols, came), last)
        weight_cols = weights(came, chips[2:], weight_cols)
    last, other = tie((last, other), weight_cols)
    hidden_in, tok_rows, cot_rows, mean, inverse = norm(
        [last, other], places[-CORES:], gain_full, shift_full, S * CORES, normed_rows
    )
    fc1_cols = weight_cols[0].reshape(width, ff_own)
    qkv_cols = weight_cols[1].reshape(width, 3 * mix_own)

    hidden = jnp.dot(hidden_in, fc1_cols, preferred_element_type=f32) + fc1_bias
    active, gelu_back = jax.vjp(lambda v: jax.nn.gelu(v, approximate=True), hidden)
    active = active.astype(bf16)
    transposed = lambda x, y: jnp.einsum("td,te->de", x, y, preferred_element_type=f32).astype(bf16)
    fc2_term = transposed(active, cot_rows)

    mark = []

    def step(x, *made):
        nonlocal mark
        if not made:
            return tie(x, mark)
        mark = list(made)
        return x

    def first_sum(x):
        sent = tie(net.spread(x))
        step(None, sent)
        return x, net.gather(sent)

    def second_sum(x, got):
        x, got = step((x, got))
        own, sent = tie(net.spread_sum(x, got))
        step(None, own, sent)
        return own, net.gather_more(sent)

    def last_sum(own, got):
        part = tie(net.spread_last(*step((own, got))))
        step(None, part)
        return part

    def second_gather(part, came):
        part, came = step((part, came))
        if net.square:
            stack = join([part[None], came[None]])
        else:
            stack = lax.all_gather(part, "dp", axis_index_groups=net.groups())
        stack = tie(stack)
        step(None, stack)
        return stack, net.gather_more(stack)

    def to_other(x):
        return net.move(step(x), dc=1) if net.square else x

    fc2_own, fc2_got = first_sum(fc2_term.reshape(1, J, ff_own // J, width))
    late_cot = step(cot_rows)
    active_grad = jnp.einsum("td,fd->tf", late_cot, fc2_rows, preferred_element_type=f32)
    hidden_grad = gelu_back(active_grad)[0].astype(bf16)
    fc1_term = transposed(hidden_in, hidden_grad)
    fc1_own, fc1_got = first_sum(fc1_term.reshape(S, J, part, ff_own))
    fc2_own, fc2_got = second_sum(fc2_own, fc2_got)
    late_in, late_cot = step((hidden_in, cot_rows))
    mixed = jnp.dot(late_in, qkv_cols, preferred_element_type=f32) + qkv_bias
    context_grad = jnp.einsum("te,de->td", late_cot, out_rows, preferred_element_type=f32).astype(
        bf16
    )
    context, mixed_grad = attention(tables, mixed, context_grad, length)
    step(None, context, mixed_grad)
    fc1_own, fc1_got = second_sum(fc1_own, fc1_got)
    fc2_part = last_sum(fc2_own, fc2_got)[0]
    fc2_came = net.gather(fc2_part)
    late_in, late_cot, late_mixed, late_context = step((hidden_in, cot_rows, mixed_grad, context))
    mixed_term = with_layout_constraint(
        jnp.concatenate(
            [transposed(late_in, late_mixed), transposed(late_cot, late_context)], axis=1
        ),
        Layout((0, 1)),
    )
    mixed_own, mixed_got = first_sum(mixed_term.reshape(S, J, part, 4 * mix_own))
    fc1_part = last_sum(fc1_own, fc1_got)
    fc1_part = swap(fc1_part)
    fc2_part, fc2_came = second_gather(fc2_part, fc2_came)
    fc2_other = net.move(fc2_part, dc=1)
    late_context, late_active = step((context, active))
    branch, branch_other = branches(late_context, out_rows, late_active, fc2_rows)
    step(None, branch, branch_other)
    branch_came = net.move(branch_other, dc=1)
    late_mixed, late_grad = step((mixed_grad, hidden_grad))
    back, back_other, norm_sums = backs(
        late_grad, fc1_cols, late_mixed, qkv_cols, tok_rows, mean, inverse
    )
    step(None, back, back_other, norm_sums)
    back_came = net.move(back_other, dc=1)
    scatter = lambda x: lax.psum_scatter(x, "shard", scatter_dimension=0, tiled=True)[0]
    late_grad, late_mixed, late_cot, norm_sums = step((hidden_grad, mixed_grad, cot_rows, norm_sums))
    mixed_sums = jnp.sum(late_mixed, axis=0, dtype=f32)
    norm_sums = jnp.swapaxes(norm_sums[:2].reshape(2, S, height), 0, 1).reshape(S, -1)
    riders = jnp.concatenate([norm_sums, jnp.broadcast_to(mixed_sums, (S, 3 * mix_own))], axis=1)
    riding = riders.shape[1]
    riders = jnp.pad(riders, ((0, 0), (0, -riding % (24 * mix_own))))
    riders = twofold(riders.reshape(S, -1, 3 * mix_own), 1)
    column_sums = jnp.concatenate(
        [
            jnp.sum(late_grad, axis=0, dtype=f32),
            pick(jnp.sum(late_cot, axis=0, dtype=f32).reshape(S, height), s, 0),
        ]
    )
    riders, column_sums = tie((riders, column_sums))
    step(None, riders, column_sums)
    mixed_own, mixed_got = second_sum(mixed_own, mixed_got)
    fc1_part, fc2_came = step((fc1_part, fc2_came))
    fc1_part = tie(jnp.swapaxes(fc1_part, 0, 1).reshape(part, S * ff_own))
    step(None, fc1_part)
    fc1_came = net.gather(fc1_part)
    if net.square:
        fc2_last = net.move(step(fc2_came), dc=1)
        fc2_mine, fc2_other = (fc2_part, fc2_came), (fc2_other, fc2_last)
    else:
        fc2_mine, fc2_other = (fc2_part, fc2_part), (fc2_other, fc2_other)
    branch_acts = add_in_order(*step((branch, branch_came)), back_planes.astype(jnp.int32))
    back_acts = add_in_order(*step((back, back_came)), back_planes.astype(jnp.int32))
    mark += [branch_acts, back_acts]
    fc1_part, fc1_came = second_gather(fc1_part, fc1_came)
    branch_sum, back_sum = scatter(branch_acts), scatter(back_acts)
    mixed_part = last_sum(mixed_own, mixed_got)
    out_part = mixed_part[:, :, 3 * mix_own :]
    mixed_part = tie(jnp.concatenate([mixed_part[:, :, : 3 * mix_own], riders], axis=1))
    step(None, mixed_part)
    mixed_part = swap(mixed_part)
    fc2_own = place_rows(net, *step((fc2_mine, fc2_other)), factor)
    step(None, fc2_own)
    fc1_other = net.move(step(fc1_part), dc=1)
    if net.square:
        fc1_came = step(fc1_came)
        mark += [fc1_came]
    mixed_part = step(mixed_part)
    riders = mixed_part[:, part:].astype(f32)
    mixed_part = jnp.concatenate([mixed_part[:, :part], out_part], axis=2)
    mixed_part = tie(jnp.swapaxes(mixed_part, 0, 1).reshape(part, S * 4 * mix_own))
    step(None, mixed_part)
    mixed_first, mixed_second = net.gather(mixed_part), net.gather_more(mixed_part)
    mixed_other = net.move(mixed_part, dc=1)
    if net.square:
        fc1_last = net.move(step(fc1_came), dc=1)
        fc1_mine, fc1_other = (fc1_part, fc1_came), (fc1_other, fc1_last)
    else:
        fc1_mine, fc1_other = (fc1_part, fc1_part), (fc1_other, fc1_other)
    count = riders.shape[1] // 2
    riders = step(riders)
    riders = (riders[:, :count] + riders[:, count:]).reshape(S, -1)[:, :riding]
    sums = jnp.concatenate(
        [
            jnp.sum(riders[:, : 2 * height], axis=0),
            column_sums[:ff_own],
            riders[:, 2 * height :].reshape(-1),
            column_sums[ff_own:],
        ]
    )
    sums = tie(sums)
    step(None, sums)
    sums = net.plane_sum(sums, 0)
    if net.square:
        fc1_own = place_columns(net, *step((fc1_mine, fc1_other)), factor)
        step(None, fc1_own)
        own, other = step((mixed_part[None], mixed_other[None]))
        placed = tie(place_mixed(net, own, other, 0, factor))
        step(None, placed)
        mixed_first, sums = tie(step((mixed_first, sums)))
        step(None, mixed_first)
        mixed_last = net.gather_more(mixed_first)
        mixed_second = tie(step(mixed_second))
        step(None, mixed_second)
        first_other, second_other = net.move(mixed_first, dc=1), net.move(mixed_second, dc=1)
        own, other = step((mixed_first[None], second_other[None]))
        placed = tie(place_mixed(net, own, other, 1, factor, placed))
        step(None, placed)
        own, other = step((mixed_second[None], first_other[None]))
        placed = tie(place_mixed(net, own, other, 2, factor, placed))
        step(None, placed)
        sums = net.plane_sum(tie(step(sums)), 1)
        mixed_last = tie(step(mixed_last))
        sums_came = net.move(tie(sums, mixed_last), dc=1)
        last_other = net.move(mixed_last, dc=1)
        placed = place_mixed(net, mixed_last[None], last_other[None], 3, factor, placed)
    else:
        mixed_near = lax.all_gather(mixed_part, "dp", axis_index_groups=net.groups())
        fc1_own = place_columns(net, *step((fc1_mine, fc1_other)), factor)
        sums = net.plane_sum(sums, 1)
        sums_came = net.move(sums, dc=1)
        placed = place_mixed(net, mixed_near, net.move(mixed_near, dc=1), 0, factor)
    qkv_own, out_own = placed
    if out_own.ndim == 4:
        out_own = jnp.transpose(out_own, (2, 0, 1, 3)).reshape(height, width)

    own_inputs = own_tokens.astype(f32)
    output = (own_inputs + branch_sum.astype(f32) + (out_bias + fc2_bias)).astype(bf16)
    normed = (own_inputs - mean[:rows, :1]) * inverse[:rows, :1]
    scaled = back_sum.astype(f32) * gain_full
    input_grad = own_cot.astype(f32) + inverse[:rows, :1] * (
        scaled
        - jnp.mean(scaled, axis=1, keepdims=True)
        - normed * jnp.mean(scaled * normed, axis=1, keepdims=True)
    )

    gain_own = (sums[:height] + sums_came[:height]) * factor
    shift_own = (sums[height : 2 * height] + sums_came[height : 2 * height]) * factor
    bias_own = sums[-height:] * factor
    pairs = jnp.where(c == 0, jnp.stack([sums, sums_came]), jnp.stack([sums_came, sums]))
    pairs = pairs[:, 2 * height : -height]
    fc1_bias_own = pairs[:, :ff_own].reshape(-1) * factor
    mixed_sums = jnp.transpose(pairs[:, ff_own:].reshape(CORES, S, 3, mix_own), (2, 1, 0, 3))
    qkv_bias_own = pick(mixed_sums.reshape(S, -1), s, 0) * factor
    return (
        output.reshape(tokens.shape),
        input_grad.reshape(tokens.shape),
        gain_own,
        shift_own,
        qkv_own,
        qkv_bias_own,
        out_own,
        bias_own,
        fc1_own,
        fc1_bias_own,
        fc2_own,
        bias_own,
    )


def solution(mesh):
    return jax.shard_map(
        local,
        mesh=mesh,
        in_specs=(
            P(("dp", "shard"), None, None),
            P(("dp", "shard"), None),
            P("shard"),
            P("shard"),
            P("shard", None),
            P("shard"),
            P("shard", None),
            P("shard"),
            P("shard", None),
            P("shard"),
            P("shard", None),
            P("shard"),
            P(("dp", "shard"), None, None),
        ),
        out_specs=(
            P(("dp", "shard"), None, None),
            P(("dp", "shard"), None, None),
            P("shard"),
            P("shard"),
            P("shard", None),
            P("shard"),
            P("shard", None),
            P("shard"),
            P("shard", None),
            P("shard"),
            P("shard", None),
            P("shard"),
        ),
        check_vma=False,
    )
```

```python
import math

import jax
import jax.numpy as jnp
from jax import lax
from jax.experimental import pallas as pl
from jax.experimental.pallas import tpu as pltpu
from jax.experimental.layout import Layout, with_layout_constraint
from jax.sharding import PartitionSpec as P

HEADS = 32
HEAD_DIM = 64
ROT = 32
CORES = 2
LANES = 128

epsilon = 1e-05
masked_value = -1e30
AXES = ("dp", "shard")
f32 = jnp.float32
bf16 = jnp.bfloat16
VMEM = 48 * 1024 * 1024


def rotary_tables(segments):
    seqs, length = segments.shape
    positions = jnp.broadcast_to(jnp.arange(length, dtype=jnp.int32), segments.shape)
    change = jnp.concatenate(
        [jnp.ones((seqs, 1), dtype=bool), segments[:, 1:] != segments[:, :-1]], axis=1
    )
    run_start = lax.cummax(jnp.where(change, positions, 0), axis=1)
    distance = (positions - run_start).astype(f32).reshape(-1, 1)
    lane = jnp.arange(LANES, dtype=jnp.int32) % HEAD_DIM
    half = ROT // 2
    frequency = jnp.exp((lane % half).astype(f32) * (-2.0 * math.log(10000.0) / ROT))
    angles = distance * frequency[None, :]
    sines = jnp.sin(angles)
    cos_table = jnp.where(lane < ROT, jnp.cos(angles), 1.0)
    low_table = jnp.where(lane < half, -sines, 0.0)
    high_table = jnp.where((lane >= half) & (lane < ROT), sines, 0.0)
    starts = jnp.broadcast_to(run_start.reshape(-1, 1), (seqs * length, LANES))
    return starts, cos_table, low_table, high_table


def attention_kernel(
    starts_ref, cos_ref, low_ref, high_ref, mixed_ref, outer_ref, context_ref, grad_ref
):
    length, width = outer_ref.shape
    half = ROT // 2
    scale = HEAD_DIM ** (-0.5)

    def wide(table):
        return jnp.concatenate([table[...]] * (width // LANES), axis=1)

    cos_table, low_table, high_table = wide(cos_ref), wide(low_ref), wide(high_ref)

    def rotate(v, sign):
        turned = pltpu.roll(v, width - half, 1) * low_table + pltpu.roll(v, half, 1) * high_table
        return v * cos_table + sign * turned

    queries = rotate(mixed_ref[:, :width], 1.0).astype(bf16)
    key_rows = rotate(mixed_ref[:, width : 2 * width], 1.0).astype(bf16)
    values = mixed_ref[:, 2 * width :].astype(bf16)
    outer = outer_ref[...]
    row = lax.broadcasted_iota(jnp.int32, (length, length), 0)
    column = lax.broadcasted_iota(jnp.int32, (length, length), 1)
    allowed = (column <= row) & (column >= starts_ref[...])
    spans = [slice(h * HEAD_DIM, (h + 1) * HEAD_DIM) for h in range(width // HEAD_DIM)]
    block = lambda x, h: x[h * length : (h + 1) * length]
    heads = range(len(spans))
    allowed = jnp.concatenate([allowed] * len(spans), axis=0)
    scores = jnp.concatenate([dot(queries[:, p], key_rows[:, p], ((1,), (1,))) for p in spans], axis=0)
    scores = jnp.where(allowed, scores * scale, masked_value)
    weights = jnp.exp(scores - jnp.max(scores, axis=1, keepdims=True))
    probs = weights / jnp.sum(weights, axis=1, keepdims=True)
    low = probs.astype(bf16)
    prob_grad = jnp.concatenate([dot(outer[:, p], values[:, p], ((1,), (1,))) for p in spans], axis=0)
    inner = jnp.sum(prob_grad * probs, axis=1, keepdims=True)
    score_grad = (probs * (prob_grad - inner)).astype(bf16)
    context = [dot(block(low, h), values[:, spans[h]], ((1,), (0,))) for h in heads]
    value_grad = [dot(block(low, h), outer[:, spans[h]], ((0,), (0,))) for h in heads]
    query_grad = [dot(block(score_grad, h), key_rows[:, spans[h]], ((1,), (0,))) for h in heads]
    key_grad = [dot(block(score_grad, h), queries[:, spans[h]], ((0,), (0,))) for h in heads]
    side = lambda x: jnp.concatenate(x, axis=1)
    context_ref[...] = side(context).astype(bf16)
    grad_ref[:, :width] = rotate(side(query_grad) * scale, -1.0).astype(bf16)
    grad_ref[:, width : 2 * width] = rotate(side(key_grad) * scale, -1.0).astype(bf16)
    grad_ref[:, 2 * width :] = side(value_grad).astype(bf16)


def attention(tables, mixed, outer, length):
    rows, width = outer.shape
    wide = lambda columns: pl.BlockSpec((length, columns), lambda i: (i, 0))
    return pl.pallas_call(
        attention_kernel,
        grid=(rows // length,),
        in_specs=[wide(LANES)] * 4 + [wide(3 * width), wide(width)],
        out_specs=[wide(width), wide(3 * width)],
        out_shape=[
            jax.ShapeDtypeStruct((rows, width), bf16),
            jax.ShapeDtypeStruct((rows, 3 * width), bf16),
        ],
        cost_estimate=pl.CostEstimate(flops=2 * 10**9, bytes_accessed=0, transcendentals=0),
        compiler_params=pltpu.CompilerParams(vmem_limit_bytes=VMEM),
    )(*tables, mixed, outer)


def call(kernel, grid, in_specs, out_specs, out_shape, scalars=0, us=0, **more):
    return pl.pallas_call(
        kernel,
        grid_spec=pltpu.PrefetchScalarGridSpec(
            num_scalar_prefetch=scalars, grid=grid, in_specs=in_specs, out_specs=out_specs
        ),
        out_shape=out_shape,
        cost_estimate=pl.CostEstimate(flops=us * 10**9 // 6, bytes_accessed=0, transcendentals=0),
        compiler_params=pltpu.CompilerParams(vmem_limit_bytes=VMEM),
        **more,
    )


def dot(a, b, dims):
    return lax.dot_general(a, b, (dims, ((), ())), preferred_element_type=f32)


def pack(w_fc1, w_qkv, row, core, planes, part, own, piece):
    third = w_qkv.shape[1] // 3 // piece
    cols = own + 3 * piece
    spots = jnp.stack([row, core]).astype(jnp.int32)

    def kernel(spots_ref, fc1_ref, q_ref, k_ref, v_ref, out_ref):
        out_ref[:, :own] = fc1_ref[...]
        for i, ref in enumerate((q_ref, k_ref, v_ref)):
            out_ref[:, own + i * piece : own + (i + 1) * piece] = ref[...]

    cut = lambda i: pl.BlockSpec(
        (part, piece), lambda p, spots: (spots[0], i * third + p * CORES + spots[1])
    )
    return call(
        kernel,
        (planes,),
        [
            pl.BlockSpec((part, own), lambda p, spots: (spots[0], p * CORES + spots[1])),
            cut(0),
            cut(1),
            cut(2),
        ],
        pl.BlockSpec((None, part, cols), lambda p, spots: (p, 0, 0)),
        jax.ShapeDtypeStruct((planes, part, cols), bf16),
        scalars=1,
    )(spots, w_fc1, w_qkv, w_qkv, w_qkv)


def assemble(w_fc1, w_qkv, arrays, order, spots, own, piece, blocks, before=None):
    _, others, rows, cols = arrays[0].shape
    planes = others + 1
    height = w_fc1.shape[0]
    third = w_qkv.shape[1] // 3 // piece

    def kernel(order_ref, spots_ref, fc1_ref, q_ref, k_ref, v_ref, *refs):
        fc1_out, qkv_out = refs[-2:]
        here = spots_ref[0]
        fc1_out[here] = fc1_ref[...]
        for i, ref in enumerate((q_ref, k_ref, v_ref)):
            qkv_out[here, :, i * piece : (i + 1) * piece] = ref[...]
        places = [(ref, m) for ref in refs[: len(arrays)] for m in range(ref.shape[0])]
        for n, (ref, m) in enumerate(places):

            @pl.when(pl.program_id(0) == n)
            def _(ref=ref, m=m):
                for k in range(1, planes):
                    there = spots_ref[k]
                    fc1_out[there] = ref[m, k - 1, :, :own]
                    qkv_out[there] = ref[m, k - 1, :, own:]

    cut = lambda i: pl.BlockSpec(
        (None, rows, piece), lambda n, order, spots: (order[n], 0, i * third + spots[planes])
    )
    result = lambda size: pl.BlockSpec(
        (planes, None, rows, size), lambda n, order, spots: (0, order[n], 0, 0)
    )
    more = {}
    if before is not None:
        first = 6 + len(arrays)
        more["input_output_aliases"] = {first: 0, first + 1: 1}
    return call(
        kernel,
        (sum(x.shape[0] for x in arrays),),
        [
            pl.BlockSpec((None, rows, own), lambda n, order, spots: (order[n], 0, spots[planes])),
            cut(0),
            cut(1),
            cut(2),
        ]
        + [pl.BlockSpec(x.shape, lambda n, order, spots: (0, 0, 0, 0)) for x in arrays]
        + [pl.BlockSpec(memory_space=pl.ANY)] * (0 if before is None else 2),
        [result(own), result(3 * piece)],
        [
            jax.ShapeDtypeStruct((planes, blocks, rows, own), bf16),
            jax.ShapeDtypeStruct((planes, blocks, rows, 3 * piece), bf16),
        ],
        scalars=2,
        **more,
    )(
        order,
        spots,
        w_fc1.reshape(blocks, rows, -1),
        *[w_qkv.reshape(blocks, rows, -1)] * 3,
        *arrays,
        *(before or ()),
    )


def norm(arrays, places, gain, shift, blocks, before=None):
    rows, width = arrays[0].shape[0] // 2, arrays[0].shape[1]

    def kernel(places_ref, gain_ref, shift_ref, *refs):
        out_ref, tokens_ref, cot_ref, mean_ref, inverse_ref = refs[-5:]
        for n in range(len(arrays)):

            @pl.when(pl.program_id(0) == n)
            def _(ref=refs[n]):
                tokens_ref[...] = ref[:rows]
                cot_ref[...] = ref[rows:]
                x = ref[:rows].astype(f32)
                mean = jnp.mean(x, axis=1, keepdims=True)
                centred = x - mean
                inverse = lax.rsqrt(jnp.mean(centred * centred, axis=1, keepdims=True) + epsilon)
                out_ref[...] = (centred * inverse * gain_ref[...] + shift_ref[...]).astype(bf16)
                mean_ref[...] = jnp.broadcast_to(mean, mean_ref.shape)
                inverse_ref[...] = jnp.broadcast_to(inverse, inverse_ref.shape)

    line = pl.BlockSpec((1, width), lambda i, places: (0, 0))
    wide = pl.BlockSpec((rows, width), lambda i, places: (places[i], 0))
    slim = pl.BlockSpec((rows, LANES), lambda i, places: (places[i], 0))
    more = {}
    if before is not None:
        more["input_output_aliases"] = {3 + len(arrays) + i: i for i in range(5)}
    return call(
        kernel,
        (len(arrays),),
        [line, line]
        + [pl.BlockSpec(x.shape, lambda i, places: (0, 0)) for x in arrays]
        + [pl.BlockSpec(memory_space=pl.ANY)] * (0 if before is None else 5),
        [wide, wide, wide, slim, slim],
        [jax.ShapeDtypeStruct((blocks * rows, width), bf16)] * 3
        + [jax.ShapeDtypeStruct((blocks * rows, LANES), f32)] * 2,
        scalars=1,
        **more,
    )(
        jnp.asarray(places, jnp.int32),
        gain.reshape(1, width),
        shift.reshape(1, width),
        *arrays,
        *(before or ()),
    )


def join(*lists):
    shape = lists[0][0].shape[1:]
    spans, arrays, total = [], [], 0
    for some in lists:
        start = total
        for x in some:
            arrays.append((total, x))
            total += x.shape[0]
        spans.append((start, total - start))

    def kernel(*refs):
        here = pl.program_id(0)
        for n, (start, x) in enumerate(arrays):
            for out, (first, count) in zip(refs[len(arrays) :], spans):
                if first <= start < first + count:

                    @pl.when((here >= start) & (here < start + x.shape[0]))
                    def _(ref=refs[n], out=out):
                        out[...] = ref[...]

    def spec(first, count):
        return pl.BlockSpec(
            (None,) + shape,
            lambda i: (jnp.clip(i - first, 0, count - 1),) + (0,) * len(shape),
        )

    results = call(
        kernel,
        (total,),
        [spec(start, x.shape[0]) for start, x in arrays],
        [spec(*span) for span in spans],
        [jax.ShapeDtypeStruct((count,) + shape, arrays[0][1].dtype) for _, count in spans],
        us=3,
    )(*[x for _, x in arrays])
    return results if len(lists) > 1 else results[0]


def add_in_order(mine, came, order):
    count = order.shape[0]
    rows, width = mine.shape[0] // count, mine.shape[1]

    def kernel(order_ref, mine_ref, came_ref, out_ref):
        out_ref[...] = (mine_ref[...] + came_ref[...].astype(f32)).astype(bf16)

    block = pl.BlockSpec((rows, width), lambda i, order: (i, 0))
    return call(
        kernel,
        (count,),
        [block, block],
        pl.BlockSpec((None, rows, width), lambda i, order: (order[i], 0, 0)),
        jax.ShapeDtypeStruct((count, rows, width), bf16),
        scalars=1,
    )(order, mine, came)


def branches(context, out_rows, active, fc2_rows):
    total, width = context.shape[0], out_rows.shape[1]
    half, block = total // 2, 256

    def kernel(context_ref, out_ref, active_ref, fc2_ref, mine_ref, other_ref):
        y = dot(context_ref[...], out_ref[...], ((1,), (0,)))
        y = y + dot(active_ref[...], fc2_ref[...], ((1,), (0,)))
        mine_ref[...] = y[:half]
        other_ref[...] = y[half:].astype(bf16)

    whole = lambda x: pl.BlockSpec(x.shape, lambda i: (0, 0))
    part = lambda rows: pl.BlockSpec((rows, block), lambda i: (0, i))
    return call(
        kernel,
        (width // block,),
        [whole(context), part(out_rows.shape[0]), whole(active), part(fc2_rows.shape[0])],
        [part(half), part(half)],
        [jax.ShapeDtypeStruct((half, width), f32), jax.ShapeDtypeStruct((half, width), bf16)],
        us=10,
    )(context, out_rows, active, fc2_rows)


def backs(hidden_grad, fc1_cols, mixed_grad, qkv_cols, tokens, mean, inverse):
    total, width = mean.shape[0], fc1_cols.shape[0]
    half, block = total // 2, 256

    def kernel(
        hidden_ref, fc1_ref, mixed_ref, qkv_ref, tokens_ref, mean_ref, inverse_ref,
        first_ref, second_ref, sums_ref,
    ):
        y = dot(hidden_ref[...], fc1_ref[...], ((1,), (1,)))
        y = y + dot(mixed_ref[...], qkv_ref[...], ((1,), (1,)))
        first_ref[...] = y[:half]
        second_ref[...] = y[half:].astype(bf16)
        normed = (tokens_ref[...].astype(f32) - mean_ref[:, :1]) * inverse_ref[:, :1]
        sums_ref[0:1, :] = jnp.sum(y * normed, axis=0, keepdims=True)
        sums_ref[1:2, :] = jnp.sum(y, axis=0, keepdims=True)
        sums_ref[2:8, :] = jnp.zeros((6, block), f32)

    whole = lambda x: pl.BlockSpec(x.shape, lambda i: (0, 0))
    part = lambda rows: pl.BlockSpec((rows, block), lambda i: (0, i))
    rhs = lambda x: pl.BlockSpec((block, x.shape[1]), lambda i: (i, 0))
    return call(
        kernel,
        (width // block,),
        [
            whole(hidden_grad),
            rhs(fc1_cols),
            whole(mixed_grad),
            rhs(qkv_cols),
            part(total),
            whole(mean),
            whole(inverse),
        ],
        [part(half), part(half), part(8)],
        [
            jax.ShapeDtypeStruct((half, width), f32),
            jax.ShapeDtypeStruct((half, width), bf16),
            jax.ShapeDtypeStruct((8, width), f32),
        ],
        us=14,
    )(hidden_grad, fc1_cols, mixed_grad, qkv_cols, tokens, mean, inverse)


def place_columns(net, mine, other, factor):
    J, planes = net.J, net.S
    _, rows, columns = mine[0].shape
    piece = columns // planes
    spots = jnp.concatenate([net.order(), jnp.stack([net.c, 1 - net.c])]).astype(jnp.int32)
    high = rows // 2

    def kernel(spots_ref, m0_ref, m1_ref, o0_ref, o1_ref, out_ref):
        here = pl.program_id(0)
        for e, (place, refs) in enumerate(
            ((net.mine, (m0_ref, m1_ref)), (net.theirs, (o0_ref, o1_ref)))
        ):
            last, _ = place(here)
            for ref, chosen in zip(refs, (jnp.logical_not(last), last)):

                @pl.when(chosen)
                def _(e=e, ref=ref):
                    for k in range(planes):
                        column = (k * CORES + spots_ref[J + e]) * piece
                        out_ref[:, pl.ds(pl.multiple_of(column, LANES), piece)] = (
                            ref[:, k * piece : (k + 1) * piece].astype(f32) * factor
                        )

    return call(
        kernel,
        (J, 2),
        [
            pl.BlockSpec(
                (None, high, columns), lambda i, h, spots, place=place, n=n: (place(i)[1][n], h, 0)
            )
            for place in (net.mine, net.theirs)
            for n in range(2)
        ],
        pl.BlockSpec((high, 2 * columns), lambda i, h, spots: (spots[i] * 2 + h, 0)),
        jax.ShapeDtypeStruct((J * rows, 2 * columns), f32),
        scalars=1,
    )(spots, *mine, *other)


def place_mixed(net, mine, other, start, factor, before=None):
    J, planes = net.J, net.S
    count, part, columns = mine.shape
    piece = columns // planes // 4
    width = planes * CORES * piece
    chips = net.order()[start : start + count]
    spots = jnp.concatenate([chips, jnp.stack([net.c, 1 - net.c])]).astype(jnp.int32)

    def kernel(spots_ref, mine_ref, other_ref, *refs):
        qkv_ref, out_ref = refs[-2:]
        for e, ref in enumerate((mine_ref, other_ref)):
            core = spots_ref[count + e]
            for k in range(planes):

                @pl.when(pl.program_id(1) == k)
                def _(k=k, core=core, ref=ref):
                    for i in range(3):
                        start = (4 * k + i) * piece
                        column = ((i * planes + k) * CORES + core) * piece
                        qkv_ref[:, pl.ds(pl.multiple_of(column, LANES), piece)] = (
                            ref[:, start : start + piece].astype(f32) * factor
                        )
                    block = ref[:, (4 * k + 3) * piece : (4 * k + 4) * piece].astype(f32)
                    out_ref[pl.ds(pl.multiple_of(core * piece, LANES), piece), :] = (
                        block * factor
                    ).T

    if part % LANES == 0:
        out_shape = (CORES * piece, planes * J * part)
        out_spec = pl.BlockSpec((CORES * piece, part), lambda i, k, spots: (0, k * J + spots[i]))
    else:
        out_shape = (planes, J, CORES * piece, part)
        out_spec = pl.BlockSpec(
            (None, None, CORES * piece, part), lambda i, k, spots: (k, spots[i], 0, 0)
        )
    before = before or ()
    return call(
        kernel,
        (count, planes),
        [
            pl.BlockSpec((None, part, columns), lambda i, k, spots: (i, 0, 0)),
            pl.BlockSpec((None, part, columns), lambda i, k, spots: (i, 0, 0)),
        ]
        + [pl.BlockSpec(memory_space=pl.ANY)] * len(before),
        [pl.BlockSpec((part, 3 * width), lambda i, k, spots: (spots[i], 0)), out_spec],
        [
            jax.ShapeDtypeStruct((width // planes, 3 * width), f32),
            jax.ShapeDtypeStruct(out_shape, f32),
        ],
        scalars=1,
        input_output_aliases={3 + i: i for i in range(len(before))},
    )(spots, mine, other, *before)


def place_rows(net, mine, other, factor):
    J = net.J
    _, rows, columns = mine[0].shape
    spots = jnp.concatenate([net.c * J + net.order(), (1 - net.c) * J + net.order(other=True)])
    arrays = (*mine, *other) if net.square else (mine[0], other[0])
    starts = [sum(x.shape[0] for x in arrays[:n]) for n in range(len(arrays))]

    def kernel(spots_ref, *refs):
        here = pl.program_id(0)
        for start, x, ref in zip(starts, arrays, refs):

            @pl.when((here >= start) & (here < start + x.shape[0]))
            def _(ref=ref):
                refs[-1][...] = ref[...].astype(f32) * factor

    def spec(start, count):
        return pl.BlockSpec(
            (None, rows, columns), lambda i, spots: (jnp.clip(i - start, 0, count - 1), 0, 0)
        )

    return call(
        kernel,
        (2 * J,),
        [spec(start, x.shape[0]) for start, x in zip(starts, arrays)],
        pl.BlockSpec((rows, columns), lambda i, spots: (spots[i], 0)),
        jax.ShapeDtypeStruct((2 * J * rows, columns), f32),
        scalars=1,
    )(spots.astype(jnp.int32), *arrays)


def tie(x, *after):
    return lax.optimization_barrier((x, after))[0]


class Links:
    def __init__(self, planes, replicas):
        self.S = planes
        self.J = replicas // CORES
        self.square = self.J == 4
        dp = lax.axis_index("dp")
        self.s = lax.axis_index("shard")
        self.c = dp % CORES
        self.j = dp // CORES
        self.first = jnp.where(self.c == 0, 2, 1)

    def move(self, x, ds=0, dc=0, steps=None):
        pairs = []
        for j in range(self.J):
            for c in range(CORES):
                for s in range(self.S):
                    turn = 0 if steps is None else (2, 1)[(c + steps) % 2]
                    to = ((j ^ turn) * CORES + (c + dc) % CORES) * self.S + (s + ds) % self.S
                    pairs.append(((j * CORES + c) * self.S + s, to))
        return lax.ppermute(x, AXES, pairs)

    def groups(self):
        return [[j * CORES + c for j in range(self.J)] for c in range(CORES)]

    def order(self, other=False):
        if not self.square:
            return jnp.arange(self.J)
        turn = 3 - self.first if other else self.first
        return jnp.stack([self.j, self.j ^ turn, self.j ^ 3 ^ turn, self.j ^ 3])

    def mine(self, i):
        return (i >= 2, (jnp.minimum(i, 1), jnp.maximum(i - 2, 0))) if self.square else (i < 0, (i, 0))

    def theirs(self, i):
        return (i % 2 == 1, (i // 2, i // 2)) if self.square else (i < 0, (i, 0))

    def gather(self, x):
        return self.move(x, steps=0) if self.square else None

    def gather_more(self, stack):
        return self.move(stack, steps=1) if self.square else None

    def spread(self, x):
        if not self.square:
            return x
        other = self.j ^ self.first
        return jnp.stack([pick(x, other, 1), pick(x, other ^ 3 ^ self.first, 1)])

    def spread_sum(self, x, got):
        if not self.square:
            return x, x
        mine = pick(x, self.j, 1), pick(x, self.j ^ 3 ^ self.first, 1)
        return [(m.astype(f32) + g.astype(f32)).astype(bf16) for m, g in zip(mine, got)]

    def spread_last(self, own, got):
        if not self.square:
            return lax.psum_scatter(
                own.astype(f32),
                "dp",
                scatter_dimension=1,
                axis_index_groups=self.groups(),
                tiled=False,
            ).astype(bf16)
        return (own.astype(f32) + got.astype(f32)).astype(bf16)

    def plane_sum(self, x, step):
        if not self.square:
            return lax.psum(x, "dp", axis_index_groups=self.groups()) if step else x
        return x + self.move(x, steps=step)


def swap(x, after=()):
    return lax.all_to_all(tie(x, *after), "shard", 0, 0, tiled=True)


def twofold(x, axis):
    high = lax.reduce_precision(x, 8, 7)
    return jnp.concatenate([high.astype(bf16), (x - high).astype(bf16)], axis=axis)


def as_rows(vector, width, multiple):
    count = -(-vector.shape[0] // (width * multiple)) * multiple
    return jnp.pad(vector, (0, count * width - vector.shape[0])).reshape(count, width)


def pick(x, index, axis):
    return lax.dynamic_index_in_dim(x, index, axis, keepdims=False)


def in_order(held, here):
    size = len(held)
    backwards = jnp.stack(held[::-1])
    return lax.dynamic_slice_in_dim(
        jnp.concatenate([backwards, backwards]), size - 1 - here, size, 0
    )


def local(
    tokens,
    segments,
    ln_gain,
    ln_bias,
    w_qkv,
    b_qkv,
    w_out,
    b_out,
    w_fc1,
    b_fc1,
    w_fc2,
    b_fc2,
    cotangent,
):
    planes = lax.axis_size("shard")
    replicas = lax.axis_size("dp")
    net = Links(planes, replicas)
    S, J, c, j, s = net.S, net.J, net.c, net.j, net.s
    seqs, length, width = tokens.shape
    rows = seqs * length
    ff = w_fc1.shape[1]
    ff_own = ff // (S * CORES)
    mix_own = width // (S * CORES)
    height = width // S
    part = height // J
    total = S * CORES * rows
    back_planes = (s - jnp.arange(S)) % S
    factor = 1.0 / math.sqrt(rows * planes * replicas)

    own_tokens = tokens.reshape(rows, width)
    own_cot = cotangent.reshape(rows, width)
    hops = [jnp.concatenate([own_tokens, own_cot])]
    hops.append(net.move(hops[0], ds=1))

    vectors = [ln_gain, ln_bias, b_qkv, b_out, b_fc1, b_fc2, segments.reshape(-1).astype(bf16)]
    small = jnp.concatenate(vectors)
    size = small.shape[0]
    held = [small] + [net.move(small, ds=k) for k in range(1, S)]

    got = swap(pack(w_fc1, w_qkv, j, c, S, part, ff_own, mix_own))
    others = [net.move(tie(hops[0], hops[1], held), dc=1), net.move(hops[1], dc=1)]
    fc2_rows = lax.dynamic_slice_in_dim(w_fc2, c * ff_own, ff_own, 0)
    out_rows = lax.dynamic_slice_in_dim(w_out, c * mix_own, mix_own, 0)
    marks = jnp.stack([v[size - rows :] for v in held])
    small_all = in_order(held, s)
    whole = []
    start = 0
    for vector in vectors[:-1]:
        whole.append(small_all[:, start : start + vector.shape[0]].reshape(-1).astype(f32))
        start += vector.shape[0]
    gain_full, shift_full, qkv_bias, out_bias, fc1_bias, fc2_bias = whole
    fc1_bias = lax.dynamic_slice_in_dim(fc1_bias, (s * CORES + c) * ff_own, ff_own, 0)
    qkv_bias = lax.dynamic_slice_in_dim(
        qkv_bias.reshape(3, width), (s * CORES + c) * mix_own, mix_own, 1
    ).reshape(-1)
    marks = jnp.stack([marks, net.move(tie(marks, hops[1], held), dc=1)])
    tables = rotary_tables(marks.reshape(-1, length).astype(jnp.int32))
    ready = tie((hops[1], others, fc2_rows, out_rows, tables, gain_full, fc1_bias, qkv_bias), hops[1])
    hop, others, fc2_rows, out_rows, tables, gain_full, fc1_bias, qkv_bias = ready

    got = tie(got, hop, others, fc2_rows, out_rows, tables, gain_full, fc1_bias, qkv_bias)
    block = jnp.concatenate([pick(got, back_planes[k], 0) for k in range(1, S)])[None]
    hops.append(net.move(tie(hop, got), ds=1))
    came = net.gather(block)
    if net.square:
        blocks = tie(join([block, came]))
    else:
        blocks = lax.all_gather(block[0], "dp", axis_index_groups=net.groups())
    came = net.gather_more(blocks)
    while len(hops) < S:
        hops.append(net.move(tie(hops[-1], blocks), ds=1))
        others.append(net.move(tie(hops[-2], blocks), dc=1))
    places = [e * S + k for k in range(S) for e in range(CORES)]
    early = [x for pair in zip(hops[: S - 1], others[: S - 1]) for x in pair]
    early = tie(early, blocks)
    normed_rows = norm(early, places[:-CORES], gain_full, shift_full, S * CORES)
    blocks = tie(blocks, normed_rows)
    spots_w = jnp.concatenate([back_planes, (s * CORES + c)[None]]).astype(jnp.int32)
    chips = net.order()
    weights = lambda x, order, *before: assemble(
        w_fc1,
        w_qkv,
        [x.reshape(-1, S - 1, part, x.shape[-1])],
        order.astype(jnp.int32),
        spots_w,
        ff_own,
        mix_own,
        J,
        *before,
    )
    weight_cols = weights(blocks, chips[: blocks.shape[0]])
    last = tie(hops[-1], weight_cols)
    other = net.move(last, dc=1)
    if net.square:
        weight_cols, came = tie((weight_cols, came), last)
        weight_cols = weights(came, chips[2:], weight_cols)
    last, other = tie((last, other), weight_cols)
    hidden_in, tok_rows, cot_rows, mean, inverse = norm(
        [last, other], places[-CORES:], gain_full, shift_full, S * CORES, normed_rows
    )
    fc1_cols = weight_cols[0].reshape(width, ff_own)
    qkv_cols = weight_cols[1].reshape(width, 3 * mix_own)

    hidden = jnp.dot(hidden_in, fc1_cols, preferred_element_type=f32) + fc1_bias
    active, gelu_back = jax.vjp(lambda v: jax.nn.gelu(v, approximate=True), hidden)
    active = active.astype(bf16)
    transposed = lambda x, y: jnp.einsum("td,te->de", x, y, preferred_element_type=f32).astype(bf16)
    fc2_term = transposed(active, cot_rows)

    mark = []

    def step(x, *made):
        nonlocal mark
        if not made:
            return tie(x, mark)
        mark = list(made)
        return x

    def first_sum(x):
        sent = tie(net.spread(x))
        step(None, sent)
        return x, net.gather(sent)

    def second_sum(x, got):
        x, got = step((x, got))
        own, sent = tie(net.spread_sum(x, got))
        step(None, own, sent)
        return own, net.gather_more(sent)

    def last_sum(own, got):
        part = tie(net.spread_last(*step((own, got))))
        step(None, part)
        return part

    def second_gather(part, came):
        part, came = step((part, came))
        if net.square:
            stack = join([part[None], came[None]])
        else:
            stack = lax.all_gather(part, "dp", axis_index_groups=net.groups())
        stack = tie(stack)
        step(None, stack)
        return stack, net.gather_more(stack)

    def to_other(x):
        return net.move(step(x), dc=1) if net.square else x

    fc2_own, fc2_got = first_sum(fc2_term.reshape(1, J, ff_own // J, width))
    late_cot = step(cot_rows)
    active_grad = jnp.einsum("td,fd->tf", late_cot, fc2_rows, preferred_element_type=f32)
    hidden_grad = gelu_back(active_grad)[0].astype(bf16)
    fc1_term = transposed(hidden_in, hidden_grad)
    fc1_own, fc1_got = first_sum(fc1_term.reshape(S, J, part, ff_own))
    fc2_own, fc2_got = second_sum(fc2_own, fc2_got)
    late_in, late_cot = step((hidden_in, cot_rows))
    mixed = jnp.dot(late_in, qkv_cols, preferred_element_type=f32) + qkv_bias
    context_grad = jnp.einsum("te,de->td", late_cot, out_rows, preferred_element_type=f32).astype(
        bf16
    )
    context, mixed_grad = attention(tables, mixed, context_grad, length)
    step(None, context, mixed_grad)
    fc1_own, fc1_got = second_sum(fc1_own, fc1_got)
    fc2_part = last_sum(fc2_own, fc2_got)[0]
    fc2_came = net.gather(fc2_part)
    late_in, late_cot, late_mixed, late_context = step((hidden_in, cot_rows, mixed_grad, context))
    mixed_term = with_layout_constraint(
        jnp.concatenate(
            [transposed(late_in, late_mixed), transposed(late_cot, late_context)], axis=1
        ),
        Layout((0, 1)),
    )
    mixed_own, mixed_got = first_sum(mixed_term.reshape(S, J, part, 4 * mix_own))
    fc1_part = last_sum(fc1_own, fc1_got)
    fc1_part = swap(fc1_part)
    fc2_part, fc2_came = second_gather(fc2_part, fc2_came)
    fc2_other = net.move(fc2_part, dc=1)
    late_context, late_active = step((context, active))
    branch, branch_other = branches(late_context, out_rows, late_active, fc2_rows)
    step(None, branch, branch_other)
    branch_came = net.move(branch_other, dc=1)
    late_mixed, late_grad = step((mixed_grad, hidden_grad))
    back, back_other, norm_sums = backs(
        late_grad, fc1_cols, late_mixed, qkv_cols, tok_rows, mean, inverse
    )
    step(None, back, back_other, norm_sums)
    back_came = net.move(back_other, dc=1)
    scatter = lambda x: lax.psum_scatter(x, "shard", scatter_dimension=0, tiled=True)[0]
    late_grad, late_mixed, late_cot, norm_sums = step((hidden_grad, mixed_grad, cot_rows, norm_sums))
    mixed_sums = jnp.sum(late_mixed, axis=0, dtype=f32)
    norm_sums = jnp.swapaxes(norm_sums[:2].reshape(2, S, height), 0, 1).reshape(S, -1)
    riders = jnp.concatenate([norm_sums, jnp.broadcast_to(mixed_sums, (S, 3 * mix_own))], axis=1)
    riding = riders.shape[1]
    riders = jnp.pad(riders, ((0, 0), (0, -riding % (24 * mix_own))))
    riders = twofold(riders.reshape(S, -1, 3 * mix_own), 1)
    column_sums = jnp.concatenate(
        [
            jnp.sum(late_grad, axis=0, dtype=f32),
            pick(jnp.sum(late_cot, axis=0, dtype=f32).reshape(S, height), s, 0),
        ]
    )
    riders, column_sums = tie((riders, column_sums))
    step(None, riders, column_sums)
    mixed_own, mixed_got = second_sum(mixed_own, mixed_got)
    fc1_part, fc2_came = step((fc1_part, fc2_came))
    fc1_part = tie(jnp.swapaxes(fc1_part, 0, 1).reshape(part, S * ff_own))
    step(None, fc1_part)
    fc1_came = net.gather(fc1_part)
    if net.square:
        fc2_last = net.move(step(fc2_came), dc=1)
        fc2_mine, fc2_other = (fc2_part, fc2_came), (fc2_other, fc2_last)
    else:
        fc2_mine, fc2_other = (fc2_part, fc2_part), (fc2_other, fc2_other)
    branch_acts = add_in_order(*step((branch, branch_came)), back_planes.astype(jnp.int32))
    back_acts = add_in_order(
        *step(tie((back, back_came), branch_acts)), back_planes.astype(jnp.int32)
    )
    mark += [branch_acts, back_acts]
    fc1_part, fc1_came = second_gather(fc1_part, fc1_came)
    branch_sum, back_sum = scatter(branch_acts), scatter(back_acts)
    mixed_part = last_sum(mixed_own, mixed_got)
    out_part = mixed_part[:, :, 3 * mix_own :]
    mixed_part = tie(jnp.concatenate([mixed_part[:, :, : 3 * mix_own], riders], axis=1))
    step(None, mixed_part)
    mixed_part = swap(mixed_part)
    fc2_own = place_rows(net, *step((fc2_mine, fc2_other)), factor)
    step(None, fc2_own)
    fc1_other = net.move(step(fc1_part), dc=1)
    if net.square:
        fc1_came = step(fc1_came)
        mark += [fc1_came]
    mixed_part = step(mixed_part)
    riders = mixed_part[:, part:].astype(f32)
    mixed_part = jnp.concatenate([mixed_part[:, :part], out_part], axis=2)
    mixed_part = tie(jnp.swapaxes(mixed_part, 0, 1).reshape(part, S * 4 * mix_own))
    step(None, mixed_part)
    mixed_first, mixed_second = net.gather(mixed_part), net.gather_more(mixed_part)
    mixed_other = net.move(mixed_part, dc=1)
    if net.square:
        fc1_last = net.move(step(fc1_came), dc=1)
        fc1_mine, fc1_other = (fc1_part, fc1_came), (fc1_other, fc1_last)
    else:
        fc1_mine, fc1_other = (fc1_part, fc1_part), (fc1_other, fc1_other)
    count = riders.shape[1] // 2
    riders = step(riders)
    riders = (riders[:, :count] + riders[:, count:]).reshape(S, -1)[:, :riding]
    sums = jnp.concatenate(
        [
            jnp.sum(riders[:, : 2 * height], axis=0),
            column_sums[:ff_own],
            riders[:, 2 * height :].reshape(-1),
            column_sums[ff_own:],
        ]
    )
    sums = tie(sums)
    step(None, sums)
    sums = net.plane_sum(sums, 0)
    if net.square:
        fc1_own = place_columns(net, *step((fc1_mine, fc1_other)), factor)
        step(None, fc1_own)
        own, other = step((mixed_part[None], mixed_other[None]))
        placed = tie(place_mixed(net, own, other, 0, factor))
        step(None, placed)
        mixed_first, sums = tie(step((mixed_first, sums)))
        step(None, mixed_first)
        mixed_last = net.gather_more(mixed_first)
        mixed_second = tie(step(mixed_second))
        step(None, mixed_second)
        first_other, second_other = net.move(mixed_first, dc=1), net.move(mixed_second, dc=1)
        own, other = step((mixed_first[None], second_other[None]))
        placed = tie(place_mixed(net, own, other, 1, factor, placed))
        step(None, placed)
        own, other = step((mixed_second[None], first_other[None]))
        placed = tie(place_mixed(net, own, other, 2, factor, placed))
        step(None, placed)
        sums = net.plane_sum(tie(step(sums)), 1)
        mixed_last = tie(step(mixed_last))
        sums_came = net.move(tie(sums, mixed_last), dc=1)
        last_other = net.move(mixed_last, dc=1)
        placed = place_mixed(net, mixed_last[None], last_other[None], 3, factor, placed)
    else:
        mixed_near = lax.all_gather(mixed_part, "dp", axis_index_groups=net.groups())
        fc1_own = place_columns(net, *step((fc1_mine, fc1_other)), factor)
        sums = net.plane_sum(sums, 1)
        sums_came = net.move(sums, dc=1)
        placed = place_mixed(net, mixed_near, net.move(mixed_near, dc=1), 0, factor)
    qkv_own, out_own = placed
    if out_own.ndim == 4:
        out_own = jnp.transpose(out_own, (2, 0, 1, 3)).reshape(height, width)

    own_inputs = own_tokens.astype(f32)
    output = (own_inputs + branch_sum.astype(f32) + (out_bias + fc2_bias)).astype(bf16)
    normed = (own_inputs - mean[:rows, :1]) * inverse[:rows, :1]
    scaled = back_sum.astype(f32) * gain_full
    input_grad = own_cot.astype(f32) + inverse[:rows, :1] * (
        scaled
        - jnp.mean(scaled, axis=1, keepdims=True)
        - normed * jnp.mean(scaled * normed, axis=1, keepdims=True)
    )

    gain_own = (sums[:height] + sums_came[:height]) * factor
    shift_own = (sums[height : 2 * height] + sums_came[height : 2 * height]) * factor
    bias_own = sums[-height:] * factor
    pairs = jnp.where(c == 0, jnp.stack([sums, sums_came]), jnp.stack([sums_came, sums]))
    pairs = pairs[:, 2 * height : -height]
    fc1_bias_own = pairs[:, :ff_own].reshape(-1) * factor
    mixed_sums = jnp.transpose(pairs[:, ff_own:].reshape(CORES, S, 3, mix_own), (2, 1, 0, 3))
    qkv_bias_own = pick(mixed_sums.reshape(S, -1), s, 0) * factor
    return (
        output.reshape(tokens.shape),
        input_grad.reshape(tokens.shape),
        gain_own,
        shift_own,
        qkv_own,
        qkv_bias_own,
        out_own,
        bias_own,
        fc1_own,
        fc1_bias_own,
        fc2_own,
        bias_own,
    )


def solution(mesh):
    return jax.shard_map(
        local,
        mesh=mesh,
        in_specs=(
            P(("dp", "shard"), None, None),
            P(("dp", "shard"), None),
            P("shard"),
            P("shard"),
            P("shard", None),
            P("shard"),
            P("shard", None),
            P("shard"),
            P("shard", None),
            P("shard"),
            P("shard", None),
            P("shard"),
            P(("dp", "shard"), None, None),
        ),
        out_specs=(
            P(("dp", "shard"), None, None),
            P(("dp", "shard"), None, None),
            P("shard"),
            P("shard"),
            P("shard", None),
            P("shard"),
            P("shard", None),
            P("shard"),
            P("shard", None),
            P("shard"),
            P("shard", None),
            P("shard"),
        ),
        check_vma=False,
    )
```

```python
import math

import jax
import jax.numpy as jnp
from jax import lax
from jax.experimental import pallas as pl
from jax.experimental.pallas import tpu as pltpu
from jax.experimental.layout import Layout, with_layout_constraint
from jax.sharding import PartitionSpec as P

HEADS = 32
HEAD_DIM = 64
ROT = 32
CORES = 2
LANES = 128

epsilon = 1e-05
masked_value = -1e30
AXES = ("dp", "shard")
f32 = jnp.float32
bf16 = jnp.bfloat16
VMEM = 48 * 1024 * 1024


def rotary_tables(segments):
    seqs, length = segments.shape
    positions = jnp.broadcast_to(jnp.arange(length, dtype=jnp.int32), segments.shape)
    change = jnp.concatenate(
        [jnp.ones((seqs, 1), dtype=bool), segments[:, 1:] != segments[:, :-1]], axis=1
    )
    run_start = lax.cummax(jnp.where(change, positions, 0), axis=1)
    distance = (positions - run_start).astype(f32).reshape(-1, 1)
    lane = jnp.arange(LANES, dtype=jnp.int32) % HEAD_DIM
    half = ROT // 2
    frequency = jnp.exp((lane % half).astype(f32) * (-2.0 * math.log(10000.0) / ROT))
    angles = distance * frequency[None, :]
    sines = jnp.sin(angles)
    cos_table = jnp.where(lane < ROT, jnp.cos(angles), 1.0)
    low_table = jnp.where(lane < half, -sines, 0.0)
    high_table = jnp.where((lane >= half) & (lane < ROT), sines, 0.0)
    starts = jnp.broadcast_to(run_start.reshape(-1, 1), (seqs * length, LANES))
    return starts, cos_table, low_table, high_table


def attention_kernel(
    starts_ref, cos_ref, low_ref, high_ref, mixed_ref, outer_ref, context_ref, grad_ref
):
    length, width = outer_ref.shape
    half = ROT // 2
    scale = HEAD_DIM ** (-0.5)

    def wide(table):
        return jnp.concatenate([table[...]] * (width // LANES), axis=1)

    cos_table, low_table, high_table = wide(cos_ref), wide(low_ref), wide(high_ref)

    def rotate(v, sign):
        turned = pltpu.roll(v, width - half, 1) * low_table + pltpu.roll(v, half, 1) * high_table
        return v * cos_table + sign * turned

    queries = rotate(mixed_ref[:, :width], 1.0).astype(bf16)
    key_rows = rotate(mixed_ref[:, width : 2 * width], 1.0).astype(bf16)
    values = mixed_ref[:, 2 * width :].astype(bf16)
    outer = outer_ref[...]
    row = lax.broadcasted_iota(jnp.int32, (length, length), 0)
    column = lax.broadcasted_iota(jnp.int32, (length, length), 1)
    allowed = (column <= row) & (column >= starts_ref[...])
    spans = [slice(h * HEAD_DIM, (h + 1) * HEAD_DIM) for h in range(width // HEAD_DIM)]
    block = lambda x, h: x[h * length : (h + 1) * length]
    heads = range(len(spans))
    allowed = jnp.concatenate([allowed] * len(spans), axis=0)
    scores = jnp.concatenate([dot(queries[:, p], key_rows[:, p], ((1,), (1,))) for p in spans], axis=0)
    scores = jnp.where(allowed, scores * scale, masked_value)
    weights = jnp.exp(scores - jnp.max(scores, axis=1, keepdims=True))
    probs = weights / jnp.sum(weights, axis=1, keepdims=True)
    low = probs.astype(bf16)
    prob_grad = jnp.concatenate([dot(outer[:, p], values[:, p], ((1,), (1,))) for p in spans], axis=0)
    inner = jnp.sum(prob_grad * probs, axis=1, keepdims=True)
    score_grad = (probs * (prob_grad - inner)).astype(bf16)
    context = [dot(block(low, h), values[:, spans[h]], ((1,), (0,))) for h in heads]
    value_grad = [dot(block(low, h), outer[:, spans[h]], ((0,), (0,))) for h in heads]
    query_grad = [dot(block(score_grad, h), key_rows[:, spans[h]], ((1,), (0,))) for h in heads]
    key_grad = [dot(block(score_grad, h), queries[:, spans[h]], ((0,), (0,))) for h in heads]
    side = lambda x: jnp.concatenate(x, axis=1)
    context_ref[...] = side(context).astype(bf16)
    grad_ref[:, :width] = rotate(side(query_grad) * scale, -1.0).astype(bf16)
    grad_ref[:, width : 2 * width] = rotate(side(key_grad) * scale, -1.0).astype(bf16)
    grad_ref[:, 2 * width :] = side(value_grad).astype(bf16)


def attention(tables, mixed, outer, length):
    rows, width = outer.shape
    wide = lambda columns: pl.BlockSpec((length, columns), lambda i: (i, 0))
    return pl.pallas_call(
        attention_kernel,
        grid=(rows // length,),
        in_specs=[wide(LANES)] * 4 + [wide(3 * width), wide(width)],
        out_specs=[wide(width), wide(3 * width)],
        out_shape=[
            jax.ShapeDtypeStruct((rows, width), bf16),
            jax.ShapeDtypeStruct((rows, 3 * width), bf16),
        ],
        cost_estimate=pl.CostEstimate(flops=2 * 10**9, bytes_accessed=0, transcendentals=0),
        compiler_params=pltpu.CompilerParams(vmem_limit_bytes=VMEM),
    )(*tables, mixed, outer)


def call(kernel, grid, in_specs, out_specs, out_shape, scalars=0, us=0, **more):
    return pl.pallas_call(
        kernel,
        grid_spec=pltpu.PrefetchScalarGridSpec(
            num_scalar_prefetch=scalars, grid=grid, in_specs=in_specs, out_specs=out_specs
        ),
        out_shape=out_shape,
        cost_estimate=pl.CostEstimate(flops=us * 10**9 // 6, bytes_accessed=0, transcendentals=0),
        compiler_params=pltpu.CompilerParams(vmem_limit_bytes=VMEM),
        **more,
    )


def dot(a, b, dims):
    return lax.dot_general(a, b, (dims, ((), ())), preferred_element_type=f32)


def pack(w_fc1, w_qkv, row, core, planes, part, own, piece):
    third = w_qkv.shape[1] // 3 // piece
    cols = own + 3 * piece
    spots = jnp.stack([row, core]).astype(jnp.int32)

    def kernel(spots_ref, fc1_ref, q_ref, k_ref, v_ref, out_ref):
        out_ref[:, :own] = fc1_ref[...]
        for i, ref in enumerate((q_ref, k_ref, v_ref)):
            out_ref[:, own + i * piece : own + (i + 1) * piece] = ref[...]

    cut = lambda i: pl.BlockSpec(
        (part, piece), lambda p, spots: (spots[0], i * third + p * CORES + spots[1])
    )
    return call(
        kernel,
        (planes,),
        [
            pl.BlockSpec((part, own), lambda p, spots: (spots[0], p * CORES + spots[1])),
            cut(0),
            cut(1),
            cut(2),
        ],
        pl.BlockSpec((None, part, cols), lambda p, spots: (p, 0, 0)),
        jax.ShapeDtypeStruct((planes, part, cols), bf16),
        scalars=1,
    )(spots, w_fc1, w_qkv, w_qkv, w_qkv)


def assemble(w_fc1, w_qkv, arrays, order, spots, own, piece, blocks, before=None):
    _, others, rows, cols = arrays[0].shape
    planes = others + 1
    height = w_fc1.shape[0]
    third = w_qkv.shape[1] // 3 // piece

    def kernel(order_ref, spots_ref, fc1_ref, q_ref, k_ref, v_ref, *refs):
        fc1_out, qkv_out = refs[-2:]
        here = spots_ref[0]
        fc1_out[here] = fc1_ref[...]
        for i, ref in enumerate((q_ref, k_ref, v_ref)):
            qkv_out[here, :, i * piece : (i + 1) * piece] = ref[...]
        places = [(ref, m) for ref in refs[: len(arrays)] for m in range(ref.shape[0])]
        for n, (ref, m) in enumerate(places):

            @pl.when(pl.program_id(0) == n)
            def _(ref=ref, m=m):
                for k in range(1, planes):
                    there = spots_ref[k]
                    fc1_out[there] = ref[m, k - 1, :, :own]
                    qkv_out[there] = ref[m, k - 1, :, own:]

    cut = lambda i: pl.BlockSpec(
        (None, rows, piece), lambda n, order, spots: (order[n], 0, i * third + spots[planes])
    )
    result = lambda size: pl.BlockSpec(
        (planes, None, rows, size), lambda n, order, spots: (0, order[n], 0, 0)
    )
    more = {}
    if before is not None:
        first = 6 + len(arrays)
        more["input_output_aliases"] = {first: 0, first + 1: 1}
    return call(
        kernel,
        (sum(x.shape[0] for x in arrays),),
        [
            pl.BlockSpec((None, rows, own), lambda n, order, spots: (order[n], 0, spots[planes])),
            cut(0),
            cut(1),
            cut(2),
        ]
        + [pl.BlockSpec(x.shape, lambda n, order, spots: (0, 0, 0, 0)) for x in arrays]
        + [pl.BlockSpec(memory_space=pl.ANY)] * (0 if before is None else 2),
        [result(own), result(3 * piece)],
        [
            jax.ShapeDtypeStruct((planes, blocks, rows, own), bf16),
            jax.ShapeDtypeStruct((planes, blocks, rows, 3 * piece), bf16),
        ],
        scalars=2,
        **more,
    )(
        order,
        spots,
        w_fc1.reshape(blocks, rows, -1),
        *[w_qkv.reshape(blocks, rows, -1)] * 3,
        *arrays,
        *(before or ()),
    )


def norm(arrays, places, gain, shift, blocks, before=None):
    rows, width = arrays[0].shape[0] // 2, arrays[0].shape[1]

    def kernel(places_ref, gain_ref, shift_ref, *refs):
        out_ref, tokens_ref, cot_ref, mean_ref, inverse_ref = refs[-5:]
        for n in range(len(arrays)):

            @pl.when(pl.program_id(0) == n)
            def _(ref=refs[n]):
                tokens_ref[...] = ref[:rows]
                cot_ref[...] = ref[rows:]
                x = ref[:rows].astype(f32)
                mean = jnp.mean(x, axis=1, keepdims=True)
                centred = x - mean
                inverse = lax.rsqrt(jnp.mean(centred * centred, axis=1, keepdims=True) + epsilon)
                out_ref[...] = (centred * inverse * gain_ref[...] + shift_ref[...]).astype(bf16)
                mean_ref[...] = jnp.broadcast_to(mean, mean_ref.shape)
                inverse_ref[...] = jnp.broadcast_to(inverse, inverse_ref.shape)

    line = pl.BlockSpec((1, width), lambda i, places: (0, 0))
    wide = pl.BlockSpec((rows, width), lambda i, places: (places[i], 0))
    slim = pl.BlockSpec((rows, LANES), lambda i, places: (places[i], 0))
    more = {}
    if before is not None:
        more["input_output_aliases"] = {3 + len(arrays) + i: i for i in range(5)}
    return call(
        kernel,
        (len(arrays),),
        [line, line]
        + [pl.BlockSpec(x.shape, lambda i, places: (0, 0)) for x in arrays]
        + [pl.BlockSpec(memory_space=pl.ANY)] * (0 if before is None else 5),
        [wide, wide, wide, slim, slim],
        [jax.ShapeDtypeStruct((blocks * rows, width), bf16)] * 3
        + [jax.ShapeDtypeStruct((blocks * rows, LANES), f32)] * 2,
        scalars=1,
        **more,
    )(
        jnp.asarray(places, jnp.int32),
        gain.reshape(1, width),
        shift.reshape(1, width),
        *arrays,
        *(before or ()),
    )


def join(*lists):
    shape = lists[0][0].shape[1:]
    spans, arrays, total = [], [], 0
    for some in lists:
        start = total
        for x in some:
            arrays.append((total, x))
            total += x.shape[0]
        spans.append((start, total - start))

    def kernel(*refs):
        here = pl.program_id(0)
        for n, (start, x) in enumerate(arrays):
            for out, (first, count) in zip(refs[len(arrays) :], spans):
                if first <= start < first + count:

                    @pl.when((here >= start) & (here < start + x.shape[0]))
                    def _(ref=refs[n], out=out):
                        out[...] = ref[...]

    def spec(first, count):
        return pl.BlockSpec(
            (None,) + shape,
            lambda i: (jnp.clip(i - first, 0, count - 1),) + (0,) * len(shape),
        )

    results = call(
        kernel,
        (total,),
        [spec(start, x.shape[0]) for start, x in arrays],
        [spec(*span) for span in spans],
        [jax.ShapeDtypeStruct((count,) + shape, arrays[0][1].dtype) for _, count in spans],
        us=3,
    )(*[x for _, x in arrays])
    return results if len(lists) > 1 else results[0]


def add_in_order(mine, came, order):
    count = order.shape[0]
    rows, width = mine.shape[0] // count, mine.shape[1]

    def kernel(order_ref, mine_ref, came_ref, out_ref):
        out_ref[...] = (mine_ref[...] + came_ref[...].astype(f32)).astype(bf16)

    block = pl.BlockSpec((rows, width), lambda i, order: (i, 0))
    return call(
        kernel,
        (count,),
        [block, block],
        pl.BlockSpec((None, rows, width), lambda i, order: (order[i], 0, 0)),
        jax.ShapeDtypeStruct((count, rows, width), bf16),
        scalars=1,
    )(order, mine, came)


def branches(context, out_rows, active, fc2_rows):
    total, width = context.shape[0], out_rows.shape[1]
    half, block = total // 2, 256

    def kernel(context_ref, out_ref, active_ref, fc2_ref, mine_ref, other_ref):
        y = dot(context_ref[...], out_ref[...], ((1,), (0,)))
        y = y + dot(active_ref[...], fc2_ref[...], ((1,), (0,)))
        mine_ref[...] = y[:half]
        other_ref[...] = y[half:].astype(bf16)

    whole = lambda x: pl.BlockSpec(x.shape, lambda i: (0, 0))
    part = lambda rows: pl.BlockSpec((rows, block), lambda i: (0, i))
    return call(
        kernel,
        (width // block,),
        [whole(context), part(out_rows.shape[0]), whole(active), part(fc2_rows.shape[0])],
        [part(half), part(half)],
        [jax.ShapeDtypeStruct((half, width), f32), jax.ShapeDtypeStruct((half, width), bf16)],
        us=10,
    )(context, out_rows, active, fc2_rows)


def backs(hidden_grad, fc1_cols, mixed_grad, qkv_cols, tokens, mean, inverse):
    total, width = mean.shape[0], fc1_cols.shape[0]
    half, block = total // 2, 256

    def kernel(
        hidden_ref, fc1_ref, mixed_ref, qkv_ref, tokens_ref, mean_ref, inverse_ref,
        first_ref, second_ref, sums_ref,
    ):
        y = dot(hidden_ref[...], fc1_ref[...], ((1,), (1,)))
        y = y + dot(mixed_ref[...], qkv_ref[...], ((1,), (1,)))
        first_ref[...] = y[:half]
        second_ref[...] = y[half:].astype(bf16)
        normed = (tokens_ref[...].astype(f32) - mean_ref[:, :1]) * inverse_ref[:, :1]
        sums_ref[0:1, :] = jnp.sum(y * normed, axis=0, keepdims=True)
        sums_ref[1:2, :] = jnp.sum(y, axis=0, keepdims=True)
        sums_ref[2:8, :] = jnp.zeros((6, block), f32)

    whole = lambda x: pl.BlockSpec(x.shape, lambda i: (0, 0))
    part = lambda rows: pl.BlockSpec((rows, block), lambda i: (0, i))
    rhs = lambda x: pl.BlockSpec((block, x.shape[1]), lambda i: (i, 0))
    return call(
        kernel,
        (width // block,),
        [
            whole(hidden_grad),
            rhs(fc1_cols),
            whole(mixed_grad),
            rhs(qkv_cols),
            part(total),
            whole(mean),
            whole(inverse),
        ],
        [part(half), part(half), part(8)],
        [
            jax.ShapeDtypeStruct((half, width), f32),
            jax.ShapeDtypeStruct((half, width), bf16),
            jax.ShapeDtypeStruct((8, width), f32),
        ],
        us=14,
    )(hidden_grad, fc1_cols, mixed_grad, qkv_cols, tokens, mean, inverse)


def place_columns(net, mine, other, factor):
    J, planes = net.J, net.S
    _, rows, columns = mine[0].shape
    piece = columns // planes
    spots = jnp.concatenate([net.order(), jnp.stack([net.c, 1 - net.c])]).astype(jnp.int32)
    high = rows // 2

    def kernel(spots_ref, m0_ref, m1_ref, o0_ref, o1_ref, out_ref):
        here = pl.program_id(0)
        for e, (place, refs) in enumerate(
            ((net.mine, (m0_ref, m1_ref)), (net.theirs, (o0_ref, o1_ref)))
        ):
            last, _ = place(here)
            for ref, chosen in zip(refs, (jnp.logical_not(last), last)):

                @pl.when(chosen)
                def _(e=e, ref=ref):
                    for k in range(planes):
                        column = (k * CORES + spots_ref[J + e]) * piece
                        out_ref[:, pl.ds(pl.multiple_of(column, LANES), piece)] = (
                            ref[:, k * piece : (k + 1) * piece].astype(f32) * factor
                        )

    return call(
        kernel,
        (J, 2),
        [
            pl.BlockSpec(
                (None, high, columns), lambda i, h, spots, place=place, n=n: (place(i)[1][n], h, 0)
            )
            for place in (net.mine, net.theirs)
            for n in range(2)
        ],
        pl.BlockSpec((high, 2 * columns), lambda i, h, spots: (spots[i] * 2 + h, 0)),
        jax.ShapeDtypeStruct((J * rows, 2 * columns), f32),
        scalars=1,
    )(spots, *mine, *other)


def place_mixed(net, mine, other, start, factor, before=None):
    J, planes = net.J, net.S
    count, part, columns = mine.shape
    piece = columns // planes // 4
    width = planes * CORES * piece
    chips = net.order()[start : start + count]
    spots = jnp.concatenate([chips, jnp.stack([net.c, 1 - net.c])]).astype(jnp.int32)

    def kernel(spots_ref, mine_ref, other_ref, *refs):
        qkv_ref, out_ref = refs[-2:]
        for e, ref in enumerate((mine_ref, other_ref)):
            core = spots_ref[count + e]
            for k in range(planes):

                @pl.when(pl.program_id(1) == k)
                def _(k=k, core=core, ref=ref):
                    for i in range(3):
                        start = (4 * k + i) * piece
                        column = ((i * planes + k) * CORES + core) * piece
                        qkv_ref[:, pl.ds(pl.multiple_of(column, LANES), piece)] = (
                            ref[:, start : start + piece].astype(f32) * factor
                        )
                    block = ref[:, (4 * k + 3) * piece : (4 * k + 4) * piece].astype(f32)
                    out_ref[pl.ds(pl.multiple_of(core * piece, LANES), piece), :] = (
                        block * factor
                    ).T

    if part % LANES == 0:
        out_shape = (CORES * piece, planes * J * part)
        out_spec = pl.BlockSpec((CORES * piece, part), lambda i, k, spots: (0, k * J + spots[i]))
    else:
        out_shape = (planes, J, CORES * piece, part)
        out_spec = pl.BlockSpec(
            (None, None, CORES * piece, part), lambda i, k, spots: (k, spots[i], 0, 0)
        )
    before = before or ()
    return call(
        kernel,
        (count, planes),
        [
            pl.BlockSpec((None, part, columns), lambda i, k, spots: (i, 0, 0)),
            pl.BlockSpec((None, part, columns), lambda i, k, spots: (i, 0, 0)),
        ]
        + [pl.BlockSpec(memory_space=pl.ANY)] * len(before),
        [pl.BlockSpec((part, 3 * width), lambda i, k, spots: (spots[i], 0)), out_spec],
        [
            jax.ShapeDtypeStruct((width // planes, 3 * width), f32),
            jax.ShapeDtypeStruct(out_shape, f32),
        ],
        scalars=1,
        input_output_aliases={3 + i: i for i in range(len(before))},
    )(spots, mine, other, *before)


def place_rows(net, mine, other, factor):
    J = net.J
    _, rows, columns = mine[0].shape
    spots = jnp.concatenate([net.c * J + net.order(), (1 - net.c) * J + net.order(other=True)])
    arrays = (*mine, *other) if net.square else (mine[0], other[0])
    starts = [sum(x.shape[0] for x in arrays[:n]) for n in range(len(arrays))]

    def kernel(spots_ref, *refs):
        here = pl.program_id(0)
        for start, x, ref in zip(starts, arrays, refs):

            @pl.when((here >= start) & (here < start + x.shape[0]))
            def _(ref=ref):
                refs[-1][...] = ref[...].astype(f32) * factor

    def spec(start, count):
        return pl.BlockSpec(
            (None, rows, columns), lambda i, spots: (jnp.clip(i - start, 0, count - 1), 0, 0)
        )

    return call(
        kernel,
        (2 * J,),
        [spec(start, x.shape[0]) for start, x in zip(starts, arrays)],
        pl.BlockSpec((rows, columns), lambda i, spots: (spots[i], 0)),
        jax.ShapeDtypeStruct((2 * J * rows, columns), f32),
        scalars=1,
    )(spots.astype(jnp.int32), *arrays)


def tie(x, *after):
    return lax.optimization_barrier((x, after))[0]


class Links:
    def __init__(self, planes, replicas):
        self.S = planes
        self.J = replicas // CORES
        self.square = self.J == 4
        dp = lax.axis_index("dp")
        self.s = lax.axis_index("shard")
        self.c = dp % CORES
        self.j = dp // CORES
        self.first = jnp.where(self.c == 0, 2, 1)

    def move(self, x, ds=0, dc=0, steps=None):
        pairs = []
        for j in range(self.J):
            for c in range(CORES):
                for s in range(self.S):
                    turn = 0 if steps is None else (2, 1)[(c + steps) % 2]
                    to = ((j ^ turn) * CORES + (c + dc) % CORES) * self.S + (s + ds) % self.S
                    pairs.append(((j * CORES + c) * self.S + s, to))
        return lax.ppermute(x, AXES, pairs)

    def groups(self):
        return [[j * CORES + c for j in range(self.J)] for c in range(CORES)]

    def order(self, other=False):
        if not self.square:
            return jnp.arange(self.J)
        turn = 3 - self.first if other else self.first
        return jnp.stack([self.j, self.j ^ turn, self.j ^ 3 ^ turn, self.j ^ 3])

    def mine(self, i):
        return (i >= 2, (jnp.minimum(i, 1), jnp.maximum(i - 2, 0))) if self.square else (i < 0, (i, 0))

    def theirs(self, i):
        return (i % 2 == 1, (i // 2, i // 2)) if self.square else (i < 0, (i, 0))

    def gather(self, x):
        return self.move(x, steps=0) if self.square else None

    def gather_more(self, stack):
        return self.move(stack, steps=1) if self.square else None

    def spread(self, x):
        if not self.square:
            return x
        other = self.j ^ self.first
        return jnp.stack([pick(x, other, 1), pick(x, other ^ 3 ^ self.first, 1)])

    def spread_sum(self, x, got):
        if not self.square:
            return x, x
        mine = pick(x, self.j, 1), pick(x, self.j ^ 3 ^ self.first, 1)
        return [(m.astype(f32) + g.astype(f32)).astype(bf16) for m, g in zip(mine, got)]

    def spread_last(self, own, got):
        if not self.square:
            return lax.psum_scatter(
                own.astype(f32),
                "dp",
                scatter_dimension=1,
                axis_index_groups=self.groups(),
                tiled=False,
            ).astype(bf16)
        return (own.astype(f32) + got.astype(f32)).astype(bf16)

    def plane_sum(self, x, step):
        if not self.square:
            return lax.psum(x, "dp", axis_index_groups=self.groups()) if step else x
        return x + self.move(x, steps=step)


def swap(x, after=()):
    return lax.all_to_all(tie(x, *after), "shard", 0, 0, tiled=True)


def twofold(x, axis):
    high = lax.reduce_precision(x, 8, 7)
    return jnp.concatenate([high.astype(bf16), (x - high).astype(bf16)], axis=axis)


def as_rows(vector, width, multiple):
    count = -(-vector.shape[0] // (width * multiple)) * multiple
    return jnp.pad(vector, (0, count * width - vector.shape[0])).reshape(count, width)


def pick(x, index, axis):
    return lax.dynamic_index_in_dim(x, index, axis, keepdims=False)


def in_order(held, here):
    size = len(held)
    backwards = jnp.stack(held[::-1])
    return lax.dynamic_slice_in_dim(
        jnp.concatenate([backwards, backwards]), size - 1 - here, size, 0
    )


def local(
    tokens,
    segments,
    ln_gain,
    ln_bias,
    w_qkv,
    b_qkv,
    w_out,
    b_out,
    w_fc1,
    b_fc1,
    w_fc2,
    b_fc2,
    cotangent,
):
    planes = lax.axis_size("shard")
    replicas = lax.axis_size("dp")
    net = Links(planes, replicas)
    S, J, c, j, s = net.S, net.J, net.c, net.j, net.s
    seqs, length, width = tokens.shape
    rows = seqs * length
    ff = w_fc1.shape[1]
    ff_own = ff // (S * CORES)
    mix_own = width // (S * CORES)
    height = width // S
    part = height // J
    total = S * CORES * rows
    back_planes = (s - jnp.arange(S)) % S
    factor = 1.0 / math.sqrt(rows * planes * replicas)

    own_tokens = tokens.reshape(rows, width)
    own_cot = cotangent.reshape(rows, width)
    hops = [jnp.concatenate([own_tokens, own_cot])]
    hops.append(net.move(hops[0], ds=1))

    vectors = [ln_gain, ln_bias, b_qkv, b_out, b_fc1, b_fc2, segments.reshape(-1).astype(bf16)]
    small = jnp.concatenate(vectors)
    size = small.shape[0]
    held = [small] + [net.move(small, ds=k) for k in range(1, S)]

    got = swap(pack(w_fc1, w_qkv, j, c, S, part, ff_own, mix_own))
    others = [net.move(tie(hops[0], hops[1], held), dc=1), net.move(hops[1], dc=1)]
    fc2_rows = lax.dynamic_slice_in_dim(w_fc2, c * ff_own, ff_own, 0)
    out_rows = lax.dynamic_slice_in_dim(w_out, c * mix_own, mix_own, 0)
    marks = jnp.stack([v[size - rows :] for v in held])
    small_all = in_order(held, s)
    whole = []
    start = 0
    for vector in vectors[:-1]:
        whole.append(small_all[:, start : start + vector.shape[0]].reshape(-1).astype(f32))
        start += vector.shape[0]
    gain_full, shift_full, qkv_bias, out_bias, fc1_bias, fc2_bias = whole
    fc1_bias = lax.dynamic_slice_in_dim(fc1_bias, (s * CORES + c) * ff_own, ff_own, 0)
    qkv_bias = lax.dynamic_slice_in_dim(
        qkv_bias.reshape(3, width), (s * CORES + c) * mix_own, mix_own, 1
    ).reshape(-1)
    marks = jnp.stack([marks, net.move(tie(marks, hops[1], held), dc=1)])
    tables = rotary_tables(marks.reshape(-1, length).astype(jnp.int32))
    ready = tie((hops[1], others, fc2_rows, out_rows, tables, gain_full, fc1_bias, qkv_bias), hops[1])
    hop, others, fc2_rows, out_rows, tables, gain_full, fc1_bias, qkv_bias = ready

    got = tie(got, hop, others, fc2_rows, out_rows, tables, gain_full, fc1_bias, qkv_bias)
    block = jnp.concatenate([pick(got, back_planes[k], 0) for k in range(1, S)])[None]
    hops.append(net.move(tie(hop, got), ds=1))
    came = net.gather(block)
    if net.square:
        blocks = tie(join([block, came]))
    else:
        blocks = lax.all_gather(block[0], "dp", axis_index_groups=net.groups())
    came = net.gather_more(blocks)
    while len(hops) < S:
        hops.append(net.move(tie(hops[-1], blocks), ds=1))
        others.append(net.move(tie(hops[-2], blocks), dc=1))
    places = [e * S + k for k in range(S) for e in range(CORES)]
    early = [x for pair in zip(hops[: S - 1], others[: S - 1]) for x in pair]
    early = tie(early, blocks)
    normed_rows = norm(early, places[:-CORES], gain_full, shift_full, S * CORES)
    blocks = tie(blocks, normed_rows)
    spots_w = jnp.concatenate([back_planes, (s * CORES + c)[None]]).astype(jnp.int32)
    chips = net.order()
    weights = lambda x, order, *before: assemble(
        w_fc1,
        w_qkv,
        [x.reshape(-1, S - 1, part, x.shape[-1])],
        order.astype(jnp.int32),
        spots_w,
        ff_own,
        mix_own,
        J,
        *before,
    )
    weight_cols = weights(blocks, chips[: blocks.shape[0]])
    last = tie(hops[-1], weight_cols)
    other = net.move(last, dc=1)
    if net.square:
        weight_cols, came = tie((weight_cols, came), last)
        weight_cols = weights(came, chips[2:], weight_cols)
    last, other = tie((last, other), weight_cols)
    hidden_in, tok_rows, cot_rows, mean, inverse = norm(
        [last, other], places[-CORES:], gain_full, shift_full, S * CORES, normed_rows
    )
    fc1_cols = weight_cols[0].reshape(width, ff_own)
    qkv_cols = weight_cols[1].reshape(width, 3 * mix_own)

    hidden = jnp.dot(hidden_in, fc1_cols, preferred_element_type=f32) + fc1_bias
    active, gelu_back = jax.vjp(lambda v: jax.nn.gelu(v, approximate=True), hidden)
    active = active.astype(bf16)
    transposed = lambda x, y: jnp.einsum("td,te->de", x, y, preferred_element_type=f32).astype(bf16)
    fc2_term = transposed(active, cot_rows)

    mark = []

    def step(x, *made):
        nonlocal mark
        if not made:
            return tie(x, mark)
        mark = list(made)
        return x

    def first_sum(x):
        sent = tie(net.spread(x))
        step(None, sent)
        return x, net.gather(sent)

    def second_sum(x, got):
        x, got = step((x, got))
        own, sent = tie(net.spread_sum(x, got))
        step(None, own, sent)
        return own, net.gather_more(sent)

    def last_sum(own, got):
        part = tie(net.spread_last(*step((own, got))))
        step(None, part)
        return part

    def second_gather(part, came):
        part, came = step((part, came))
        if net.square:
            stack = join([part[None], came[None]])
        else:
            stack = lax.all_gather(part, "dp", axis_index_groups=net.groups())
        stack = tie(stack)
        step(None, stack)
        return stack, net.gather_more(stack)

    def to_other(x):
        return net.move(step(x), dc=1) if net.square else x

    fc2_own, fc2_got = first_sum(fc2_term.reshape(1, J, ff_own // J, width))
    late_cot = step(cot_rows)
    active_grad = jnp.einsum("td,fd->tf", late_cot, fc2_rows, preferred_element_type=f32)
    hidden_grad = gelu_back(active_grad)[0].astype(bf16)
    fc1_term = transposed(hidden_in, hidden_grad)
    fc1_own, fc1_got = first_sum(fc1_term.reshape(S, J, part, ff_own))
    fc2_own, fc2_got = second_sum(fc2_own, fc2_got)
    late_in, late_cot = step((hidden_in, cot_rows))
    mixed = jnp.dot(late_in, qkv_cols, preferred_element_type=f32) + qkv_bias
    context_grad = jnp.einsum("te,de->td", late_cot, out_rows, preferred_element_type=f32).astype(
        bf16
    )
    context, mixed_grad = attention(tables, mixed, context_grad, length)
    step(None, context, mixed_grad)
    fc1_own, fc1_got = second_sum(fc1_own, fc1_got)
    fc2_part = last_sum(fc2_own, fc2_got)[0]
    fc2_came = net.gather(fc2_part)
    late_in, late_cot, late_mixed, late_context = step((hidden_in, cot_rows, mixed_grad, context))
    mixed_term = with_layout_constraint(
        jnp.concatenate(
            [transposed(late_in, late_mixed), transposed(late_cot, late_context)], axis=1
        ),
        Layout((0, 1)),
    )
    mixed_own, mixed_got = first_sum(mixed_term.reshape(S, J, part, 4 * mix_own))
    fc1_part = last_sum(fc1_own, fc1_got)
    fc1_part = swap(fc1_part)
    fc2_part, fc2_came = second_gather(fc2_part, fc2_came)
    fc2_other = net.move(fc2_part, dc=1)
    late_context, late_active = step((context, active))
    branch, branch_other = branches(late_context, out_rows, late_active, fc2_rows)
    step(None, branch, branch_other)
    branch_came = net.move(branch_other, dc=1)
    late_mixed, late_grad = step((mixed_grad, hidden_grad))
    back, back_other, norm_sums = backs(
        late_grad, fc1_cols, late_mixed, qkv_cols, tok_rows, mean, inverse
    )
    step(None, back, back_other, norm_sums)
    back_came = net.move(back_other, dc=1)
    scatter = lambda x: lax.psum_scatter(x, "shard", scatter_dimension=0, tiled=True)[0]
    late_grad, late_mixed, late_cot, norm_sums = step((hidden_grad, mixed_grad, cot_rows, norm_sums))
    mixed_sums = jnp.sum(late_mixed, axis=0, dtype=f32)
    norm_sums = jnp.swapaxes(norm_sums[:2].reshape(2, S, height), 0, 1).reshape(S, -1)
    riders = jnp.concatenate([norm_sums, jnp.broadcast_to(mixed_sums, (S, 3 * mix_own))], axis=1)
    riding = riders.shape[1]
    riders = jnp.pad(riders, ((0, 0), (0, -riding % (24 * mix_own))))
    riders = twofold(riders.reshape(S, -1, 3 * mix_own), 1)
    column_sums = jnp.concatenate(
        [
            jnp.sum(late_grad, axis=0, dtype=f32),
            pick(jnp.sum(late_cot, axis=0, dtype=f32).reshape(S, height), s, 0),
        ]
    )
    riders, column_sums = tie((riders, column_sums))
    step(None, riders, column_sums)
    mixed_own, mixed_got = second_sum(mixed_own, mixed_got)
    fc1_part, fc2_came = step((fc1_part, fc2_came))
    fc1_part = tie(jnp.swapaxes(fc1_part, 0, 1).reshape(part, S * ff_own))
    step(None, fc1_part)
    fc1_came = net.gather(fc1_part)
    if net.square:
        fc2_last = net.move(step(fc2_came), dc=1)
        fc2_mine, fc2_other = (fc2_part, fc2_came), (fc2_other, fc2_last)
    else:
        fc2_mine, fc2_other = (fc2_part, fc2_part), (fc2_other, fc2_other)
    branch_acts = add_in_order(*step((branch, branch_came)), back_planes.astype(jnp.int32))
    back_acts = add_in_order(
        *step(tie((back, back_came), branch_acts)), back_planes.astype(jnp.int32)
    )
    mark += [branch_acts, back_acts]
    fc1_part, fc1_came = second_gather(fc1_part, fc1_came)
    branch_sum, back_sum = scatter(branch_acts), scatter(back_acts)
    mixed_part = last_sum(mixed_own, mixed_got)
    out_part = mixed_part[:, :, 3 * mix_own :]
    mixed_part = tie(jnp.concatenate([mixed_part[:, :, : 3 * mix_own], riders], axis=1))
    step(None, mixed_part)
    mixed_part = swap(mixed_part)
    fc2_own = place_rows(net, *step((fc2_mine, fc2_other)), factor)
    step(None, fc2_own)
    fc1_other = net.move(step(fc1_part), dc=1)
    if net.square:
        fc1_came = step(fc1_came)
        mark += [fc1_came]
    mixed_part = step(mixed_part)
    riders = mixed_part[:, part:].astype(f32)
    mixed_part = jnp.concatenate([mixed_part[:, :part], out_part], axis=2)
    mixed_part = tie(jnp.swapaxes(mixed_part, 0, 1).reshape(part, S * 4 * mix_own))
    step(None, mixed_part)
    mixed_first, mixed_second = net.gather(mixed_part), net.gather_more(mixed_part)
    mixed_other = net.move(mixed_part, dc=1)
    if net.square:
        fc1_last = net.move(step(fc1_came), dc=1)
        fc1_mine, fc1_other = (fc1_part, fc1_came), (fc1_other, fc1_last)
    else:
        fc1_mine, fc1_other = (fc1_part, fc1_part), (fc1_other, fc1_other)
    if net.square:
        fc1_own = place_columns(net, *step((fc1_mine, fc1_other)), factor)
        step(None, fc1_own)
        count = riders.shape[1] // 2
        riders = step(riders)
        riders = (riders[:, :count] + riders[:, count:]).reshape(S, -1)[:, :riding]
        sums = jnp.concatenate(
            [
                jnp.sum(riders[:, : 2 * height], axis=0),
                column_sums[:ff_own],
                riders[:, 2 * height :].reshape(-1),
                column_sums[ff_own:],
            ]
        )
        sums = tie(sums)
        step(None, sums)
        sums = net.plane_sum(sums, 0)
        own, other = step((mixed_part[None], mixed_other[None]))
        placed = tie(place_mixed(net, own, other, 0, factor))
        step(None, placed)
        mixed_first, sums = tie(step((mixed_first, sums)))
        step(None, mixed_first)
        mixed_last = net.gather_more(mixed_first)
        mixed_second = tie(step(mixed_second))
        step(None, mixed_second)
        first_other, second_other = net.move(mixed_first, dc=1), net.move(mixed_second, dc=1)
        own, other = step((mixed_first[None], second_other[None]))
        placed = tie(place_mixed(net, own, other, 1, factor, placed))
        step(None, placed)
        own, other = step((mixed_second[None], first_other[None]))
        placed = tie(place_mixed(net, own, other, 2, factor, placed))
        step(None, placed)
        sums = net.plane_sum(tie(step(sums)), 1)
        mixed_last = tie(step(mixed_last))
        sums_came = net.move(tie(sums, mixed_last), dc=1)
        last_other = net.move(mixed_last, dc=1)
        placed = place_mixed(net, mixed_last[None], last_other[None], 3, factor, placed)
    else:
        mixed_near = lax.all_gather(mixed_part, "dp", axis_index_groups=net.groups())
        count = riders.shape[1] // 2
        riders = step(riders)
        riders = (riders[:, :count] + riders[:, count:]).reshape(S, -1)[:, :riding]
        sums = jnp.concatenate(
            [
                jnp.sum(riders[:, : 2 * height], axis=0),
                column_sums[:ff_own],
                riders[:, 2 * height :].reshape(-1),
                column_sums[ff_own:],
            ]
        )
        sums = tie(sums)
        step(None, sums)
        sums = net.plane_sum(sums, 0)
        fc1_own = place_columns(net, *step((fc1_mine, fc1_other)), factor)
        sums = net.plane_sum(sums, 1)
        sums_came = net.move(sums, dc=1)
        placed = place_mixed(net, mixed_near, net.move(mixed_near, dc=1), 0, factor)
    qkv_own, out_own = placed
    if out_own.ndim == 4:
        out_own = jnp.transpose(out_own, (2, 0, 1, 3)).reshape(height, width)

    own_inputs = own_tokens.astype(f32)
    output = (own_inputs + branch_sum.astype(f32) + (out_bias + fc2_bias)).astype(bf16)
    normed = (own_inputs - mean[:rows, :1]) * inverse[:rows, :1]
    scaled = back_sum.astype(f32) * gain_full
    input_grad = own_cot.astype(f32) + inverse[:rows, :1] * (
        scaled
        - jnp.mean(scaled, axis=1, keepdims=True)
        - normed * jnp.mean(scaled * normed, axis=1, keepdims=True)
    )

    gain_own = (sums[:height] + sums_came[:height]) * factor
    shift_own = (sums[height : 2 * height] + sums_came[height : 2 * height]) * factor
    bias_own = sums[-height:] * factor
    pairs = jnp.where(c == 0, jnp.stack([sums, sums_came]), jnp.stack([sums_came, sums]))
    pairs = pairs[:, 2 * height : -height]
    fc1_bias_own = pairs[:, :ff_own].reshape(-1) * factor
    mixed_sums = jnp.transpose(pairs[:, ff_own:].reshape(CORES, S, 3, mix_own), (2, 1, 0, 3))
    qkv_bias_own = pick(mixed_sums.reshape(S, -1), s, 0) * factor
    return (
        output.reshape(tokens.shape),
        input_grad.reshape(tokens.shape),
        gain_own,
        shift_own,
        qkv_own,
        qkv_bias_own,
        out_own,
        bias_own,
        fc1_own,
        fc1_bias_own,
        fc2_own,
        bias_own,
    )


def solution(mesh):
    return jax.shard_map(
        local,
        mesh=mesh,
        in_specs=(
            P(("dp", "shard"), None, None),
            P(("dp", "shard"), None),
            P("shard"),
            P("shard"),
            P("shard", None),
            P("shard"),
            P("shard", None),
            P("shard"),
            P("shard", None),
            P("shard"),
            P("shard", None),
            P("shard"),
            P(("dp", "shard"), None, None),
        ),
        out_specs=(
            P(("dp", "shard"), None, None),
            P(("dp", "shard"), None, None),
            P("shard"),
            P("shard"),
            P("shard", None),
            P("shard"),
            P("shard", None),
            P("shard"),
            P("shard", None),
            P("shard"),
            P("shard", None),
            P("shard"),
        ),
        check_vma=False,
    )
```

```python
import math

import jax
import jax.numpy as jnp
from jax import lax
from jax.experimental import pallas as pl
from jax.experimental.pallas import tpu as pltpu
from jax.experimental.layout import Layout, with_layout_constraint
from jax.sharding import PartitionSpec as P

HEADS = 32
HEAD_DIM = 64
ROT = 32
CORES = 2
LANES = 128

epsilon = 1e-05
masked_value = -1e30
AXES = ("dp", "shard")
f32 = jnp.float32
bf16 = jnp.bfloat16
VMEM = 48 * 1024 * 1024


def rotary_tables(segments):
    seqs, length = segments.shape
    positions = jnp.broadcast_to(jnp.arange(length, dtype=jnp.int32), segments.shape)
    change = jnp.concatenate(
        [jnp.ones((seqs, 1), dtype=bool), segments[:, 1:] != segments[:, :-1]], axis=1
    )
    run_start = lax.cummax(jnp.where(change, positions, 0), axis=1)
    distance = (positions - run_start).astype(f32).reshape(-1, 1)
    lane = jnp.arange(LANES, dtype=jnp.int32) % HEAD_DIM
    half = ROT // 2
    frequency = jnp.exp((lane % half).astype(f32) * (-2.0 * math.log(10000.0) / ROT))
    angles = distance * frequency[None, :]
    sines = jnp.sin(angles)
    cos_table = jnp.where(lane < ROT, jnp.cos(angles), 1.0)
    low_table = jnp.where(lane < half, -sines, 0.0)
    high_table = jnp.where((lane >= half) & (lane < ROT), sines, 0.0)
    starts = jnp.broadcast_to(run_start.reshape(-1, 1), (seqs * length, LANES))
    return starts, cos_table, low_table, high_table


def attention_kernel(
    starts_ref, cos_ref, low_ref, high_ref, mixed_ref, outer_ref, context_ref, grad_ref
):
    length, width = outer_ref.shape
    half = ROT // 2
    scale = HEAD_DIM ** (-0.5)

    def wide(table):
        return jnp.concatenate([table[...]] * (width // LANES), axis=1)

    cos_table, low_table, high_table = wide(cos_ref), wide(low_ref), wide(high_ref)

    def rotate(v, sign):
        turned = pltpu.roll(v, width - half, 1) * low_table + pltpu.roll(v, half, 1) * high_table
        return v * cos_table + sign * turned

    queries = rotate(mixed_ref[:, :width], 1.0).astype(bf16)
    key_rows = rotate(mixed_ref[:, width : 2 * width], 1.0).astype(bf16)
    values = mixed_ref[:, 2 * width :].astype(bf16)
    outer = outer_ref[...]
    row = lax.broadcasted_iota(jnp.int32, (length, length), 0)
    column = lax.broadcasted_iota(jnp.int32, (length, length), 1)
    allowed = (column <= row) & (column >= starts_ref[...])
    spans = [slice(h * HEAD_DIM, (h + 1) * HEAD_DIM) for h in range(width // HEAD_DIM)]
    block = lambda x, h: x[h * length : (h + 1) * length]
    heads = range(len(spans))
    allowed = jnp.concatenate([allowed] * len(spans), axis=0)
    scores = jnp.concatenate([dot(queries[:, p], key_rows[:, p], ((1,), (1,))) for p in spans], axis=0)
    scores = jnp.where(allowed, scores * scale, masked_value)
    weights = jnp.exp(scores - jnp.max(scores, axis=1, keepdims=True))
    probs = weights / jnp.sum(weights, axis=1, keepdims=True)
    low = probs.astype(bf16)
    prob_grad = jnp.concatenate([dot(outer[:, p], values[:, p], ((1,), (1,))) for p in spans], axis=0)
    inner = jnp.sum(prob_grad * probs, axis=1, keepdims=True)
    score_grad = (probs * (prob_grad - inner)).astype(bf16)
    context = [dot(block(low, h), values[:, spans[h]], ((1,), (0,))) for h in heads]
    value_grad = [dot(block(low, h), outer[:, spans[h]], ((0,), (0,))) for h in heads]
    query_grad = [dot(block(score_grad, h), key_rows[:, spans[h]], ((1,), (0,))) for h in heads]
    key_grad = [dot(block(score_grad, h), queries[:, spans[h]], ((0,), (0,))) for h in heads]
    side = lambda x: jnp.concatenate(x, axis=1)
    context_ref[...] = side(context).astype(bf16)
    grad_ref[:, :width] = rotate(side(query_grad) * scale, -1.0).astype(bf16)
    grad_ref[:, width : 2 * width] = rotate(side(key_grad) * scale, -1.0).astype(bf16)
    grad_ref[:, 2 * width :] = side(value_grad).astype(bf16)


def attention(tables, mixed, outer, length):
    rows, width = outer.shape
    wide = lambda columns: pl.BlockSpec((length, columns), lambda i: (i, 0))
    return pl.pallas_call(
        attention_kernel,
        grid=(rows // length,),
        in_specs=[wide(LANES)] * 4 + [wide(3 * width), wide(width)],
        out_specs=[wide(width), wide(3 * width)],
        out_shape=[
            jax.ShapeDtypeStruct((rows, width), bf16),
            jax.ShapeDtypeStruct((rows, 3 * width), bf16),
        ],
        cost_estimate=pl.CostEstimate(flops=2 * 10**9, bytes_accessed=0, transcendentals=0),
        compiler_params=pltpu.CompilerParams(vmem_limit_bytes=VMEM),
    )(*tables, mixed, outer)


def call(kernel, grid, in_specs, out_specs, out_shape, scalars=0, us=0, **more):
    return pl.pallas_call(
        kernel,
        grid_spec=pltpu.PrefetchScalarGridSpec(
            num_scalar_prefetch=scalars, grid=grid, in_specs=in_specs, out_specs=out_specs
        ),
        out_shape=out_shape,
        cost_estimate=pl.CostEstimate(flops=us * 10**9 // 6, bytes_accessed=0, transcendentals=0),
        compiler_params=pltpu.CompilerParams(vmem_limit_bytes=VMEM),
        **more,
    )


def dot(a, b, dims):
    return lax.dot_general(a, b, (dims, ((), ())), preferred_element_type=f32)


def pack(w_fc1, w_qkv, row, core, planes, part, own, piece):
    third = w_qkv.shape[1] // 3 // piece
    cols = own + 3 * piece
    spots = jnp.stack([row, core]).astype(jnp.int32)

    def kernel(spots_ref, fc1_ref, q_ref, k_ref, v_ref, out_ref):
        out_ref[:, :own] = fc1_ref[...]
        for i, ref in enumerate((q_ref, k_ref, v_ref)):
            out_ref[:, own + i * piece : own + (i + 1) * piece] = ref[...]

    cut = lambda i: pl.BlockSpec(
        (part, piece), lambda p, spots: (spots[0], i * third + p * CORES + spots[1])
    )
    return call(
        kernel,
        (planes,),
        [
            pl.BlockSpec((part, own), lambda p, spots: (spots[0], p * CORES + spots[1])),
            cut(0),
            cut(1),
            cut(2),
        ],
        pl.BlockSpec((None, part, cols), lambda p, spots: (p, 0, 0)),
        jax.ShapeDtypeStruct((planes, part, cols), bf16),
        scalars=1,
    )(spots, w_fc1, w_qkv, w_qkv, w_qkv)


def assemble(w_fc1, w_qkv, arrays, order, spots, own, piece, blocks, before=None):
    _, others, rows, cols = arrays[0].shape
    planes = others + 1
    height = w_fc1.shape[0]
    third = w_qkv.shape[1] // 3 // piece

    def kernel(order_ref, spots_ref, fc1_ref, q_ref, k_ref, v_ref, *refs):
        fc1_out, qkv_out = refs[-2:]
        here = spots_ref[0]
        fc1_out[here] = fc1_ref[...]
        for i, ref in enumerate((q_ref, k_ref, v_ref)):
            qkv_out[here, :, i * piece : (i + 1) * piece] = ref[...]
        places = [(ref, m) for ref in refs[: len(arrays)] for m in range(ref.shape[0])]
        for n, (ref, m) in enumerate(places):

            @pl.when(pl.program_id(0) == n)
            def _(ref=ref, m=m):
                for k in range(1, planes):
                    there = spots_ref[k]
                    fc1_out[there] = ref[m, k - 1, :, :own]
                    qkv_out[there] = ref[m, k - 1, :, own:]

    cut = lambda i: pl.BlockSpec(
        (None, rows, piece), lambda n, order, spots: (order[n], 0, i * third + spots[planes])
    )
    result = lambda size: pl.BlockSpec(
        (planes, None, rows, size), lambda n, order, spots: (0, order[n], 0, 0)
    )
    more = {}
    if before is not None:
        first = 6 + len(arrays)
        more["input_output_aliases"] = {first: 0, first + 1: 1}
    return call(
        kernel,
        (sum(x.shape[0] for x in arrays),),
        [
            pl.BlockSpec((None, rows, own), lambda n, order, spots: (order[n], 0, spots[planes])),
            cut(0),
            cut(1),
            cut(2),
        ]
        + [pl.BlockSpec(x.shape, lambda n, order, spots: (0, 0, 0, 0)) for x in arrays]
        + [pl.BlockSpec(memory_space=pl.ANY)] * (0 if before is None else 2),
        [result(own), result(3 * piece)],
        [
            jax.ShapeDtypeStruct((planes, blocks, rows, own), bf16),
            jax.ShapeDtypeStruct((planes, blocks, rows, 3 * piece), bf16),
        ],
        scalars=2,
        **more,
    )(
        order,
        spots,
        w_fc1.reshape(blocks, rows, -1),
        *[w_qkv.reshape(blocks, rows, -1)] * 3,
        *arrays,
        *(before or ()),
    )


def norm(arrays, places, gain, shift, blocks, before=None):
    rows, width = arrays[0].shape[0] // 2, arrays[0].shape[1]

    def kernel(places_ref, gain_ref, shift_ref, *refs):
        out_ref, tokens_ref, cot_ref, mean_ref, inverse_ref = refs[-5:]
        for n in range(len(arrays)):

            @pl.when(pl.program_id(0) == n)
            def _(ref=refs[n]):
                tokens_ref[...] = ref[:rows]
                cot_ref[...] = ref[rows:]
                x = ref[:rows].astype(f32)
                mean = jnp.mean(x, axis=1, keepdims=True)
                centred = x - mean
                inverse = lax.rsqrt(jnp.mean(centred * centred, axis=1, keepdims=True) + epsilon)
                out_ref[...] = (centred * inverse * gain_ref[...] + shift_ref[...]).astype(bf16)
                mean_ref[...] = jnp.broadcast_to(mean, mean_ref.shape)
                inverse_ref[...] = jnp.broadcast_to(inverse, inverse_ref.shape)

    line = pl.BlockSpec((1, width), lambda i, places: (0, 0))
    wide = pl.BlockSpec((rows, width), lambda i, places: (places[i], 0))
    slim = pl.BlockSpec((rows, LANES), lambda i, places: (places[i], 0))
    more = {}
    if before is not None:
        more["input_output_aliases"] = {3 + len(arrays) + i: i for i in range(5)}
    return call(
        kernel,
        (len(arrays),),
        [line, line]
        + [pl.BlockSpec(x.shape, lambda i, places: (0, 0)) for x in arrays]
        + [pl.BlockSpec(memory_space=pl.ANY)] * (0 if before is None else 5),
        [wide, wide, wide, slim, slim],
        [jax.ShapeDtypeStruct((blocks * rows, width), bf16)] * 3
        + [jax.ShapeDtypeStruct((blocks * rows, LANES), f32)] * 2,
        scalars=1,
        **more,
    )(
        jnp.asarray(places, jnp.int32),
        gain.reshape(1, width),
        shift.reshape(1, width),
        *arrays,
        *(before or ()),
    )


def join(*lists):
    shape = lists[0][0].shape[1:]
    spans, arrays, total = [], [], 0
    for some in lists:
        start = total
        for x in some:
            arrays.append((total, x))
            total += x.shape[0]
        spans.append((start, total - start))

    def kernel(*refs):
        here = pl.program_id(0)
        for n, (start, x) in enumerate(arrays):
            for out, (first, count) in zip(refs[len(arrays) :], spans):
                if first <= start < first + count:

                    @pl.when((here >= start) & (here < start + x.shape[0]))
                    def _(ref=refs[n], out=out):
                        out[...] = ref[...]

    def spec(first, count):
        return pl.BlockSpec(
            (None,) + shape,
            lambda i: (jnp.clip(i - first, 0, count - 1),) + (0,) * len(shape),
        )

    results = call(
        kernel,
        (total,),
        [spec(start, x.shape[0]) for start, x in arrays],
        [spec(*span) for span in spans],
        [jax.ShapeDtypeStruct((count,) + shape, arrays[0][1].dtype) for _, count in spans],
        us=3,
    )(*[x for _, x in arrays])
    return results if len(lists) > 1 else results[0]


def add_in_order(mine, came, order):
    count = order.shape[0]
    rows, width = mine.shape[0] // count, mine.shape[1]

    def kernel(order_ref, mine_ref, came_ref, out_ref):
        out_ref[...] = (mine_ref[...] + came_ref[...].astype(f32)).astype(bf16)

    block = pl.BlockSpec((rows, width), lambda i, order: (i, 0))
    return call(
        kernel,
        (count,),
        [block, block],
        pl.BlockSpec((None, rows, width), lambda i, order: (order[i], 0, 0)),
        jax.ShapeDtypeStruct((count, rows, width), bf16),
        scalars=1,
    )(order, mine, came)


def branches(context, out_rows, active, fc2_rows):
    total, width = context.shape[0], out_rows.shape[1]
    half, block = total // 2, 256

    def kernel(context_ref, out_ref, active_ref, fc2_ref, mine_ref, other_ref):
        y = dot(context_ref[...], out_ref[...], ((1,), (0,)))
        y = y + dot(active_ref[...], fc2_ref[...], ((1,), (0,)))
        mine_ref[...] = y[:half]
        other_ref[...] = y[half:].astype(bf16)

    whole = lambda x: pl.BlockSpec(x.shape, lambda i: (0, 0))
    part = lambda rows: pl.BlockSpec((rows, block), lambda i: (0, i))
    return call(
        kernel,
        (width // block,),
        [whole(context), part(out_rows.shape[0]), whole(active), part(fc2_rows.shape[0])],
        [part(half), part(half)],
        [jax.ShapeDtypeStruct((half, width), f32), jax.ShapeDtypeStruct((half, width), bf16)],
        us=10,
    )(context, out_rows, active, fc2_rows)


def backs(hidden_grad, fc1_cols, mixed_grad, qkv_cols, tokens, mean, inverse):
    total, width = mean.shape[0], fc1_cols.shape[0]
    half, block = total // 2, 256

    def kernel(
        hidden_ref, fc1_ref, mixed_ref, qkv_ref, tokens_ref, mean_ref, inverse_ref,
        first_ref, second_ref, sums_ref,
    ):
        y = dot(hidden_ref[...], fc1_ref[...], ((1,), (1,)))
        y = y + dot(mixed_ref[...], qkv_ref[...], ((1,), (1,)))
        first_ref[...] = y[:half]
        second_ref[...] = y[half:].astype(bf16)
        normed = (tokens_ref[...].astype(f32) - mean_ref[:, :1]) * inverse_ref[:, :1]
        sums_ref[0:1, :] = jnp.sum(y * normed, axis=0, keepdims=True)
        sums_ref[1:2, :] = jnp.sum(y, axis=0, keepdims=True)
        sums_ref[2:8, :] = jnp.zeros((6, block), f32)

    whole = lambda x: pl.BlockSpec(x.shape, lambda i: (0, 0))
    part = lambda rows: pl.BlockSpec((rows, block), lambda i: (0, i))
    rhs = lambda x: pl.BlockSpec((block, x.shape[1]), lambda i: (i, 0))
    return call(
        kernel,
        (width // block,),
        [
            whole(hidden_grad),
            rhs(fc1_cols),
            whole(mixed_grad),
            rhs(qkv_cols),
            part(total),
            whole(mean),
            whole(inverse),
        ],
        [part(half), part(half), part(8)],
        [
            jax.ShapeDtypeStruct((half, width), f32),
            jax.ShapeDtypeStruct((half, width), bf16),
            jax.ShapeDtypeStruct((8, width), f32),
        ],
        us=14,
    )(hidden_grad, fc1_cols, mixed_grad, qkv_cols, tokens, mean, inverse)


def place_columns(net, mine, other, factor):
    J, planes = net.J, net.S
    _, rows, columns = mine[0].shape
    piece = columns // planes
    spots = jnp.concatenate([net.order(), jnp.stack([net.c, 1 - net.c])]).astype(jnp.int32)
    high = rows // 2

    def kernel(spots_ref, m0_ref, m1_ref, o0_ref, o1_ref, out_ref):
        here = pl.program_id(0)
        for e, (place, refs) in enumerate(
            ((net.mine, (m0_ref, m1_ref)), (net.theirs, (o0_ref, o1_ref)))
        ):
            last, _ = place(here)
            for ref, chosen in zip(refs, (jnp.logical_not(last), last)):

                @pl.when(chosen)
                def _(e=e, ref=ref):
                    for k in range(planes):
                        column = (k * CORES + spots_ref[J + e]) * piece
                        out_ref[:, pl.ds(pl.multiple_of(column, LANES), piece)] = (
                            ref[:, k * piece : (k + 1) * piece].astype(f32) * factor
                        )

    return call(
        kernel,
        (J, 2),
        [
            pl.BlockSpec(
                (None, high, columns), lambda i, h, spots, place=place, n=n: (place(i)[1][n], h, 0)
            )
            for place in (net.mine, net.theirs)
            for n in range(2)
        ],
        pl.BlockSpec((high, 2 * columns), lambda i, h, spots: (spots[i] * 2 + h, 0)),
        jax.ShapeDtypeStruct((J * rows, 2 * columns), f32),
        scalars=1,
    )(spots, *mine, *other)


def place_mixed(net, mine, other, start, factor, before=None):
    J, planes = net.J, net.S
    count, part, columns = mine.shape
    piece = columns // planes // 4
    width = planes * CORES * piece
    chips = net.order()[start : start + count]
    spots = jnp.concatenate([chips, jnp.stack([net.c, 1 - net.c])]).astype(jnp.int32)

    def kernel(spots_ref, mine_ref, other_ref, *refs):
        qkv_ref, out_ref = refs[-2:]
        for e, ref in enumerate((mine_ref, other_ref)):
            core = spots_ref[count + e]
            for k in range(planes):

                @pl.when(pl.program_id(1) == k)
                def _(k=k, core=core, ref=ref):
                    for i in range(3):
                        start = (4 * k + i) * piece
                        column = ((i * planes + k) * CORES + core) * piece
                        qkv_ref[:, pl.ds(pl.multiple_of(column, LANES), piece)] = (
                            ref[:, start : start + piece].astype(f32) * factor
                        )
                    block = ref[:, (4 * k + 3) * piece : (4 * k + 4) * piece].astype(f32)
                    out_ref[pl.ds(pl.multiple_of(core * piece, LANES), piece), :] = (
                        block * factor
                    ).T

    if part % LANES == 0:
        out_shape = (CORES * piece, planes * J * part)
        out_spec = pl.BlockSpec((CORES * piece, part), lambda i, k, spots: (0, k * J + spots[i]))
    else:
        out_shape = (planes, J, CORES * piece, part)
        out_spec = pl.BlockSpec(
            (None, None, CORES * piece, part), lambda i, k, spots: (k, spots[i], 0, 0)
        )
    before = before or ()
    return call(
        kernel,
        (count, planes),
        [
            pl.BlockSpec((None, part, columns), lambda i, k, spots: (i, 0, 0)),
            pl.BlockSpec((None, part, columns), lambda i, k, spots: (i, 0, 0)),
        ]
        + [pl.BlockSpec(memory_space=pl.ANY)] * len(before),
        [pl.BlockSpec((part, 3 * width), lambda i, k, spots: (spots[i], 0)), out_spec],
        [
            jax.ShapeDtypeStruct((width // planes, 3 * width), f32),
            jax.ShapeDtypeStruct(out_shape, f32),
        ],
        scalars=1,
        input_output_aliases={3 + i: i for i in range(len(before))},
    )(spots, mine, other, *before)


def place_rows(net, mine, other, factor):
    J = net.J
    _, rows, columns = mine[0].shape
    spots = jnp.concatenate([net.c * J + net.order(), (1 - net.c) * J + net.order(other=True)])
    arrays = (*mine, *other) if net.square else (mine[0], other[0])
    starts = [sum(x.shape[0] for x in arrays[:n]) for n in range(len(arrays))]

    def kernel(spots_ref, *refs):
        here = pl.program_id(0)
        for start, x, ref in zip(starts, arrays, refs):

            @pl.when((here >= start) & (here < start + x.shape[0]))
            def _(ref=ref):
                refs[-1][...] = ref[...].astype(f32) * factor

    def spec(start, count):
        return pl.BlockSpec(
            (None, rows, columns), lambda i, spots: (jnp.clip(i - start, 0, count - 1), 0, 0)
        )

    return call(
        kernel,
        (2 * J,),
        [spec(start, x.shape[0]) for start, x in zip(starts, arrays)],
        pl.BlockSpec((rows, columns), lambda i, spots: (spots[i], 0)),
        jax.ShapeDtypeStruct((2 * J * rows, columns), f32),
        scalars=1,
    )(spots.astype(jnp.int32), *arrays)


def tie(x, *after):
    return lax.optimization_barrier((x, after))[0]


class Links:
    def __init__(self, planes, replicas):
        self.S = planes
        self.J = replicas // CORES
        self.square = self.J == 4
        dp = lax.axis_index("dp")
        self.s = lax.axis_index("shard")
        self.c = dp % CORES
        self.j = dp // CORES
        self.first = jnp.where(self.c == 0, 2, 1)

    def move(self, x, ds=0, dc=0, steps=None):
        pairs = []
        for j in range(self.J):
            for c in range(CORES):
                for s in range(self.S):
                    turn = 0 if steps is None else (2, 1)[(c + steps) % 2]
                    to = ((j ^ turn) * CORES + (c + dc) % CORES) * self.S + (s + ds) % self.S
                    pairs.append(((j * CORES + c) * self.S + s, to))
        return lax.ppermute(x, AXES, pairs)

    def groups(self):
        return [[j * CORES + c for j in range(self.J)] for c in range(CORES)]

    def order(self, other=False):
        if not self.square:
            return jnp.arange(self.J)
        turn = 3 - self.first if other else self.first
        return jnp.stack([self.j, self.j ^ turn, self.j ^ 3 ^ turn, self.j ^ 3])

    def mine(self, i):
        return (i >= 2, (jnp.minimum(i, 1), jnp.maximum(i - 2, 0))) if self.square else (i < 0, (i, 0))

    def theirs(self, i):
        return (i % 2 == 1, (i // 2, i // 2)) if self.square else (i < 0, (i, 0))

    def gather(self, x):
        return self.move(x, steps=0) if self.square else None

    def gather_more(self, stack):
        return self.move(stack, steps=1) if self.square else None

    def spread(self, x):
        if not self.square:
            return x
        other = self.j ^ self.first
        return jnp.stack([pick(x, other, 1), pick(x, other ^ 3 ^ self.first, 1)])

    def spread_sum(self, x, got):
        if not self.square:
            return x, x
        mine = pick(x, self.j, 1), pick(x, self.j ^ 3 ^ self.first, 1)
        return [(m.astype(f32) + g.astype(f32)).astype(bf16) for m, g in zip(mine, got)]

    def spread_last(self, own, got):
        if not self.square:
            return lax.psum_scatter(
                own.astype(f32),
                "dp",
                scatter_dimension=1,
                axis_index_groups=self.groups(),
                tiled=False,
            ).astype(bf16)
        return (own.astype(f32) + got.astype(f32)).astype(bf16)

    def plane_sum(self, x, step):
        if not self.square:
            return lax.psum(x, "dp", axis_index_groups=self.groups()) if step else x
        return x + self.move(x, steps=step)


def swap(x, after=()):
    return lax.all_to_all(tie(x, *after), "shard", 0, 0, tiled=True)


def twofold(x, axis):
    high = lax.reduce_precision(x, 8, 7)
    return jnp.concatenate([high.astype(bf16), (x - high).astype(bf16)], axis=axis)


def as_rows(vector, width, multiple):
    count = -(-vector.shape[0] // (width * multiple)) * multiple
    return jnp.pad(vector, (0, count * width - vector.shape[0])).reshape(count, width)


def pick(x, index, axis):
    return lax.dynamic_index_in_dim(x, index, axis, keepdims=False)


def in_order(held, here):
    size = len(held)
    backwards = jnp.stack(held[::-1])
    return lax.dynamic_slice_in_dim(
        jnp.concatenate([backwards, backwards]), size - 1 - here, size, 0
    )


def local(
    tokens,
    segments,
    ln_gain,
    ln_bias,
    w_qkv,
    b_qkv,
    w_out,
    b_out,
    w_fc1,
    b_fc1,
    w_fc2,
    b_fc2,
    cotangent,
):
    planes = lax.axis_size("shard")
    replicas = lax.axis_size("dp")
    net = Links(planes, replicas)
    S, J, c, j, s = net.S, net.J, net.c, net.j, net.s
    seqs, length, width = tokens.shape
    rows = seqs * length
    ff = w_fc1.shape[1]
    ff_own = ff // (S * CORES)
    mix_own = width // (S * CORES)
    height = width // S
    part = height // J
    total = S * CORES * rows
    back_planes = (s - jnp.arange(S)) % S
    factor = 1.0 / math.sqrt(rows * planes * replicas)

    own_tokens = tokens.reshape(rows, width)
    own_cot = cotangent.reshape(rows, width)
    hops = [jnp.concatenate([own_tokens, own_cot])]
    hops.append(net.move(hops[0], ds=1))

    vectors = [ln_gain, ln_bias, b_qkv, b_out, b_fc1, b_fc2, segments.reshape(-1).astype(bf16)]
    small = jnp.concatenate(vectors)
    size = small.shape[0]
    held = [small] + [net.move(small, ds=k) for k in range(1, S)]

    got = swap(pack(w_fc1, w_qkv, j, c, S, part, ff_own, mix_own))
    others = [net.move(tie(hops[0], hops[1], held), dc=1), net.move(hops[1], dc=1)]
    fc2_rows = lax.dynamic_slice_in_dim(w_fc2, c * ff_own, ff_own, 0)
    out_rows = lax.dynamic_slice_in_dim(w_out, c * mix_own, mix_own, 0)
    marks = jnp.stack([v[size - rows :] for v in held])
    small_all = in_order(held, s)
    whole = []
    start = 0
    for vector in vectors[:-1]:
        whole.append(small_all[:, start : start + vector.shape[0]].reshape(-1).astype(f32))
        start += vector.shape[0]
    gain_full, shift_full, qkv_bias, out_bias, fc1_bias, fc2_bias = whole
    fc1_bias = lax.dynamic_slice_in_dim(fc1_bias, (s * CORES + c) * ff_own, ff_own, 0)
    qkv_bias = lax.dynamic_slice_in_dim(
        qkv_bias.reshape(3, width), (s * CORES + c) * mix_own, mix_own, 1
    ).reshape(-1)
    marks = jnp.stack([marks, net.move(tie(marks, hops[1], held), dc=1)])
    tables = rotary_tables(marks.reshape(-1, length).astype(jnp.int32))
    ready = tie((hops[1], others, fc2_rows, out_rows, tables, gain_full, fc1_bias, qkv_bias), hops[1])
    hop, others, fc2_rows, out_rows, tables, gain_full, fc1_bias, qkv_bias = ready

    got = tie(got, hop, others, fc2_rows, out_rows, tables, gain_full, fc1_bias, qkv_bias)
    block = jnp.concatenate([pick(got, back_planes[k], 0) for k in range(1, S)])[None]
    hops.append(net.move(tie(hop, got), ds=1))
    came = net.gather(block)
    if net.square:
        blocks = tie(join([block, came]))
    else:
        blocks = lax.all_gather(block[0], "dp", axis_index_groups=net.groups())
    came = net.gather_more(blocks)
    while len(hops) < S:
        hops.append(net.move(tie(hops[-1], blocks), ds=1))
        others.append(net.move(tie(hops[-2], blocks), dc=1))
    places = [e * S + k for k in range(S) for e in range(CORES)]
    early = [x for pair in zip(hops[: S - 1], others[: S - 1]) for x in pair]
    early = tie(early, blocks)
    normed_rows = norm(early, places[:-CORES], gain_full, shift_full, S * CORES)
    blocks = tie(blocks, normed_rows)
    spots_w = jnp.concatenate([back_planes, (s * CORES + c)[None]]).astype(jnp.int32)
    chips = net.order()
    weights = lambda x, order, *before: assemble(
        w_fc1,
        w_qkv,
        [x.reshape(-1, S - 1, part, x.shape[-1])],
        order.astype(jnp.int32),
        spots_w,
        ff_own,
        mix_own,
        J,
        *before,
    )
    weight_cols = weights(blocks, chips[: blocks.shape[0]])
    last = tie(hops[-1], weight_cols)
    other = net.move(last, dc=1)
    if net.square:
        weight_cols, came = tie((weight_cols, came), last)
        weight_cols = weights(came, chips[2:], weight_cols)
    last, other = tie((last, other), weight_cols)
    hidden_in, tok_rows, cot_rows, mean, inverse = norm(
        [last, other], places[-CORES:], gain_full, shift_full, S * CORES, normed_rows
    )
    fc1_cols = weight_cols[0].reshape(width, ff_own)
    qkv_cols = weight_cols[1].reshape(width, 3 * mix_own)

    hidden = jnp.dot(hidden_in, fc1_cols, preferred_element_type=f32) + fc1_bias
    active, gelu_back = jax.vjp(lambda v: jax.nn.gelu(v, approximate=True), hidden)
    active = active.astype(bf16)
    transposed = lambda x, y: jnp.einsum("td,te->de", x, y, preferred_element_type=f32).astype(bf16)
    fc2_term = transposed(active, cot_rows)

    mark = []

    def step(x, *made):
        nonlocal mark
        if not made:
            return tie(x, mark)
        mark = list(made)
        return x

    def first_sum(x):
        sent = tie(net.spread(x))
        step(None, sent)
        return x, net.gather(sent)

    def second_sum(x, got):
        x, got = step((x, got))
        own, sent = tie(net.spread_sum(x, got))
        step(None, own, sent)
        return own, net.gather_more(sent)

    def last_sum(own, got):
        part = tie(net.spread_last(*step((own, got))))
        step(None, part)
        return part

    def second_gather(part, came):
        part, came = step((part, came))
        if net.square:
            stack = join([part[None], came[None]])
        else:
            stack = lax.all_gather(part, "dp", axis_index_groups=net.groups())
        stack = tie(stack)
        step(None, stack)
        return stack, net.gather_more(stack)

    def to_other(x):
        return net.move(step(x), dc=1) if net.square else x

    fc2_own, fc2_got = first_sum(fc2_term.reshape(1, J, ff_own // J, width))
    late_cot = step(cot_rows)
    active_grad = jnp.einsum("td,fd->tf", late_cot, fc2_rows, preferred_element_type=f32)
    hidden_grad = gelu_back(active_grad)[0].astype(bf16)
    fc1_term = transposed(hidden_in, hidden_grad)
    fc1_own, fc1_got = first_sum(fc1_term.reshape(S, J, part, ff_own))
    fc2_own, fc2_got = second_sum(fc2_own, fc2_got)
    late_in, late_cot = step((hidden_in, cot_rows))
    mixed = jnp.dot(late_in, qkv_cols, preferred_element_type=f32) + qkv_bias
    context_grad = jnp.einsum("te,de->td", late_cot, out_rows, preferred_element_type=f32).astype(
        bf16
    )
    context, mixed_grad = attention(tables, mixed, context_grad, length)
    step(None, context, mixed_grad)
    fc1_own, fc1_got = second_sum(fc1_own, fc1_got)
    fc2_part = last_sum(fc2_own, fc2_got)[0]
    fc2_came = net.gather(fc2_part)
    late_in, late_cot, late_mixed, late_context = step((hidden_in, cot_rows, mixed_grad, context))
    mixed_term = with_layout_constraint(
        jnp.concatenate(
            [transposed(late_in, late_mixed), transposed(late_cot, late_context)], axis=1
        ),
        Layout((0, 1)),
    )
    mixed_own, mixed_got = first_sum(mixed_term.reshape(S, J, part, 4 * mix_own))
    fc1_part = last_sum(fc1_own, fc1_got)
    fc1_part = swap(fc1_part)
    fc2_part, fc2_came = second_gather(fc2_part, fc2_came)
    fc2_other = net.move(fc2_part, dc=1)
    late_context, late_active = step((context, active))
    branch, branch_other = branches(late_context, out_rows, late_active, fc2_rows)
    step(None, branch, branch_other)
    branch_came = net.move(branch_other, dc=1)
    late_mixed, late_grad = step((mixed_grad, hidden_grad))
    back, back_other, norm_sums = backs(
        late_grad, fc1_cols, late_mixed, qkv_cols, tok_rows, mean, inverse
    )
    step(None, back, back_other, norm_sums)
    back_came = net.move(back_other, dc=1)
    scatter = lambda x: lax.psum_scatter(x, "shard", scatter_dimension=0, tiled=True)[0]
    late_grad, late_mixed, late_cot, norm_sums = step((hidden_grad, mixed_grad, cot_rows, norm_sums))
    mixed_sums = jnp.sum(late_mixed, axis=0, dtype=f32)
    norm_sums = jnp.swapaxes(norm_sums[:2].reshape(2, S, height), 0, 1).reshape(S, -1)
    riders = jnp.concatenate([norm_sums, jnp.broadcast_to(mixed_sums, (S, 3 * mix_own))], axis=1)
    riding = riders.shape[1]
    riders = jnp.pad(riders, ((0, 0), (0, -riding % (24 * mix_own))))
    riders = twofold(riders.reshape(S, -1, 3 * mix_own), 1)
    column_sums = jnp.concatenate(
        [
            jnp.sum(late_grad, axis=0, dtype=f32),
            pick(jnp.sum(late_cot, axis=0, dtype=f32).reshape(S, height), s, 0),
        ]
    )
    riders, column_sums = tie((riders, column_sums))
    step(None, riders, column_sums)
    mixed_own, mixed_got = second_sum(mixed_own, mixed_got)
    fc1_part, fc2_came = step((fc1_part, fc2_came))
    fc1_part = tie(jnp.swapaxes(fc1_part, 0, 1).reshape(part, S * ff_own))
    step(None, fc1_part)
    fc1_came = net.gather(fc1_part)
    if net.square:
        fc2_last = net.move(step(fc2_came), dc=1)
        fc2_mine, fc2_other = (fc2_part, fc2_came), (fc2_other, fc2_last)
    else:
        fc2_mine, fc2_other = (fc2_part, fc2_part), (fc2_other, fc2_other)
    branch_acts = add_in_order(*step((branch, branch_came)), back_planes.astype(jnp.int32))
    back_acts = add_in_order(
        *step(tie((back, back_came), branch_acts)), back_planes.astype(jnp.int32)
    )
    mark += [branch_acts, back_acts]
    fc1_part, fc1_came = second_gather(fc1_part, fc1_came)
    branch_sum, back_sum = scatter(branch_acts), scatter(back_acts)
    mixed_part = last_sum(mixed_own, mixed_got)
    out_part = mixed_part[:, :, 3 * mix_own :]
    mixed_part = tie(jnp.concatenate([mixed_part[:, :, : 3 * mix_own], riders], axis=1))
    step(None, mixed_part)
    mixed_part = swap(mixed_part)
    fc2_own = place_rows(net, *step((fc2_mine, fc2_other)), factor)
    step(None, fc2_own)
    fc1_other = net.move(step(fc1_part), dc=1)
    if net.square:
        fc1_came = step(fc1_came)
        mark += [fc1_came]
    mixed_part = step(mixed_part)
    riders = mixed_part[:, part:].astype(f32)
    mixed_part = jnp.concatenate([mixed_part[:, :part], out_part], axis=2)
    mixed_part = tie(jnp.swapaxes(mixed_part, 0, 1).reshape(part, S * 4 * mix_own))
    step(None, mixed_part)
    mixed_first, mixed_second = net.gather(mixed_part), net.gather_more(mixed_part)
    mixed_other = net.move(mixed_part, dc=1)
    if net.square:
        fc1_last = net.move(step(fc1_came), dc=1)
        fc1_mine, fc1_other = (fc1_part, fc1_came), (fc1_other, fc1_last)
    else:
        fc1_mine, fc1_other = (fc1_part, fc1_part), (fc1_other, fc1_other)
    if net.square:
        fc1_own = place_columns(net, *step((fc1_mine, fc1_other)), factor)
        step(None, fc1_own)
        count = riders.shape[1] // 2
        riders = step(riders)
        riders = (riders[:, :count] + riders[:, count:]).reshape(S, -1)[:, :riding]
        sums = jnp.concatenate(
            [
                jnp.sum(riders[:, : 2 * height], axis=0),
                column_sums[:ff_own],
                riders[:, 2 * height :].reshape(-1),
                column_sums[ff_own:],
            ]
        )
        sums = tie(sums)
        step(None, sums)
        sums = net.plane_sum(sums, 0)
        own, other = step((mixed_part[None], mixed_other[None]))
        placed = tie(place_mixed(net, own, other, 0, factor))
        step(None, placed)
        mixed_first, sums = tie(step((mixed_first, sums)))
        step(None, mixed_first)
        mixed_last = net.gather_more(mixed_first)
        mixed_second = tie(step(mixed_second))
        step(None, mixed_second)
        first_other, second_other = net.move(mixed_first, dc=1), net.move(mixed_second, dc=1)
        own, other = step((mixed_first[None], second_other[None]))
        placed = tie(place_mixed(net, own, other, 1, factor, placed))
        step(None, placed)
        sums = net.plane_sum(tie(step(sums)), 1)
        own, other = step((mixed_second[None], first_other[None]))
        placed = tie(place_mixed(net, own, other, 2, factor, placed))
        step(None, placed)
        mixed_last = tie(step(mixed_last))
        sums_came = net.move(tie(sums, mixed_last), dc=1)
        last_other = net.move(mixed_last, dc=1)
        placed = place_mixed(net, mixed_last[None], last_other[None], 3, factor, placed)
    else:
        mixed_near = lax.all_gather(mixed_part, "dp", axis_index_groups=net.groups())
        count = riders.shape[1] // 2
        riders = step(riders)
        riders = (riders[:, :count] + riders[:, count:]).reshape(S, -1)[:, :riding]
        sums = jnp.concatenate(
            [
                jnp.sum(riders[:, : 2 * height], axis=0),
                column_sums[:ff_own],
                riders[:, 2 * height :].reshape(-1),
                column_sums[ff_own:],
            ]
        )
        sums = tie(sums)
        step(None, sums)
        sums = net.plane_sum(sums, 0)
        fc1_own = place_columns(net, *step((fc1_mine, fc1_other)), factor)
        sums = net.plane_sum(sums, 1)
        sums_came = net.move(sums, dc=1)
        placed = place_mixed(net, mixed_near, net.move(mixed_near, dc=1), 0, factor)
    qkv_own, out_own = placed
    if out_own.ndim == 4:
        out_own = jnp.transpose(out_own, (2, 0, 1, 3)).reshape(height, width)

    own_inputs = own_tokens.astype(f32)
    output = (own_inputs + branch_sum.astype(f32) + (out_bias + fc2_bias)).astype(bf16)
    normed = (own_inputs - mean[:rows, :1]) * inverse[:rows, :1]
    scaled = back_sum.astype(f32) * gain_full
    input_grad = own_cot.astype(f32) + inverse[:rows, :1] * (
        scaled
        - jnp.mean(scaled, axis=1, keepdims=True)
        - normed * jnp.mean(scaled * normed, axis=1, keepdims=True)
    )

    gain_own = (sums[:height] + sums_came[:height]) * factor
    shift_own = (sums[height : 2 * height] + sums_came[height : 2 * height]) * factor
    bias_own = sums[-height:] * factor
    pairs = jnp.where(c == 0, jnp.stack([sums, sums_came]), jnp.stack([sums_came, sums]))
    pairs = pairs[:, 2 * height : -height]
    fc1_bias_own = pairs[:, :ff_own].reshape(-1) * factor
    mixed_sums = jnp.transpose(pairs[:, ff_own:].reshape(CORES, S, 3, mix_own), (2, 1, 0, 3))
    qkv_bias_own = pick(mixed_sums.reshape(S, -1), s, 0) * factor
    return (
        output.reshape(tokens.shape),
        input_grad.reshape(tokens.shape),
        gain_own,
        shift_own,
        qkv_own,
        qkv_bias_own,
        out_own,
        bias_own,
        fc1_own,
        fc1_bias_own,
        fc2_own,
        bias_own,
    )


def solution(mesh):
    return jax.shard_map(
        local,
        mesh=mesh,
        in_specs=(
            P(("dp", "shard"), None, None),
            P(("dp", "shard"), None),
            P("shard"),
            P("shard"),
            P("shard", None),
            P("shard"),
            P("shard", None),
            P("shard"),
            P("shard", None),
            P("shard"),
            P("shard", None),
            P("shard"),
            P(("dp", "shard"), None, None),
        ),
        out_specs=(
            P(("dp", "shard"), None, None),
            P(("dp", "shard"), None, None),
            P("shard"),
            P("shard"),
            P("shard", None),
            P("shard"),
            P("shard", None),
            P("shard"),
            P("shard", None),
            P("shard"),
            P("shard", None),
            P("shard"),
        ),
        check_vma=False,
    )
```
